32 devices in a mesh: dp: 8 (over y, x, core), seq: 4 (over z).
Axes of the slice: x: 2, y: 2, z: 4, core: 2. Of those that a mesh axis runs over, the one named last changes fastest.
Arguments:
- tokens: bfloat16 [64, 256, 768], P('dp', 'seq'), may hold values from -6 to 6
- lengths: int32 [64], P('dp'), may hold values from 193 to 197, as said below
- w_qkv: bfloat16 [768, 2304], P(('dp', 'seq')), may hold values from -0.25 to 0.25
- w_out: bfloat16 [768, 768], P(('dp', 'seq')), may hold values from -0.75 to 0.75
- router: bfloat16 [768, 8], P(('dp', 'seq')), may hold values from -0.109375 to 0.109375
- gain_one: bfloat16 [768], P(('dp', 'seq')), may hold values from 0.5 to 1.5
- shift_one: bfloat16 [768], P(('dp', 'seq')), may hold values from -0.59765625 to 0.59765625
- gain_two: bfloat16 [768], P(('dp', 'seq')), may hold values from 0.5 to 1.5
- shift_two: bfloat16 [768], P(('dp', 'seq')), may hold values from -0.59765625 to 0.59765625
- w_up: bfloat16 [8, 768, 3072], P('dp', None, 'seq'), may hold values from -2 to 2
- w_down: bfloat16 [8, 3072, 768], P('dp', 'seq'), may hold values from -1.75 to 1.75
- cotangent: bfloat16 [64, 256, 768], P('dp', 'seq'), may hold values from -6 to 6
Outputs:
- block_out: bfloat16 [64, 256, 768], P('dp', 'seq')
- grad_input: float32 [64, 256, 768], P('dp', 'seq')
- grad_qkv: float32 [768, 2304], P(('dp', 'seq'))
- grad_out_w: float32 [768, 768], P(('dp', 'seq'))
- grad_router: float32 [768, 8], P(('dp', 'seq'))
- grad_gain_one: float32 [768], P(('dp', 'seq'))
- grad_shift_one: float32 [768], P(('dp', 'seq'))
- grad_gain_two: float32 [768], P(('dp', 'seq'))
- grad_shift_two: float32 [768], P(('dp', 'seq'))
- grad_up: float32 [8, 768, 3072], P('dp', None, 'seq')
- grad_down: float32 [8, 3072, 768], P('dp', 'seq')
The draws below stay inside these ranges and needn't reach their ends.
Inputs may be any that keep to these rules, and one draw needn't show every extreme that they name: `lengths`: each image's count of valid tokens, which are its first positions; some image has exactly 197.
All inputs are finite; a program needn't handle non-finite values.
Results may differ from the reference program's by a relative error of at most 0.025.
Values may be sent and summed in bfloat16 or wider, within the bound.
A program may use at most 128 MiB of HBM per device.

```python
import jax
import jax.numpy as jnp
from jax import lax

D = 768
H = 12
HD = 64
F = 3072
PAD = 256
VALID = 197
E = 8
BLK = 64
IMG_DEV = 8
IMAGES = 64
N_DP = 8
N_SEQ = 4


def draw_lengths(key, part):
    key_counts, key_pick = jax.random.split(key)
    drawn = jax.random.randint(key_counts, (IMAGES,), PAD - BLK + 1, VALID + 1)
    chosen = jax.random.randint(key_pick, (), 0, IMAGES)
    return jnp.where(jnp.arange(IMAGES) == chosen, VALID, drawn).astype(jnp.int32)


def levels(stream_key, extent, pieces, smallest, top_value):
    factor_of, own = 1.0, jax.random.fold_in(stream_key, 6)
    for dim, parts in pieces:
        draws = jnp.exp(jax.random.uniform(jax.random.fold_in(own, dim), (parts,), jnp.float32, smallest / len(pieces), top_value / len(pieces)))
        factor_of = factor_of * jnp.repeat(draws, extent[dim] // parts).reshape([-1 if axis == dim else 1 for axis in range(len(extent))])
    return factor_of


def noise(stream_key, dims, deviation, reach, cuts=(), kind=jnp.bfloat16):
    factor_of = levels(stream_key, dims, cuts, -0.22, 0.18) if cuts else 1.0
    entries = jax.random.normal(stream_key, dims, jnp.float32) * deviation * factor_of
    return jnp.minimum(jnp.maximum(entries, -reach), reach).astype(kind)


def setup_inputs(seed: int = 0) -> dict:
    keys = jax.random.split(jax.random.key(seed), 13)
    return {
        "tokens": noise(keys[0], (IMAGES, PAD, D), 1.0, 6.0, ((0, 8), (1, 4))),
        "lengths": draw_lengths(jax.random.fold_in(keys[12], 71), 0),
        "w_qkv": noise(keys[2], (D, 3 * D), 512 ** -0.5, 0.25, ((0, 32),)),
        "w_out": noise(keys[3], (D, D), 64 ** -0.5, 0.75, ((0, 32),)),
        "router": noise(keys[4], (D, E), (4 * D) ** -0.5, 0.109375, ((0, 32),)),
        "gain_one": jnp.clip(1.0 + 0.1 * jax.random.normal(keys[5], (D,), jnp.float32), 0.5, 1.5).astype(jnp.bfloat16),
        "shift_one": noise(keys[6], (D,), 0.1, 0.59765625, ((0, 32),)),
        "gain_two": jnp.clip(1.0 + 0.1 * jax.random.normal(keys[7], (D,), jnp.float32), 0.5, 1.5).astype(jnp.bfloat16),
        "shift_two": noise(keys[8], (D,), 0.1, 0.59765625, ((0, 32),)),
        "w_up": noise(keys[9], (E, D, F), 8 ** -0.5, 2.0, ((0, 8), (2, 4))),
        "w_down": noise(keys[10], (E, F, D), 12 ** -0.5, 1.75, ((0, 8), (1, 4))),
        "cotangent": noise(keys[11], (IMAGES, PAD, D), 1.0, 6.0, ((0, 8), (1, 4))),
    }


@jax.custom_vjp
def low(v):
    return lax.optimization_barrier(v.astype(jnp.bfloat16)).astype(jnp.float32)

@jax.custom_vjp
def low_back(v):
    return v

def low_keep(v):
    return (low(v), None)

def low_pass(kept, grad):
    return (grad,)

def back_keep(v):
    return (v, None)

def back_low(kept, grad):
    return (low(grad),)
low.defvjp(low_keep, low_pass)
low_back.defvjp(back_keep, back_low)
HIGHEST = lax.Precision.HIGHEST

def layer_norm(values, gain_vec, shift_vec):
    centred = values - lax.optimization_barrier(jnp.mean(values, axis=-1, keepdims=True))
    spread = lax.optimization_barrier(jnp.mean(centred * centred, axis=-1, keepdims=True))
    return centred * lax.rsqrt(spread + 1e-06) * gain_vec + shift_vec

def image_group(images, valid_mask, weights):
    w_qkv, w_out, router, gain_one, shift_one, gain_two, shift_two, w_up, w_down = weights
    group_size = images.shape[0]
    normed = layer_norm(images, gain_one, shift_one)
    mixed_qkv = low(low_back(jnp.einsum('gld,de->gle', low(normed), w_qkv, precision=HIGHEST)))
    queries = mixed_qkv[:, :, :D].reshape(group_size, PAD, H, HD)
    keys_all = mixed_qkv[:, :, D:2 * D].reshape(group_size, PAD, H, HD)
    values_all = mixed_qkv[:, :, 2 * D:].reshape(group_size, PAD, H, HD)
    scores = jnp.einsum('gqhd,gkhd->ghqk', queries, keys_all, precision=HIGHEST) * HD ** (-0.5)
    scores = low_back(jnp.where(valid_mask[:, None, None, :], scores, -1000000000.0))
    attn_probs = low(jax.nn.softmax(scores, axis=-1))
    attended = jnp.einsum('ghqk,gkhd->gqhd', attn_probs, values_all, precision=HIGHEST).reshape(group_size, PAD, D)
    attended = low(low_back(attended))
    branch = low_back(jnp.einsum('gld,de->gle', attended, w_out, precision=HIGHEST))
    middle = images + branch
    normed_two = low(layer_norm(middle, gain_two, shift_two))
    logits = low_back(jnp.einsum('gld,de->gle', normed_two, router, precision=HIGHEST))
    blocked = logits.reshape(group_size, N_SEQ, BLK, -1)
    keep_mask = valid_mask.reshape(group_size, N_SEQ, BLK, 1)
    block_peak = jnp.floor(lax.optimization_barrier(jnp.max(jnp.where(keep_mask, blocked, -1000000000.0), axis=2, keepdims=True)))
    dispatch = jnp.where(keep_mask, jnp.exp(blocked - block_peak), 0.0)
    factor = jnp.exp(block_peak - lax.optimization_barrier(jnp.max(block_peak, axis=1, keepdims=True)))[:, :, 0, :]
    rows_blocked = normed_two.reshape(group_size, N_SEQ, BLK, D)
    numerator = jnp.einsum('gcte,gctd->gced', low(dispatch), rows_blocked, precision=HIGHEST)
    numerator = lax.optimization_barrier(jnp.sum(factor[:, :, :, None] * numerator, axis=1))
    denominator = lax.optimization_barrier(jnp.sum(factor * lax.optimization_barrier(jnp.sum(dispatch, axis=2)), axis=1))
    slots = low(low_back(numerator / denominator[:, :, None]))
    hidden = low_back(jnp.einsum('ged,edf->gef', slots, w_up, precision=HIGHEST))
    active = low(jax.nn.gelu(hidden, approximate=True))
    expert_out = low(low_back(jnp.einsum('gef,efd->ged', active, w_down, precision=HIGHEST)))
    combine = low(jax.nn.softmax(logits, axis=-1))
    moe_out = low_back(jnp.einsum('gle,ged->gld', combine, expert_out, precision=HIGHEST))
    return middle + moe_out

def reference(tokens, lengths, w_qkv, w_out, router, gain_one, shift_one, gain_two, shift_two, w_up, w_down, cotangent):
    valid_mask = jnp.arange(PAD, dtype=jnp.int32)[None, :] < lengths[:, None]
    params = tuple((member.astype(jnp.float32) for member in (w_qkv, w_out, router, gain_one, shift_one, gain_two, shift_two, w_up, w_down)))
    inputs = tokens.astype(jnp.float32)

    def forward(images_all, weights):

        def visit_group(carried, package):
            return (carried, jax.checkpoint(image_group)(package[0], package[1], weights))
        grouped = (images_all.reshape(N_DP, IMG_DEV, PAD, D), valid_mask.reshape(N_DP, IMG_DEV, PAD))
        _, stacked = lax.scan(visit_group, None, grouped)
        return stacked.reshape(images_all.shape)
    block_out, pullback = jax.vjp(forward, inputs, params)
    grad_input, gradients = pullback(cotangent.astype(jnp.float32))
    return (block_out.astype(jnp.bfloat16), grad_input, gradients[0], gradients[1], gradients[2], gradients[3], gradients[4], gradients[5], gradients[6], gradients[7], gradients[8])
```

```python
import jax
import jax.numpy as jnp
from jax import lax
from jax.sharding import PartitionSpec as P

H = 12
HD = 64
BF = jnp.bfloat16
F32 = jnp.float32


def dot(spec, a, b):
    return jnp.einsum(spec, a, b, preferred_element_type=F32)


def unit_norm(values):
    centred = values - jnp.mean(values, axis=-1, keepdims=True)
    inverse = lax.rsqrt(jnp.mean(centred * centred, axis=-1, keepdims=True) + 1e-06)
    return centred * inverse, inverse


def norm_back(grad_rows, unit_rows, inverse, gain):
    scaled = grad_rows * gain
    centred = scaled - jnp.mean(scaled, axis=-1, keepdims=True)
    correction = unit_rows * jnp.mean(scaled * unit_rows, axis=-1, keepdims=True)
    return (
        inverse * (centred - correction),
        jnp.sum(grad_rows * unit_rows, axis=(0, 1)),
        jnp.sum(grad_rows, axis=(0, 1)),
    )


def gelu_tanh(values):
    return jax.nn.gelu(values, approximate=True)


def to_images(array):
    return lax.all_to_all(array, "seq", split_axis=0, concat_axis=1, tiled=True)


def to_blocks(array):
    return lax.all_to_all(array, "seq", split_axis=1, concat_axis=0, tiled=True)


def to_experts(rows):
    rows = lax.all_to_all(rows, "dp", split_axis=1, concat_axis=0, tiled=True)
    return lax.all_gather(rows, "seq", axis=0, tiled=True)


def from_experts(rows):
    rows = lax.psum_scatter(rows, "seq", scatter_dimension=0, tiled=True).astype(BF)
    return lax.all_to_all(rows, "dp", split_axis=0, concat_axis=1, tiled=True)


def plain_plan(
    tokens, lengths, w_qkv, w_out, router, gain_one, shift_one, gain_two, shift_two,
    w_up, w_down, cotangent,
):
    groups = lax.axis_size("seq")
    model_width, slots_all = w_qkv.shape[1] // 3, router.shape[1]
    packed = jnp.concatenate(
        [w_qkv, w_out, router]
        + [vec[:, None] for vec in (gain_one, shift_one, gain_two, shift_two)],
        axis=1,
    )
    packed = lax.all_gather(packed, ("dp", "seq"), axis=0, tiled=True)
    split = 4 * model_width
    w_qkv, w_out = packed[:, : 3 * model_width], packed[:, 3 * model_width : split]
    router = packed[:, split : split + slots_all]
    gain_one, shift_one, gain_two, shift_two = (
        packed[:, split + slots_all + k].astype(F32) for k in range(4)
    )
    x = to_images(tokens).astype(F32)
    cot = to_images(cotangent)
    images, length_all = x.shape[:2]
    lengths_own = lax.dynamic_slice_in_dim(lengths, lax.axis_index("seq") * images, images)
    valid = jnp.arange(length_all, dtype=jnp.int32)[None, :] < lengths_own[:, None]

    unit_one, inverse_one = unit_norm(x)
    normed_one = (unit_one * gain_one + shift_one).astype(BF)
    qkv = dot("btd,de->bte", normed_one, w_qkv).astype(BF).reshape(images, length_all, 3, H, HD)
    queries, keys_all, values_all = qkv[:, :, 0], qkv[:, :, 1], qkv[:, :, 2]
    scores = dot("bqhd,bkhd->bhqk", queries, keys_all) * HD ** (-0.5)
    probs = jax.nn.softmax(jnp.where(valid[:, None, None, :], scores, -1000000000.0), axis=-1)
    probs_low = probs.astype(BF)
    attended = dot("bhqk,bkhd->bqhd", probs_low, values_all).astype(BF)
    attended = attended.reshape(images, length_all, model_width)
    middle = x + dot("btd,de->bte", attended, w_out)
    unit_two, inverse_two = unit_norm(middle)
    normed_two = (unit_two * gain_two + shift_two).astype(BF)
    logits = dot("btd,de->bte", normed_two, router)
    top = jnp.floor(jnp.max(jnp.where(valid[:, :, None], logits, -1000000000.0), axis=1))
    dispatch = jnp.where(valid[:, :, None], jnp.exp(logits - top[:, None, :]), 0.0)
    dispatch_low = dispatch.astype(BF)
    denominator = jnp.sum(dispatch, axis=1)
    slot_vals = dot("bte,btd->bed", dispatch_low, normed_two) / denominator[:, :, None]
    slot_rows = to_experts(slot_vals.astype(BF))
    hidden = dot("red,edf->ref", slot_rows, w_up)
    active = gelu_tanh(hidden).astype(BF)
    expert_out = from_experts(dot("ref,efd->red", active, w_down))
    combine = jax.nn.softmax(logits, axis=-1)
    combine_low = combine.astype(BF)
    block_out = (middle + dot("bte,bed->btd", combine_low, expert_out)).astype(BF)

    d_combine = dot("btd,bed->bte", cot, expert_out)
    d_expert = dot("bte,btd->bed", combine_low, cot).astype(BF)
    d_rows = to_experts(d_expert)
    d_active = dot("red,efd->ref", d_rows, w_down)
    grad_down = dot("ref,red->efd", active, d_rows)
    d_hidden = jax.vjp(gelu_tanh, hidden)[1](d_active)[0].astype(BF)
    grad_up = dot("red,ref->edf", slot_rows, d_hidden)
    d_slots = from_experts(dot("ref,edf->red", d_hidden, w_up))
    d_slots_wide = d_slots.astype(F32)
    inner = jnp.sum(slot_vals * d_slots_wide, axis=-1)
    projected = dot("btd,bed->bte", normed_two, d_slots)
    d_logits = (projected - inner[:, None, :]) / denominator[:, None, :] * dispatch
    d_logits = d_logits + combine * (
        d_combine - jnp.sum(combine * d_combine, axis=-1, keepdims=True)
    )
    d_logits = d_logits.astype(BF)
    scaled = d_slots_wide / denominator[:, :, None]
    scaled_high = scaled.astype(BF)
    scaled_rest = (scaled - scaled_high.astype(F32)).astype(BF)
    d_normed_two = (
        dot("bte,bed->btd", dispatch_low, scaled_high)
        + dot("bte,bed->btd", dispatch_low, scaled_rest)
        + dot("bte,de->btd", d_logits, router)
    )
    grad_router = dot("btd,bte->de", normed_two, d_logits)
    d_norm, grad_gain_two, grad_shift_two = norm_back(d_normed_two, unit_two, inverse_two, gain_two)
    d_middle = cot.astype(F32) + d_norm
    d_branch = d_middle.astype(BF)
    grad_out_w = dot("btd,bte->de", attended, d_branch)
    d_attended = dot("bte,de->btd", d_branch, w_out).astype(BF)
    d_attended = d_attended.reshape(images, length_all, H, HD)
    d_values = dot("bhqk,bqhd->bkhd", probs_low, d_attended)
    d_probs = dot("bqhd,bkhd->bhqk", d_attended, values_all)
    d_scores = probs * (d_probs - jnp.sum(probs * d_probs, axis=-1, keepdims=True))
    d_scores = d_scores.astype(BF)
    d_queries = dot("bhqk,bkhd->bqhd", d_scores, keys_all) * HD ** (-0.5)
    d_keys = dot("bhqk,bqhd->bkhd", d_scores, queries) * HD ** (-0.5)
    d_qkv = jnp.stack([d_queries, d_keys, d_values], axis=2).astype(BF)
    d_qkv = d_qkv.reshape(images, length_all, 3 * model_width)
    grad_qkv = dot("btd,bte->de", normed_one, d_qkv)
    d_normed_one = dot("bte,de->btd", d_qkv, w_qkv)
    d_norm, grad_gain_one, grad_shift_one = norm_back(d_normed_one, unit_one, inverse_one, gain_one)
    grad_input = to_blocks(d_middle + d_norm)

    vectors = (grad_gain_one, grad_shift_one, grad_gain_two, grad_shift_two)
    packed = jnp.concatenate(
        [grad_qkv, grad_out_w, grad_router] + [vec[:, None] for vec in vectors], axis=1
    )
    packed = lax.psum_scatter(packed, ("dp", "seq"), scatter_dimension=0, tiled=True)
    return (
        to_blocks(block_out),
        grad_input,
        packed[:, : 3 * model_width],
        packed[:, 3 * model_width : split],
        packed[:, split : split + slots_all],
        packed[:, split + slots_all],
        packed[:, split + slots_all + 1],
        packed[:, split + slots_all + 2],
        packed[:, split + slots_all + 3],
        grad_up,
        grad_down,
    )


def solution(mesh):
    rows, vector = P(("dp", "seq"), None), P(("dp", "seq"))
    tokens = P("dp", "seq", None)
    up, down = P("dp", None, "seq"), P("dp", "seq", None)
    return jax.shard_map(
        plain_plan,
        mesh=mesh,
        in_specs=(tokens, P("dp"), rows, rows, rows)
        + (vector,) * 4
        + (up, down, tokens),
        out_specs=(tokens, tokens, rows, rows, rows) + (vector,) * 4 + (up, down),
        check_vma=False,
    )
```

```python
import jax
import jax.numpy as jnp
from jax import lax
from jax.experimental import pallas as pl
from jax.experimental.pallas import tpu as pltpu
from jax.sharding import PartitionSpec as P

H = 12
HD = 64
BF = jnp.bfloat16
F32 = jnp.float32


def dot(spec, a, b):
    return jnp.einsum(spec, a, b, preferred_element_type=F32)


def unit_norm(values):
    centred = values - jnp.mean(values, axis=-1, keepdims=True)
    inverse = lax.rsqrt(jnp.mean(centred * centred, axis=-1, keepdims=True) + 1e-06)
    return centred * inverse, inverse


def norm_back(grad_rows, unit_rows, inverse, gain):
    scaled = grad_rows * gain
    centred = scaled - jnp.mean(scaled, axis=-1, keepdims=True)
    correction = unit_rows * jnp.mean(scaled * unit_rows, axis=-1, keepdims=True)
    return (
        inverse * (centred - correction),
        jnp.sum(grad_rows * unit_rows, axis=(0, 1)),
        jnp.sum(grad_rows, axis=(0, 1)),
    )


def gelu_tanh(values):
    return jax.nn.gelu(values, approximate=True)


def to_images(array):
    return lax.all_to_all(array, "seq", split_axis=0, concat_axis=1, tiled=True)


def to_blocks(array):
    return lax.all_to_all(array, "seq", split_axis=1, concat_axis=0, tiled=True)


def to_experts(rows):
    rows = lax.all_to_all(rows, "dp", split_axis=1, concat_axis=0, tiled=True)
    return lax.all_gather(rows, "seq", axis=0, tiled=True)


def from_experts(rows):
    rows = lax.psum_scatter(rows, "seq", scatter_dimension=0, tiled=True).astype(BF)
    return lax.all_to_all(rows, "dp", split_axis=0, concat_axis=1, tiled=True)


def plain_plan(
    tokens, lengths, w_qkv, w_out, router, gain_one, shift_one, gain_two, shift_two,
    w_up, w_down, cotangent,
):
    groups = lax.axis_size("seq")
    model_width, slots_all = w_qkv.shape[1] // 3, router.shape[1]
    packed = jnp.concatenate(
        [w_qkv, w_out, router]
        + [vec[:, None] for vec in (gain_one, shift_one, gain_two, shift_two)],
        axis=1,
    )
    packed = lax.all_gather(packed, ("dp", "seq"), axis=0, tiled=True)
    split = 4 * model_width
    w_qkv, w_out = packed[:, : 3 * model_width], packed[:, 3 * model_width : split]
    router = packed[:, split : split + slots_all]
    gain_one, shift_one, gain_two, shift_two = (
        packed[:, split + slots_all + k].astype(F32) for k in range(4)
    )
    x = to_images(tokens).astype(F32)
    cot = to_images(cotangent)
    images, length_all = x.shape[:2]
    lengths_own = lax.dynamic_slice_in_dim(lengths, lax.axis_index("seq") * images, images)
    valid = jnp.arange(length_all, dtype=jnp.int32)[None, :] < lengths_own[:, None]

    unit_one, inverse_one = unit_norm(x)
    normed_one = (unit_one * gain_one + shift_one).astype(BF)
    qkv = dot("btd,de->bte", normed_one, w_qkv).astype(BF).reshape(images, length_all, 3, H, HD)
    queries, keys_all, values_all = qkv[:, :, 0], qkv[:, :, 1], qkv[:, :, 2]
    scores = dot("bqhd,bkhd->bhqk", queries, keys_all) * HD ** (-0.5)
    probs = jax.nn.softmax(jnp.where(valid[:, None, None, :], scores, -1000000000.0), axis=-1)
    probs_low = probs.astype(BF)
    attended = dot("bhqk,bkhd->bqhd", probs_low, values_all).astype(BF)
    attended = attended.reshape(images, length_all, model_width)
    middle = x + dot("btd,de->bte", attended, w_out)
    unit_two, inverse_two = unit_norm(middle)
    normed_two = (unit_two * gain_two + shift_two).astype(BF)
    logits = dot("btd,de->bte", normed_two, router)
    top = jnp.floor(jnp.max(jnp.where(valid[:, :, None], logits, -1000000000.0), axis=1))
    dispatch = jnp.where(valid[:, :, None], jnp.exp(logits - top[:, None, :]), 0.0)
    dispatch_low = dispatch.astype(BF)
    denominator = jnp.sum(dispatch, axis=1)
    slot_vals = dot("bte,btd->bed", dispatch_low, normed_two) / denominator[:, :, None]
    slot_rows = to_experts(slot_vals.astype(BF))
    hidden = dot("red,edf->ref", slot_rows, w_up)
    active = gelu_tanh(hidden).astype(BF)
    expert_out = from_experts(dot("ref,efd->red", active, w_down))
    combine = jax.nn.softmax(logits, axis=-1)
    combine_low = combine.astype(BF)
    block_out = (middle + dot("bte,bed->btd", combine_low, expert_out)).astype(BF)

    d_combine = dot("btd,bed->bte", cot, expert_out)
    d_expert = dot("bte,btd->bed", combine_low, cot).astype(BF)
    d_rows = to_experts(d_expert)
    d_active = dot("red,efd->ref", d_rows, w_down)
    grad_down = dot("ref,red->efd", active, d_rows)
    d_hidden = jax.vjp(gelu_tanh, hidden)[1](d_active)[0].astype(BF)
    grad_up = dot("red,ref->edf", slot_rows, d_hidden)
    d_slots = from_experts(dot("ref,edf->red", d_hidden, w_up))
    d_slots_wide = d_slots.astype(F32)
    inner = jnp.sum(slot_vals * d_slots_wide, axis=-1)
    projected = dot("btd,bed->bte", normed_two, d_slots)
    d_logits = (projected - inner[:, None, :]) / denominator[:, None, :] * dispatch
    d_logits = d_logits + combine * (
        d_combine - jnp.sum(combine * d_combine, axis=-1, keepdims=True)
    )
    d_logits = d_logits.astype(BF)
    scaled = d_slots_wide / denominator[:, :, None]
    scaled_high = scaled.astype(BF)
    scaled_rest = (scaled - scaled_high.astype(F32)).astype(BF)
    d_normed_two = (
        dot("bte,bed->btd", dispatch_low, scaled_high)
        + dot("bte,bed->btd", dispatch_low, scaled_rest)
        + dot("bte,de->btd", d_logits, router)
    )
    grad_router = dot("btd,bte->de", normed_two, d_logits)
    d_norm, grad_gain_two, grad_shift_two = norm_back(d_normed_two, unit_two, inverse_two, gain_two)
    d_middle = cot.astype(F32) + d_norm
    d_branch = d_middle.astype(BF)
    grad_out_w = dot("btd,bte->de", attended, d_branch)
    d_attended = dot("bte,de->btd", d_branch, w_out).astype(BF)
    d_attended = d_attended.reshape(images, length_all, H, HD)
    d_values = dot("bhqk,bqhd->bkhd", probs_low, d_attended)
    d_probs = dot("bqhd,bkhd->bhqk", d_attended, values_all)
    d_scores = probs * (d_probs - jnp.sum(probs * d_probs, axis=-1, keepdims=True))
    d_scores = d_scores.astype(BF)
    d_queries = dot("bhqk,bkhd->bqhd", d_scores, keys_all) * HD ** (-0.5)
    d_keys = dot("bhqk,bqhd->bkhd", d_scores, queries) * HD ** (-0.5)
    d_qkv = jnp.stack([d_queries, d_keys, d_values], axis=2).astype(BF)
    d_qkv = d_qkv.reshape(images, length_all, 3 * model_width)
    grad_qkv = dot("btd,bte->de", normed_one, d_qkv)
    d_normed_one = dot("bte,de->btd", d_qkv, w_qkv)
    d_norm, grad_gain_one, grad_shift_one = norm_back(d_normed_one, unit_one, inverse_one, gain_one)
    grad_input = to_blocks(d_middle + d_norm)

    vectors = (grad_gain_one, grad_shift_one, grad_gain_two, grad_shift_two)
    packed = jnp.concatenate(
        [grad_qkv, grad_out_w, grad_router] + [vec[:, None] for vec in vectors], axis=1
    )
    packed = lax.psum_scatter(packed, ("dp", "seq"), scatter_dimension=0, tiled=True)
    return (
        to_blocks(block_out),
        grad_input,
        packed[:, : 3 * model_width],
        packed[:, 3 * model_width : split],
        packed[:, split : split + slots_all],
        packed[:, split + slots_all],
        packed[:, split + slots_all + 1],
        packed[:, split + slots_all + 2],
        packed[:, split + slots_all + 3],
        grad_up,
        grad_down,
    )


MESH = pl.DeviceIdType.MESH
VM = pltpu.VMEM


def nt(a, b):
    return lax.dot_general(a, b, (((1,), (1,)), ((), ())), preferred_element_type=F32)


def tn(a, b):
    return lax.dot_general(a, b, (((0,), (0,)), ((), ())), preferred_element_type=F32)


def mm(a, b):
    return jnp.dot(a, b, preferred_element_type=F32)


def ds(start, size):
    return pl.ds(pl.multiple_of(start, size), size)


def remote(src, dst, send, recv, device):
    return pltpu.make_async_remote_copy(
        src_ref=src, dst_ref=dst, send_sem=send, recv_sem=recv, device_id=device,
        device_id_type=MESH,
    )


def place():
    d, z = lax.axis_index("dp"), lax.axis_index("seq")
    core, x, y = lax.rem(d, 2), lax.rem(d // 2, 2), d // 4
    return d, z, d + 2 - 4 * x, d + 4 - 8 * y, d + 1 - 2 * core


def other(d, kind):
    core, x, y = lax.rem(d, 2), lax.rem(d // 2, 2), d // 4
    return {"x": d + 2 - 4 * x, "y": d + 4 - 8 * y, "core": d + 1 - 2 * core}[kind]


def greet(devices):
    barrier = pltpu.get_barrier_semaphore()
    for device in devices:
        pl.semaphore_signal(barrier, inc=1, device_id=device, device_id_type=MESH)
    pl.semaphore_wait(barrier, len(devices))


def gather_steps(packed, stage, full, zsend, zrecv, send, recv):
    d, z, dx, dy, dc = place()
    rows = 4 * packed.shape[0] // 2
    half = rows // 2
    over_x, over_y, over_c = (dx, z), (dy, z), (dc, z)

    def block(owner, part):
        if part is None:
            return full.at[ds(owner * rows, rows)]
        return full.at[ds(owner * rows + part * half, half)]

    first = [
        remote(packed, stage.at[z], zsend.at[k - 1], zrecv.at[k - 1], (d, lax.rem(z + k, 4)))
        for k in range(1, 4)
    ]

    def copy(n, owner, part, device):
        ref = block(owner, part)
        return remote(ref, ref, send.at[n], recv.at[n], device)

    ddx, ddy = other(dx, "y"), other(dy, "x")
    plan = [
        copy(0, d, 0, over_x),
        copy(1, d, 1, over_y),
        copy(2, d, 1, over_x),
        copy(3, d, 0, over_y),
        copy(4, d, None, over_c),
        copy(5, dx, 0, over_y),
        copy(6, dy, 1, over_x),
        copy(7, dx, 0, over_c),
        copy(8, dy, 1, over_c),
        copy(9, dx, 1, over_c),
        copy(10, dy, 0, over_c),
        copy(11, ddx, 0, over_c),
        copy(12, ddx, 1, over_c),
    ]
    s = dc
    sx, sy = other(s, "x"), other(s, "y")
    sd = other(sx, "y")
    landing = [
        (dx, 0), (dy, 1), (dx, 1), (dy, 0), (s, None), (ddx, 0), (ddx, 1),
        (sx, 0), (sy, 1), (sx, 1), (sy, 0), (sd, 0), (sd, 1),
    ]

    def arrived(n):
        ref = block(*landing[n])
        remote(ref, ref, send.at[n], recv.at[n], over_x).wait_recv()

    def start():
        for one in first:
            one.start()

    def assemble():
        own = pltpu.make_async_copy(packed, stage.at[z], zrecv.at[3])
        own.start()
        own.wait()
        for one in first:
            one.wait_recv()
        quarter = packed.shape[0] // 2
        wide = packed.shape[1]
        for side in range(2):
            value = jnp.concatenate(
                [
                    stage[k].astype(F32)[side * quarter : (side + 1) * quarter]
                    for k in range(4)
                ],
                axis=0,
            )
            full[ds(d * rows, rows), side * wide : (side + 1) * wide] = value.astype(BF)
        for n in range(5):
            plan[n].start()

    def forward_one():
        arrived(0)
        plan[5].start()
        plan[7].start()
        arrived(1)
        plan[6].start()
        plan[8].start()

    def forward_two():
        arrived(2)
        plan[9].start()
        arrived(3)
        plan[10].start()
        arrived(5)
        plan[11].start()
        arrived(6)
        plan[12].start()

    def finish():
        for n in (4, 7, 8, 9, 10, 11, 12):
            arrived(n)
        for one in first + plan:
            one.wait_send()

    return start, assemble, forward_one, forward_two, finish


def image_steps(blocks, whole, send, recv, images, local_sem):
    d, z = lax.axis_index("dp"), lax.axis_index("seq")
    size = blocks.shape[1]
    length = 4 * size

    def make(i, k):
        there = lax.rem(z + k, 4)
        src = blocks.at[there * images + i]
        dst = whole.at[ds(i * length + z * size, size)]
        if k == 0:
            return pltpu.make_async_copy(src, dst, local_sem.at[i])
        return remote(
            src, dst, send.at[i * 3 + k - 1], recv.at[i * 3 + k - 1], (d, there)
        )

    table = [[make(i, k) for k in range(4)] for i in range(images)]

    def start(i):
        for one in table[i]:
            one.start()

    def arrived(i):
        table[i][0].wait()
        for one in table[i][1:]:
            one.wait_recv()

    def finish():
        for i in range(images):
            for one in table[i][1:]:
                one.wait_send()

    return start, arrived, finish


def unit_rows(x):
    centred = x - jnp.mean(x, axis=-1, keepdims=True)
    inverse = lax.rsqrt(jnp.mean(centred * centred, axis=-1, keepdims=True) + 1e-06)
    return centred * inverse, inverse


def head_masks():
    lane = lax.broadcasted_iota(jnp.int32, (1, 2 * HD), 1)
    left = jnp.where(lane < HD, 1.0, 0.0)
    return left.astype(BF), (1.0 - left).astype(BF)


def split_heads(pair):
    left, right = head_masks()
    return jnp.concatenate([pair * left, pair * right], axis=0)


def forward_kernel(
    lengths, packed, tokens, cotangent,
    full, small, xs, cots, qkv, probs, attended, middle, n_one, n_two,
    disp, comb, slots, denom,
    stage, bias, zsend, zrecv, wsend, wrecv, tsend, trecv, csend, crecv, local,
):
    d, z, dx, dy, dc = place()
    width = tokens.shape[2]
    images = tokens.shape[0] // 4
    length = 4 * tokens.shape[1]
    pairs = width // (2 * HD)
    zs = [(d, lax.rem(z + k, 4)) for k in range(1, 4)]
    greet(zs + [(dx, z), (dy, z), (dc, z)])
    w_start, w_assemble, w_one, w_two, w_finish = gather_steps(
        packed, stage, full, zsend, zrecv, wsend, wrecv
    )
    t_start, t_arrived, t_finish = image_steps(tokens, xs, tsend, trecv, images, local)
    c_start, c_arrived, c_finish = image_steps(cotangent, cots, csend, crecv, images, local)
    w_start()
    for i in range(images):
        t_start(i)
    w_assemble()
    w_one()
    w_two()
    for i in range(images):
        t_arrived(i)
    for i in range(images):
        c_start(i)
    w_finish()
    small[...] = full[:, 4 * width : 4 * width + 128].astype(F32).T[:16]
    gains = [small[8 + k : 9 + k, :] for k in range(4)]

    rows = 64

    def norm_one(k, carry):
        at = ds(k * rows, rows)
        unit, _ = unit_rows(xs[at, :].astype(F32))
        n_one[at, :] = (unit * gains[0] + gains[1]).astype(BF)
        return carry

    lax.fori_loop(0, images * length // rows, norm_one, 0)

    def project(k, carry):
        at = ds(k * 256, 256)
        qkv[:, at] = mm(n_one[...], full[:, at]).astype(BF)
        return carry

    lax.fori_loop(0, 3 * width // 256, project, 0)

    key = lax.broadcasted_iota(jnp.int32, (1, length), 1)
    for i in range(images):
        bias[i] = jnp.where(key < lengths[z * images + i], 0.0, -1000000000.0)

    def attend(t, carry):
        i, p = t // pairs, lax.rem(t, pairs)
        at = ds(i * length, length)
        q = qkv[at, ds(p * 128, 128)] * jnp.asarray(HD ** (-0.5), BF)
        keys = split_heads(qkv[at, ds(width + p * 128, 128)])
        values = split_heads(qkv[at, ds(2 * width + p * 128, 128)])
        scores = nt(q, keys)
        for h in range(2):
            part = scores[:, h * length : (h + 1) * length] + bias[i]
            top = jnp.max(part, axis=-1, keepdims=True)
            e = jnp.exp(part - top)
            total = jnp.sum(e, axis=-1, keepdims=True)
            probs[t, :, h * length : (h + 1) * length] = (e * (1.0 / total)).astype(BF)
        attended[at, ds(p * 128, 128)] = mm(probs[t], values).astype(BF)
        return carry

    lax.fori_loop(0, images * pairs, attend, 0)

    def project_out(k, carry):
        at = ds(k * 256, 256)
        weight = full[:, ds(3 * width + k * 256, 256)]
        middle[:, at] = xs[:, at].astype(F32) + mm(attended[...], weight)
        return carry

    lax.fori_loop(0, width // 256, project_out, 0)

    def norm_two(k, carry):
        at = ds(k * rows, rows)
        unit, _ = unit_rows(middle[at, :])
        n_two[at, :] = (unit * gains[2] + gains[3]).astype(BF)
        return carry

    lax.fori_loop(0, images * length // rows, norm_two, 0)
    router = small[0:8, :].astype(BF)
    for i in range(images):
        at = slice(i * length, (i + 1) * length)
        logits = nt(router, n_two[at, :])
        inside = key < lengths[z * images + i]
        top = jnp.floor(
            jnp.max(jnp.where(inside, logits, -1000000000.0), axis=-1, keepdims=True)
        )
        dispatch = jnp.where(inside, jnp.exp(logits - top), 0.0)
        peak = jnp.max(logits, axis=0, keepdims=True)
        e = jnp.exp(logits - peak)
        disp[:, at] = dispatch
        comb[:, at] = e / jnp.sum(e, axis=0, keepdims=True)
        total = jnp.sum(dispatch, axis=-1, keepdims=True)
        denom[i] = jnp.broadcast_to(total, denom.shape[1:])
        slots[i] = mm(dispatch.astype(BF), n_two[at, :]) / total
    for i in range(images):
        c_arrived(i)
    t_finish()
    c_finish()


def run_forward(lengths, packed, tokens, cotangent):
    width = tokens.shape[2]
    images, length = tokens.shape[0] // 4, 4 * tokens.shape[1]
    count = images * length
    pairs = width // (2 * HD)

    def shape(*dims, kind=BF):
        return jax.ShapeDtypeStruct(dims, kind)

    outs = (
        shape(width, 2 * packed.shape[1]),
        shape(16, width, kind=F32),
        shape(count, width),
        shape(count, width),
        shape(count, 3 * width),
        shape(images * pairs, length, 2 * length),
        shape(count, width),
        shape(count, width, kind=F32),
        shape(count, width),
        shape(count, width),
        shape(8, count, kind=F32),
        shape(8, count, kind=F32),
        shape(images, 8, width, kind=F32),
        shape(images, 8, 128, kind=F32),
    )
    dma = pltpu.SemaphoreType.DMA
    return pl.pallas_call(
        forward_kernel,
        out_shape=outs,
        in_specs=[pl.BlockSpec(memory_space=pltpu.SMEM)]
        + [pl.BlockSpec(memory_space=VM)]
        + [pl.BlockSpec(memory_space=pl.ANY)] * 2,
        out_specs=[pl.BlockSpec(memory_space=VM)] * len(outs),
        scratch_shapes=[
            VM((4,) + packed.shape, BF),
            VM((images, 1, length), F32),
            dma((3,)), dma((4,)), dma((13,)), dma((13,)),
            dma((3 * images,)), dma((3 * images,)), dma((3 * images,)), dma((3 * images,)),
            dma((images,)),
        ],
        compiler_params=pltpu.CompilerParams(
            collective_id=0, has_side_effects=True, vmem_limit_bytes=60 * 2**20
        ),
        name="forward",
    )(lengths, packed, tokens, cotangent)


def kernel_plan(
    tokens, lengths, w_qkv, w_out, router, gain_one, shift_one, gain_two, shift_two,
    w_up, w_down, cotangent,
):
    model_width, slots_all = w_qkv.shape[1] // 3, router.shape[1]
    vectors = jnp.stack([gain_one, shift_one, gain_two, shift_two], axis=1)
    filler = jnp.zeros((w_qkv.shape[0], 256 - slots_all - 4), BF)
    packed = jnp.concatenate([w_qkv, w_out, router, vectors, filler], axis=1)
    half = packed.shape[1] // 2
    packed = jnp.concatenate([packed[:, :half], packed[:, half:]], axis=0)
    (full, small, xs, cots, qkv, probs, attended, middle, n_one, n_two, disp, comb, slots, denom) = (
        run_forward(lengths, packed, tokens, cotangent)
    )
    images, length_all = 2, 256
    split = 4 * model_width
    w_qkv, w_out = full[:, : 3 * model_width], full[:, 3 * model_width : split]
    router = full[:, split : split + slots_all]
    gain_one, shift_one, gain_two, shift_two = (small[8 + k] for k in range(4))
    cot = cots.reshape(images, length_all, model_width)
    qkv = qkv.reshape(images, length_all, 3, H, HD)
    queries, keys_all, values_all = qkv[:, :, 0], qkv[:, :, 1], qkv[:, :, 2]
    probs_low = probs.reshape(images, H // 2, length_all, 2, length_all).transpose(0, 1, 3, 2, 4)
    probs_low = probs_low.reshape(images, H, length_all, length_all)
    probs = probs_low.astype(F32)
    attended = attended.reshape(images, length_all, model_width)
    middle = middle.reshape(images, length_all, model_width)
    normed_one = n_one.reshape(images, length_all, model_width)
    normed_two = n_two.reshape(images, length_all, model_width)
    unit_one, inverse_one = unit_norm(xs.reshape(images, length_all, model_width).astype(F32))
    unit_two, inverse_two = unit_norm(middle)
    dispatch = disp.T.reshape(images, length_all, slots_all)
    combine = comb.T.reshape(images, length_all, slots_all)
    dispatch_low = dispatch.astype(BF)
    denominator = denom[:, :, 0]
    slot_vals = slots
    slot_rows = to_experts(slot_vals.astype(BF))
    hidden = dot("red,edf->ref", slot_rows, w_up)
    active = gelu_tanh(hidden).astype(BF)
    expert_out = from_experts(dot("ref,efd->red", active, w_down))
    combine_low = combine.astype(BF)
    block_out = (middle + dot("bte,bed->btd", combine_low, expert_out)).astype(BF)

    d_combine = dot("btd,bed->bte", cot, expert_out)
    d_expert = dot("bte,btd->bed", combine_low, cot).astype(BF)
    d_rows = to_experts(d_expert)
    d_active = dot("red,efd->ref", d_rows, w_down)
    grad_down = dot("ref,red->efd", active, d_rows)
    d_hidden = jax.vjp(gelu_tanh, hidden)[1](d_active)[0].astype(BF)
    grad_up = dot("red,ref->edf", slot_rows, d_hidden)
    d_slots = from_experts(dot("ref,edf->red", d_hidden, w_up))
    d_slots_wide = d_slots.astype(F32)
    inner = jnp.sum(slot_vals * d_slots_wide, axis=-1)
    projected = dot("btd,bed->bte", normed_two, d_slots)
    d_logits = (projected - inner[:, None, :]) / denominator[:, None, :] * dispatch
    d_logits = d_logits + combine * (
        d_combine - jnp.sum(combine * d_combine, axis=-1, keepdims=True)
    )
    d_logits = d_logits.astype(BF)
    scaled = d_slots_wide / denominator[:, :, None]
    scaled_high = scaled.astype(BF)
    scaled_rest = (scaled - scaled_high.astype(F32)).astype(BF)
    d_normed_two = (
        dot("bte,bed->btd", dispatch_low, scaled_high)
        + dot("bte,bed->btd", dispatch_low, scaled_rest)
        + dot("bte,de->btd", d_logits, router)
    )
    grad_router = dot("btd,bte->de", normed_two, d_logits)
    d_norm, grad_gain_two, grad_shift_two = norm_back(d_normed_two, unit_two, inverse_two, gain_two)
    d_middle = cot.astype(F32) + d_norm
    d_branch = d_middle.astype(BF)
    grad_out_w = dot("btd,bte->de", attended, d_branch)
    d_attended = dot("bte,de->btd", d_branch, w_out).astype(BF)
    d_attended = d_attended.reshape(images, length_all, H, HD)
    d_values = dot("bhqk,bqhd->bkhd", probs_low, d_attended)
    d_probs = dot("bqhd,bkhd->bhqk", d_attended, values_all)
    d_scores = probs * (d_probs - jnp.sum(probs * d_probs, axis=-1, keepdims=True))
    d_scores = d_scores.astype(BF)
    d_queries = dot("bhqk,bkhd->bqhd", d_scores, keys_all) * HD ** (-0.5)
    d_keys = dot("bhqk,bqhd->bkhd", d_scores, queries) * HD ** (-0.5)
    d_qkv = jnp.stack([d_queries, d_keys, d_values], axis=2).astype(BF)
    d_qkv = d_qkv.reshape(images, length_all, 3 * model_width)
    grad_qkv = dot("btd,bte->de", normed_one, d_qkv)
    d_normed_one = dot("bte,de->btd", d_qkv, w_qkv)
    d_norm, grad_gain_one, grad_shift_one = norm_back(d_normed_one, unit_one, inverse_one, gain_one)
    grad_input = to_blocks(d_middle + d_norm)

    vectors = (grad_gain_one, grad_shift_one, grad_gain_two, grad_shift_two)
    packed = jnp.concatenate(
        [grad_qkv, grad_out_w, grad_router] + [vec[:, None] for vec in vectors], axis=1
    )
    packed = lax.psum_scatter(packed, ("dp", "seq"), scatter_dimension=0, tiled=True)
    return (
        to_blocks(block_out),
        grad_input,
        packed[:, : 3 * model_width],
        packed[:, 3 * model_width : split],
        packed[:, split : split + slots_all],
        packed[:, split + slots_all],
        packed[:, split + slots_all + 1],
        packed[:, split + slots_all + 2],
        packed[:, split + slots_all + 3],
        grad_up,
        grad_down,
    )


def solution(mesh):
    plan = kernel_plan if dict(mesh.shape) == {"dp": 8, "seq": 4} else plain_plan
    rows, vector = P(("dp", "seq"), None), P(("dp", "seq"))
    tokens = P("dp", "seq", None)
    up, down = P("dp", None, "seq"), P("dp", "seq", None)
    return jax.shard_map(
        plan,
        mesh=mesh,
        in_specs=(tokens, P("dp"), rows, rows, rows)
        + (vector,) * 4
        + (up, down, tokens),
        out_specs=(tokens, tokens, rows, rows, rows) + (vector,) * 4 + (up, down),
        check_vma=False,
    )
```

```python
import jax
import jax.numpy as jnp
from jax import lax
from jax.experimental import pallas as pl
from jax.experimental.pallas import tpu as pltpu
from jax.sharding import PartitionSpec as P

H = 12
HD = 64
BF = jnp.bfloat16
F32 = jnp.float32


def dot(spec, a, b):
    return jnp.einsum(spec, a, b, preferred_element_type=F32)


def unit_norm(values):
    centred = values - jnp.mean(values, axis=-1, keepdims=True)
    inverse = lax.rsqrt(jnp.mean(centred * centred, axis=-1, keepdims=True) + 1e-06)
    return centred * inverse, inverse


def norm_back(grad_rows, unit_rows, inverse, gain):
    scaled = grad_rows * gain
    centred = scaled - jnp.mean(scaled, axis=-1, keepdims=True)
    correction = unit_rows * jnp.mean(scaled * unit_rows, axis=-1, keepdims=True)
    return (
        inverse * (centred - correction),
        jnp.sum(grad_rows * unit_rows, axis=(0, 1)),
        jnp.sum(grad_rows, axis=(0, 1)),
    )


def gelu_tanh(values):
    return jax.nn.gelu(values, approximate=True)


def to_images(array):
    return lax.all_to_all(array, "seq", split_axis=0, concat_axis=1, tiled=True)


def to_blocks(array):
    return lax.all_to_all(array, "seq", split_axis=1, concat_axis=0, tiled=True)


def to_experts(rows):
    rows = lax.all_to_all(rows, "dp", split_axis=1, concat_axis=0, tiled=True)
    return lax.all_gather(rows, "seq", axis=0, tiled=True)


def from_experts(rows):
    rows = lax.psum_scatter(rows, "seq", scatter_dimension=0, tiled=True).astype(BF)
    return lax.all_to_all(rows, "dp", split_axis=0, concat_axis=1, tiled=True)


def plain_plan(
    tokens, lengths, w_qkv, w_out, router, gain_one, shift_one, gain_two, shift_two,
    w_up, w_down, cotangent,
):
    groups = lax.axis_size("seq")
    model_width, slots_all = w_qkv.shape[1] // 3, router.shape[1]
    packed = jnp.concatenate(
        [w_qkv, w_out, router]
        + [vec[:, None] for vec in (gain_one, shift_one, gain_two, shift_two)],
        axis=1,
    )
    packed = lax.all_gather(packed, ("dp", "seq"), axis=0, tiled=True)
    split = 4 * model_width
    w_qkv, w_out = packed[:, : 3 * model_width], packed[:, 3 * model_width : split]
    router = packed[:, split : split + slots_all]
    gain_one, shift_one, gain_two, shift_two = (
        packed[:, split + slots_all + k].astype(F32) for k in range(4)
    )
    x = to_images(tokens).astype(F32)
    cot = to_images(cotangent)
    images, length_all = x.shape[:2]
    lengths_own = lax.dynamic_slice_in_dim(lengths, lax.axis_index("seq") * images, images)
    valid = jnp.arange(length_all, dtype=jnp.int32)[None, :] < lengths_own[:, None]

    unit_one, inverse_one = unit_norm(x)
    normed_one = (unit_one * gain_one + shift_one).astype(BF)
    qkv = dot("btd,de->bte", normed_one, w_qkv).astype(BF).reshape(images, length_all, 3, H, HD)
    queries, keys_all, values_all = qkv[:, :, 0], qkv[:, :, 1], qkv[:, :, 2]
    scores = dot("bqhd,bkhd->bhqk", queries, keys_all) * HD ** (-0.5)
    probs = jax.nn.softmax(jnp.where(valid[:, None, None, :], scores, -1000000000.0), axis=-1)
    probs_low = probs.astype(BF)
    attended = dot("bhqk,bkhd->bqhd", probs_low, values_all).astype(BF)
    attended = attended.reshape(images, length_all, model_width)
    middle = x + dot("btd,de->bte", attended, w_out)
    unit_two, inverse_two = unit_norm(middle)
    normed_two = (unit_two * gain_two + shift_two).astype(BF)
    logits = dot("btd,de->bte", normed_two, router)
    top = jnp.floor(jnp.max(jnp.where(valid[:, :, None], logits, -1000000000.0), axis=1))
    dispatch = jnp.where(valid[:, :, None], jnp.exp(logits - top[:, None, :]), 0.0)
    dispatch_low = dispatch.astype(BF)
    denominator = jnp.sum(dispatch, axis=1)
    slot_vals = dot("bte,btd->bed", dispatch_low, normed_two) / denominator[:, :, None]
    slot_rows = to_experts(slot_vals.astype(BF))
    hidden = dot("red,edf->ref", slot_rows, w_up)
    active = gelu_tanh(hidden).astype(BF)
    expert_out = from_experts(dot("ref,efd->red", active, w_down))
    combine = jax.nn.softmax(logits, axis=-1)
    combine_low = combine.astype(BF)
    block_out = (middle + dot("bte,bed->btd", combine_low, expert_out)).astype(BF)

    d_combine = dot("btd,bed->bte", cot, expert_out)
    d_expert = dot("bte,btd->bed", combine_low, cot).astype(BF)
    d_rows = to_experts(d_expert)
    d_active = dot("red,efd->ref", d_rows, w_down)
    grad_down = dot("ref,red->efd", active, d_rows)
    d_hidden = jax.vjp(gelu_tanh, hidden)[1](d_active)[0].astype(BF)
    grad_up = dot("red,ref->edf", slot_rows, d_hidden)
    d_slots = from_experts(dot("ref,edf->red", d_hidden, w_up))
    d_slots_wide = d_slots.astype(F32)
    inner = jnp.sum(slot_vals * d_slots_wide, axis=-1)
    projected = dot("btd,bed->bte", normed_two, d_slots)
    d_logits = (projected - inner[:, None, :]) / denominator[:, None, :] * dispatch
    d_logits = d_logits + combine * (
        d_combine - jnp.sum(combine * d_combine, axis=-1, keepdims=True)
    )
    d_logits = d_logits.astype(BF)
    scaled = d_slots_wide / denominator[:, :, None]
    scaled_high = scaled.astype(BF)
    scaled_rest = (scaled - scaled_high.astype(F32)).astype(BF)
    d_normed_two = (
        dot("bte,bed->btd", dispatch_low, scaled_high)
        + dot("bte,bed->btd", dispatch_low, scaled_rest)
        + dot("bte,de->btd", d_logits, router)
    )
    grad_router = dot("btd,bte->de", normed_two, d_logits)
    d_norm, grad_gain_two, grad_shift_two = norm_back(d_normed_two, unit_two, inverse_two, gain_two)
    d_middle = cot.astype(F32) + d_norm
    d_branch = d_middle.astype(BF)
    grad_out_w = dot("btd,bte->de", attended, d_branch)
    d_attended = dot("bte,de->btd", d_branch, w_out).astype(BF)
    d_attended = d_attended.reshape(images, length_all, H, HD)
    d_values = dot("bhqk,bqhd->bkhd", probs_low, d_attended)
    d_probs = dot("bqhd,bkhd->bhqk", d_attended, values_all)
    d_scores = probs * (d_probs - jnp.sum(probs * d_probs, axis=-1, keepdims=True))
    d_scores = d_scores.astype(BF)
    d_queries = dot("bhqk,bkhd->bqhd", d_scores, keys_all) * HD ** (-0.5)
    d_keys = dot("bhqk,bqhd->bkhd", d_scores, queries) * HD ** (-0.5)
    d_qkv = jnp.stack([d_queries, d_keys, d_values], axis=2).astype(BF)
    d_qkv = d_qkv.reshape(images, length_all, 3 * model_width)
    grad_qkv = dot("btd,bte->de", normed_one, d_qkv)
    d_normed_one = dot("bte,de->btd", d_qkv, w_qkv)
    d_norm, grad_gain_one, grad_shift_one = norm_back(d_normed_one, unit_one, inverse_one, gain_one)
    grad_input = to_blocks(d_middle + d_norm)

    vectors = (grad_gain_one, grad_shift_one, grad_gain_two, grad_shift_two)
    packed = jnp.concatenate(
        [grad_qkv, grad_out_w, grad_router] + [vec[:, None] for vec in vectors], axis=1
    )
    packed = lax.psum_scatter(packed, ("dp", "seq"), scatter_dimension=0, tiled=True)
    return (
        to_blocks(block_out),
        grad_input,
        packed[:, : 3 * model_width],
        packed[:, 3 * model_width : split],
        packed[:, split : split + slots_all],
        packed[:, split + slots_all],
        packed[:, split + slots_all + 1],
        packed[:, split + slots_all + 2],
        packed[:, split + slots_all + 3],
        grad_up,
        grad_down,
    )


MESH = pl.DeviceIdType.MESH
VM = pltpu.VMEM
SMALL = 256
ROWS = 64


def nt(a, b):
    return lax.dot_general(a, b, (((1,), (1,)), ((), ())), preferred_element_type=F32)


def tn(a, b):
    return lax.dot_general(a, b, (((0,), (0,)), ((), ())), preferred_element_type=F32)


def mm(a, b):
    return jnp.dot(a, b, preferred_element_type=F32)


def ds(start, size):
    return pl.ds(pl.multiple_of(start, size), size)


def remote(src, dst, send, recv, device):
    return pltpu.make_async_remote_copy(
        src_ref=src, dst_ref=dst, send_sem=send, recv_sem=recv, device_id=device,
        device_id_type=MESH,
    )


def other(d, kind):
    core, x, y = lax.rem(d, 2), lax.rem(d // 2, 2), d // 4
    return {"x": d + 2 - 4 * x, "y": d + 4 - 8 * y, "core": d + 1 - 2 * core}[kind]


def gather_steps(packed, stage, full, zsend, zrecv, send, recv):
    d, z = lax.axis_index("dp"), lax.axis_index("seq")
    dx, dy, dc = other(d, "x"), other(d, "y"), other(d, "core")
    half = packed.shape[0]
    rows = 2 * half
    over_x, over_y, over_c = (dx, z), (dy, z), (dc, z)

    def block(owner, part):
        if part is None:
            return full.at[ds(owner * rows, rows)]
        return full.at[ds(owner * rows + part * half, half)]

    first = [
        remote(packed, stage.at[z], zsend.at[k - 1], zrecv.at[k - 1], (d, lax.rem(z + k, 4)))
        for k in range(1, 4)
    ]

    def copy(n, owner, part, device):
        ref = block(owner, part)
        return remote(ref, ref, send.at[n], recv.at[n], device)

    dd = other(dx, "y")
    plan = [
        copy(0, d, 0, over_x), copy(1, d, 1, over_y), copy(2, d, 1, over_x),
        copy(3, d, 0, over_y), copy(4, d, None, over_c), copy(5, dx, 0, over_y),
        copy(6, dy, 1, over_x), copy(7, dx, 0, over_c), copy(8, dy, 1, over_c),
        copy(9, dx, 1, over_c), copy(10, dy, 0, over_c), copy(11, dd, 0, over_c),
        copy(12, dd, 1, over_c),
    ]
    cx, cy = other(dc, "x"), other(dc, "y")
    cd = other(cx, "y")
    landing = [
        (dx, 0), (dy, 1), (dx, 1), (dy, 0), (dc, None), (dd, 0), (dd, 1),
        (cx, 0), (cy, 1), (cx, 1), (cy, 0), (cd, 0), (cd, 1),
    ]

    def arrived(n):
        ref = block(*landing[n])
        remote(ref, ref, send.at[n], recv.at[n], over_x).wait_recv()

    def start():
        for one in first:
            one.start()

    def assemble():
        own = pltpu.make_async_copy(packed, stage.at[z], zrecv.at[3])
        own.start()
        own.wait()
        for one in first:
            one.wait_recv()
        quarter, wide = packed.shape[0] // 2, packed.shape[1]
        for side in range(2):
            value = jnp.concatenate(
                [
                    stage[k].astype(F32)[side * quarter : (side + 1) * quarter]
                    for k in range(4)
                ],
                axis=0,
            )
            full[ds(d * rows, rows), side * wide : (side + 1) * wide] = value.astype(BF)
        for n in range(5):
            plan[n].start()

    def forward_one():
        arrived(0)
        plan[5].start()
        plan[7].start()
        arrived(1)
        plan[6].start()
        plan[8].start()

    def forward_two():
        arrived(2)
        plan[9].start()
        arrived(3)
        plan[10].start()
        arrived(5)
        plan[11].start()
        arrived(6)
        plan[12].start()

    def finish():
        for n in (4, 7, 8, 9, 10, 11, 12):
            arrived(n)
        for one in first + plan:
            one.wait_send()

    return start, assemble, forward_one, forward_two, finish


def image_steps(blocks, whole, send, recv, local_sem, images, home):
    d, z = lax.axis_index("dp"), lax.axis_index("seq")
    size = blocks.shape[1]
    length = 4 * size

    def make(i, k):
        there = lax.rem(z + k, 4)
        if home:
            src = whole.at[ds(i * length + there * size, size)]
            dst = blocks.at[z * images + i]
        else:
            src = blocks.at[there * images + i]
            dst = whole.at[ds(i * length + z * size, size)]
        if k == 0:
            return pltpu.make_async_copy(src, dst, local_sem.at[i])
        return remote(src, dst, send.at[i * 3 + k - 1], recv.at[i * 3 + k - 1], (d, there))

    table = [[make(i, k) for k in range(4)] for i in range(images)]

    def start(i):
        for one in table[i]:
            one.start()

    def arrived(i):
        table[i][0].wait()
        for one in table[i][1:]:
            one.wait_recv()

    def sent():
        for i in range(images):
            for one in table[i][1:]:
                one.wait_send()

    return start, arrived, sent


def swap_steps(src, dst, send, recv, to_expert):
    d, z = lax.axis_index("dp"), lax.axis_index("seq")
    count = dst.shape[0]
    me = d * 4 + z

    def start():
        def one(k, carry):
            j = lax.rem(me + k, count)
            e = j // 4
            row = src.at[e] if to_expert else src.at[j]
            remote(row, dst.at[me], send, recv, (e, lax.rem(j, 4))).start()
            return carry

        lax.fori_loop(1, count, one, 0)
        pltpu.make_async_copy(src.at[d] if to_expert else src.at[me], dst.at[me], recv).start()

    def arrived():
        pltpu.make_async_copy(dst, dst, recv).wait()

    def sent():
        part = dst.at[pl.ds(0, count - 1)]
        remote(part, part, send, recv, (other(d, "x"), z)).wait_send()

    return start, arrived, sent


def reduce_steps(grads, pairs, inter, out_stage, in_stage, sems, chunk, lo, hi, emit):
    d, z = lax.axis_index("dp"), lax.axis_index("seq")
    dx, dy, dc = other(d, "x"), other(d, "y"), other(d, "core")
    core = lax.rem(d, 2)
    over_x, over_y, over_c = (dx, z), (dy, z), (dc, z)
    rows = pairs.shape[1]
    half, quarter = rows // 2, rows // 4
    cols = slice(lo, hi)
    send1, recv1, send2, recv2, send3, recv3 = sems
    chips = pairs.shape[0]

    step1 = []
    for m in range(chips):
        block = grads.at[ds((2 * m + 1 - core) * rows, rows), cols]
        n = chunk * chips + m
        step1.append(remote(block, pairs.at[m, :, cols], send1.at[n], recv1.at[n], over_c))
    here, mx, my, md = d // 2, dx // 2, dy // 2, other(dx, "y") // 2

    def part(m, h):
        return pairs.at[m, h * half : (h + 1) * half, cols]

    def hop(k, m, h, device):
        n = chunk * 6 + k
        return remote(part(m, h), inter.at[k, :, cols], send2.at[n], recv2.at[n], device)

    step2 = [
        hop(0, md, 0, over_y), hop(1, md, 1, over_x), hop(2, my, 0, over_y),
        hop(3, mx, 1, over_x), hop(4, mx, 0, over_x), hop(5, my, 1, over_y),
    ]
    narrow = slice(lo // 2, hi // 2)
    step3 = []
    for k in range(1, 4):
        n = chunk * 3 + k - 1
        there = lax.rem(z + k, 4)
        step3.append(
            remote(
                out_stage.at[there, :, narrow], in_stage.at[k - 1, :, narrow],
                send3.at[n], recv3.at[n], (d, there),
            )
        )

    def one():
        for c in step1:
            c.start()

    def two():
        for m in range(chips):
            step1[m].wait_recv()
            own = grads[ds((2 * m + core) * rows, rows), cols].astype(F32)
            pairs[m, :, cols] = (own + pairs[m, :, cols].astype(F32)).astype(BF)
        for k in range(4):
            step2[k].start()

    def three():
        for k, m, h in ((0, mx, 0), (1, my, 1)):
            step2[k].wait_recv()
            at = slice(h * half, (h + 1) * half)
            total = pairs[m, at, cols].astype(F32) + inter[k, :, cols].astype(F32)
            pairs[m, at, cols] = total.astype(BF)
            step2[4 + k].start()

    def four():
        for k in (2, 3, 4, 5):
            step2[k].wait_recv()
        own = pairs[here, :, cols].astype(F32)
        top = own[:half] + inter[2, :, cols].astype(F32) + inter[4, :, cols].astype(F32)
        low = own[half:] + inter[3, :, cols].astype(F32) + inter[5, :, cols].astype(F32)
        total = jnp.concatenate([top, low], axis=0)
        middle = (hi - lo) // 2
        for t in range(4):
            shard = total[t * quarter : (t + 1) * quarter]
            both = jnp.concatenate([shard[:, :middle], shard[:, middle:]], axis=0)
            out_stage[t, :, narrow] = both.astype(BF)
        for c in step3:
            c.start()

    def five():
        total = out_stage[z, :, narrow].astype(F32)
        for k in range(3):
            step3[k].wait_recv()
            total = total + in_stage[k, :, narrow].astype(F32)
        emit(jnp.concatenate([total[:quarter], total[quarter:]], axis=1))

    def sent():
        for c in step1 + step2 + step3:
            c.wait_send()

    return one, two, three, four, five, sent


def unit_rows(x):
    centred = x - jnp.mean(x, axis=-1, keepdims=True)
    inverse = lax.rsqrt(jnp.mean(centred * centred, axis=-1, keepdims=True) + 1e-06)
    return centred * inverse, inverse


def fold_rows(x):
    total = x[:8]
    for k in range(1, x.shape[0] // 8):
        total = total + x[8 * k : 8 * (k + 1)]
    return total


def norm_rows_back(grad, unit, inverse, gain):
    scaled = grad * gain
    centred = scaled - jnp.mean(scaled, axis=-1, keepdims=True)
    correction = unit * jnp.mean(scaled * unit, axis=-1, keepdims=True)
    return inverse * (centred - correction)


def split_heads(pair):
    lane = lax.broadcasted_iota(jnp.int32, (1, 2 * HD), 1)
    left = jnp.where(lane < HD, 1.0, 0.0)
    return jnp.concatenate([pair * left.astype(BF), pair * (1.0 - left).astype(BF)], axis=0)


def join_heads(pair):
    lane = lax.broadcasted_iota(jnp.int32, (1, 2 * HD), 1)
    rows = pair.shape[0] // 2
    return jnp.where(lane < HD, pair[:rows], pair[rows:])


def gelu_parts(v):
    inner = jnp.tanh(0.7978845608 * (v + 0.044715 * v * v * v))
    slope = 0.5 * (1.0 + inner) + 0.5 * v * (1.0 - inner * inner) * 0.7978845608 * (
        1.0 + 3.0 * 0.044715 * v * v
    )
    return 0.5 * v * (1.0 + inner), slope


def block_kernel(
    lengths, w_qkv, w_out, smalls, tokens, cotangent, w_up, w_down,
    block_out, grad_input, grad_qkv, grad_out_w, grad_small, grad_up, grad_down,
    packed, stage, full, small, xs, cots, qkv, probs, attended, middle, n_one, n_two,
    disp, comb, dcomb, slots, bias, up, down, out_rows, pair_in, pair_out, row_sums,
    recv_a, recv_b, recv_c, recv_d, send_b, send_d, turned_one, turned_att,
    d_norm, d_diff, d_branch, d_attended, d_qkv, g_rows, g_blocks, cot_home,
    grads, pairs_buf, inter, out_stage, in_stage,
    zsend, zrecv, wsend, wrecv, tsend, trecv, csend, crecv, bsend, brecv, gsend, grecv,
    local, loads, swap_send, swap_recv, send1, recv1, send2, recv2, send3, recv3,
):
    d, z = lax.axis_index("dp"), lax.axis_index("seq")
    width = tokens.shape[2]
    images = tokens.shape[0] // 4
    length = 4 * tokens.shape[1]
    count = images * length
    groups = width // 256
    experts = disp.shape[0]
    devices = recv_a.shape[0]
    me = d * 4 + z

    barrier = pltpu.get_barrier_semaphore()

    def greet(k, carry):
        j = lax.rem(me + k, devices)
        pl.semaphore_signal(
            barrier, inc=1, device_id=(j // 4, lax.rem(j, 4)), device_id_type=MESH
        )
        return carry

    lax.fori_loop(1, devices, greet, 0)
    load_up = pltpu.make_async_copy(w_up.at[0], up, loads.at[0])
    load_down = pltpu.make_async_copy(w_down.at[0], down, loads.at[1])
    load_home = pltpu.make_async_copy(cotangent, cot_home, loads.at[2])
    for load in (load_up, load_down, load_home):
        load.start()
    own = w_qkv[...]
    pieces = [w_out[...]]
    for g in range(groups):
        for k in range(3):
            pieces.append(own[:, k * width + g * 256 : k * width + (g + 1) * 256])
    pieces.append(smalls[...])
    line = jnp.concatenate([piece.astype(F32) for piece in pieces], axis=1)
    wide = packed.shape[1]
    packed[...] = jnp.concatenate([line[:, :wide], line[:, wide:]], axis=0).astype(BF)
    pl.semaphore_wait(barrier, devices - 1)

    w_start, w_assemble, w_one, w_two, w_finish = gather_steps(
        packed, stage, full, zsend, zrecv, wsend, wrecv
    )
    t_start, t_arrived, t_sent = image_steps(tokens, xs, tsend, trecv, local, images, False)
    c_start, c_arrived, c_sent = image_steps(cotangent, cots, csend, crecv, local, images, False)
    w_start()
    for i in range(images):
        t_start(i)
    w_assemble()
    w_one()
    w_two()
    for i in range(images):
        t_arrived(i)
    for i in range(images):
        c_start(i)
    w_finish()
    small[...] = full[:, 4 * width : 4 * width + 128].astype(F32).T[:16]
    gains = [small[8 + k : 9 + k, :] for k in range(4)]

    def norm_one(k, carry):
        at = ds(k * ROWS, ROWS)
        unit, _ = unit_rows(xs[at, :].astype(F32))
        n_one[at, :] = (unit * gains[0] + gains[1]).astype(BF)
        return carry

    lax.fori_loop(0, count // ROWS, norm_one, 0)

    def project(k, carry):
        qkv[:, ds(k * 256, 256)] = mm(n_one[...], full[:, ds(width + k * 256, 256)]).astype(BF)
        return carry

    lax.fori_loop(0, 3 * groups, project, 0)

    key = lax.broadcasted_iota(jnp.int32, (1, length), 1)
    for i in range(images):
        bias[i] = jnp.where(key < lengths[z * images + i], 0.0, -1000000000.0)
    scale = jnp.asarray(HD ** (-0.5), BF)

    def heads(t):
        i, p = lax.rem(t, images), t // images
        base = (p // 2) * 768 + lax.rem(p, 2) * 128
        return i, p, ds(i * length, length), base

    def attend(t, carry):
        i, p, at, base = heads(t)
        keys = split_heads(qkv[at, ds(base + 256, 128)])
        values = split_heads(qkv[at, ds(base + 512, 128)])
        scores = nt(qkv[at, ds(base, 128)] * scale, keys)
        for h in range(2):
            part = scores[:, h * length : (h + 1) * length] + bias[i]
            e = jnp.exp(part - jnp.max(part, axis=-1, keepdims=True))
            total = jnp.sum(e, axis=-1, keepdims=True)
            probs[t, :, h * length : (h + 1) * length] = (e * (1.0 / total)).astype(BF)
        attended[at, ds(p * 128, 128)] = mm(probs[t], values).astype(BF)
        return carry

    lax.fori_loop(0, images * 2 * groups, attend, 0)

    def project_out(k, carry):
        at = ds(k * 256, 256)
        middle[:, at] = xs[:, at].astype(F32) + mm(attended[...], full[:, at])
        return carry

    lax.fori_loop(0, groups, project_out, 0)

    def norm_two(k, carry):
        at = ds(k * ROWS, ROWS)
        unit, _ = unit_rows(middle[at, :])
        n_two[at, :] = (unit * gains[2] + gains[3]).astype(BF)
        return carry

    lax.fori_loop(0, count // ROWS, norm_two, 0)
    router = small[0:8, :].astype(BF)
    spans = [slice(i * length, (i + 1) * length) for i in range(images)]
    denominators = []
    for i, at in enumerate(spans):
        logits = nt(router, n_two[at, :])
        inside = key < lengths[z * images + i]
        top = jnp.floor(
            jnp.max(jnp.where(inside, logits, -1000000000.0), axis=-1, keepdims=True)
        )
        dispatch = jnp.where(inside, jnp.exp(logits - top), 0.0)
        e = jnp.exp(logits - jnp.max(logits, axis=0, keepdims=True))
        disp[:, at] = dispatch
        comb[:, at] = e / jnp.sum(e, axis=0, keepdims=True)
        denominators.append(jnp.sum(dispatch, axis=-1, keepdims=True))
        slots[i] = mm(dispatch.astype(BF), n_two[at, :]) / denominators[i]

    swap_a = swap_steps(pair_in.at[0], recv_a, swap_send.at[0], swap_recv.at[0], True)
    swap_b = swap_steps(send_b, recv_b, swap_send.at[1], swap_recv.at[1], False)
    swap_c = swap_steps(pair_in.at[1], recv_c, swap_send.at[2], swap_recv.at[2], True)
    swap_d = swap_steps(send_d, recv_d, swap_send.at[3], swap_recv.at[3], False)

    def to_pairs(which, values):
        for e in range(experts):
            pair_in[which, e] = jnp.concatenate(
                [value[e : e + 1] for value in values], axis=0
            ).astype(BF)

    def from_pairs(ref):
        for j in range(devices):
            row_sums[images * j : images * (j + 1), :] = ref[j].astype(F32)
        return row_sums[...].astype(BF)

    def spread(ref, value):
        row_sums[...] = value
        for j in range(devices):
            ref[j] = row_sums[images * j : images * (j + 1), :].astype(BF)

    def collect(ref):
        for e in range(experts):
            total = ref[4 * e].astype(F32)
            for k in range(1, 4):
                total = total + ref[4 * e + k].astype(F32)
            for i in range(images):
                pair_out[i, e : e + 1, :] = total[i : i + 1]
        return [pair_out[i].astype(BF) for i in range(images)]

    to_pairs(0, [slots[i] for i in range(images)])
    swap_a[0]()
    for i in range(images):
        c_arrived(i)
    turned_one[...] = n_one[...].T
    load_up.wait()
    load_down.wait()
    swap_a[1]()
    rows_low = from_pairs(recv_a)
    hidden = mm(rows_low, up[...])
    active, slope = gelu_parts(hidden)
    active = active.astype(BF)
    spread(send_b, mm(active, down[...]))
    swap_b[0]()
    turned_att[...] = attended[...].T
    swap_b[1]()
    outs = collect(recv_b)
    combs = [comb[:, at].astype(BF) for at in spans]
    sends = []
    for i, at in enumerate(spans):
        sends.append(mm(combs[i], cots[at, :]))
        dcomb[:, at] = nt(outs[i], cots[at, :])
    to_pairs(1, sends)
    swap_c[0]()
    b_start, b_arrived, b_sent = image_steps(
        block_out, out_rows, bsend, brecv, local, images, True
    )
    for i, at in enumerate(spans):
        for k in range(groups):
            cut = slice(k * 256, (k + 1) * 256)
            moe = tn(combs[i], outs[i][:, cut])
            out_rows[at, cut] = (middle[at, cut] + moe).astype(BF)
    swap_c[1]()
    d_rows = from_pairs(recv_c)
    d_active = nt(d_rows, down[...])
    d_hidden = (d_active * slope).astype(BF)
    spread(send_d, nt(d_hidden, up[...]))
    swap_d[0]()
    grad_down[0] = tn(active, d_rows)
    grad_up[0] = tn(rows_low, d_hidden)
    swap_d[1]()
    for i in range(images):
        b_start(i)
    d_slots = collect(recv_d)

    router_grad = jnp.zeros((experts, width), F32)
    for i, at in enumerate(spans):
        wide_slots = d_slots[i].astype(F32)
        inner = jnp.sum(slots[i] * wide_slots, axis=-1, keepdims=True)
        projected = nt(d_slots[i], n_two[at, :])
        weight, change = comb[:, at], dcomb[:, at]
        d_logits = (projected - inner) / denominators[i] * disp[:, at]
        d_logits = d_logits + weight * (
            change - jnp.sum(weight * change, axis=0, keepdims=True)
        )
        router_grad = router_grad + mm(d_logits.astype(BF), n_two[at, :])
        scaled = wide_slots / denominators[i]
        high = scaled.astype(BF).astype(F32)
        left = jnp.concatenate(
            [disp[:, at], disp[:, at], d_logits, jnp.zeros_like(d_logits)], axis=0
        ).astype(BF)
        right = jnp.concatenate(
            [high, scaled - high, small[0:8, :], jnp.zeros_like(scaled)], axis=0
        ).astype(BF)
        for k in range(groups):
            cut = slice(k * 256, (k + 1) * 256)
            d_norm[at, cut] = tn(left, right[:, cut])

    nothing = jnp.zeros((8, width), F32)

    def back_two(k, carry):
        at = ds(k * ROWS, ROWS)
        grad = d_norm[at, :]
        unit, inverse = unit_rows(middle[at, :])
        change = norm_rows_back(grad, unit, inverse, gains[2])
        d_diff[at, :] = change
        d_branch[at, :] = (change + cots[at, :].astype(F32)).astype(BF)
        return carry[0] + fold_rows(grad * unit), carry[1] + fold_rows(grad)

    gain_two, shift_two = lax.fori_loop(0, count // ROWS, back_two, (nothing, nothing))

    def emit_out(value):
        grad_out_w[...] = value

    def emit_group(g):
        def emit(value):
            for k in range(3):
                grad_qkv[:, k * width + g * 256 : k * width + (g + 1) * 256] = value[
                    :, k * 256 : (k + 1) * 256
                ]
            if value.shape[1] > 768:
                grad_small[...] = value[:, 768:896]

        return emit

    sems = (send1, recv1, send2, recv2, send3, recv3)
    chunks = []
    for c in range(groups + 1):
        hi = grads.shape[1] if c == groups else (c + 1) * 768
        emit = emit_out if c == 0 else emit_group(c - 1)
        chunks.append(
            reduce_steps(
                grads, pairs_buf, inter, out_stage, in_stage, sems, c, c * 768, hi, emit
            )
        )

    def grad_out(k, carry):
        at = ds(k * 256, 256)
        grads[:, at] = mm(turned_att[...], d_branch[:, at]).astype(BF)
        return carry

    lax.fori_loop(0, groups, grad_out, 0)
    chunks[0][0]()

    def back_out(k, carry):
        at = ds(k * 256, 256)
        d_attended[:, at] = nt(d_branch[...], full[at, 0:width]).astype(BF)
        return carry

    lax.fori_loop(0, groups, back_out, 0)

    def attend_back(t, carry):
        i, p, at, base = heads(t)
        q = qkv[at, ds(base, 128)] * scale
        keys = split_heads(qkv[at, ds(base + 256, 128)])
        values = split_heads(qkv[at, ds(base + 512, 128)])
        grad = d_attended[at, ds(p * 128, 128)]
        d_values = join_heads(tn(probs[t], grad))
        d_probs = nt(grad, values)
        cuts = []
        for h in range(2):
            cut = slice(h * length, (h + 1) * length)
            weight = probs[t, :, cut].astype(F32)
            change = weight * d_probs[:, cut]
            total = jnp.sum(change, axis=-1, keepdims=True)
            cuts.append((change - weight * total).astype(BF))
        d_scores = jnp.concatenate(cuts, axis=1)
        d_qkv[at, ds(base, 128)] = (mm(d_scores, keys) * HD ** (-0.5)).astype(BF)
        d_qkv[at, ds(base + 256, 128)] = join_heads(tn(d_scores, q)).astype(BF)
        d_qkv[at, ds(base + 512, 128)] = d_values.astype(BF)
        return carry

    def group_grads(g):
        def one(k, carry):
            at = ds(g * 768 + k * 256, 256)
            to = ds(width + g * 768 + k * 256, 256)
            grads[:, to] = mm(turned_one[...], d_qkv[:, at]).astype(BF)
            return carry

        lax.fori_loop(0, 3, one, 0)

    per_group = 2 * images
    lax.fori_loop(0, per_group, attend_back, 0)
    chunks[0][1]()
    group_grads(0)
    chunks[1][0]()
    lax.fori_loop(per_group, 2 * per_group, attend_back, 0)
    chunks[0][2]()
    chunks[1][1]()
    group_grads(1)
    chunks[2][0]()
    lax.fori_loop(2 * per_group, 3 * per_group, attend_back, 0)
    chunks[0][3]()
    chunks[1][2]()
    chunks[2][1]()

    def back_qkv(k, carry):
        at = ds(k * 256, 256)
        d_norm[:, at] = nt(d_qkv[...], full[at, width : 4 * width])
        return carry

    lax.fori_loop(0, groups, back_qkv, 0)

    def back_one(k, carry):
        at = ds(k * ROWS, ROWS)
        grad = d_norm[at, :]
        unit, inverse = unit_rows(xs[at, :].astype(F32))
        change = norm_rows_back(grad, unit, inverse, gains[0])
        g_rows[at, :] = (change + d_diff[at, :]).astype(BF)
        return carry[0] + fold_rows(grad * unit), carry[1] + fold_rows(grad)

    gain_one, shift_one = lax.fori_loop(0, count // ROWS, back_one, (nothing, nothing))
    g_start, g_arrived, g_sent = image_steps(g_blocks, g_rows, gsend, grecv, local, images, True)
    for i in range(images):
        b_arrived(i)
        g_start(i)
    sums = [
        jnp.sum(value, axis=0, keepdims=True)
        for value in (gain_one, shift_one, gain_two, shift_two)
    ]
    tall = jnp.concatenate(
        [router_grad] + sums + [jnp.zeros((128 - experts - 4, width), F32)], axis=0
    )
    grads[:, 4 * width : 4 * width + 128] = tall.T.astype(BF)
    grads[:, 4 * width + 128 :] = jnp.zeros((width, SMALL - 128), BF)
    group_grads(2)
    chunks[3][0]()
    chunks[1][3]()
    chunks[2][2]()
    chunks[3][1]()
    chunks[0][4]()
    chunks[2][3]()
    chunks[1][4]()
    chunks[3][2]()
    chunks[3][3]()
    chunks[2][4]()
    for i in range(images):
        g_arrived(i)
        for s in range(4):
            j = s * images + i
            grad_input[j] = g_blocks[j].astype(F32) + 0.0
    load_home.wait()
    for j in range(4 * images):
        grad_input[j] = grad_input[j] + cot_home[j].astype(F32)
    chunks[3][4]()
    t_sent()
    c_sent()
    b_sent()
    g_sent()
    for swap in (swap_a, swap_b, swap_c, swap_d):
        swap[2]()
    for chunk in chunks:
        chunk[5]()


def kernel_plan(
    tokens, lengths, w_qkv, w_out, router, gain_one, shift_one, gain_two, shift_two,
    w_up, w_down, cotangent,
):
    own_rows, width = w_out.shape
    images, size = tokens.shape[0] // 4, tokens.shape[1]
    length, experts = 4 * size, router.shape[1]
    count = images * length
    groups = width // 256
    pairs = 2 * groups
    devices = 4 * experts
    columns = 4 * width + SMALL
    fan = w_up.shape[2]
    vectors = jnp.stack([gain_one, shift_one, gain_two, shift_two], axis=1)
    filler = jnp.zeros((own_rows, SMALL - experts - 4), BF)
    smalls = jnp.concatenate([router, vectors, filler], axis=1)

    def shape(*dims, kind=F32):
        return jax.ShapeDtypeStruct(dims, kind)

    outs = (
        shape(*tokens.shape, kind=BF),
        shape(*tokens.shape),
        shape(own_rows, 3 * width),
        shape(own_rows, width),
        shape(own_rows, 128),
        shape(*w_up.shape),
        shape(*w_down.shape),
    )
    dma = pltpu.SemaphoreType.DMA
    vmem, anywhere = pl.BlockSpec(memory_space=VM), pl.BlockSpec(memory_space=pl.ANY)
    quarter = 4 * own_rows
    pair = (images, width)
    scratch = [
        VM((2 * own_rows, columns // 2), BF),
        VM((4, 2 * own_rows, columns // 2), BF),
        VM((width, columns), BF),
        VM((16, width), F32),
        VM((count, width), BF),
        VM((count, width), BF),
        VM((count, 3 * width), BF),
        VM((images * pairs, length, 2 * length), BF),
        VM((count, width), BF),
        VM((count, width), F32),
        VM((count, width), BF),
        VM((count, width), BF),
        VM((experts, count), F32),
        VM((experts, count), F32),
        VM((experts, count), F32),
        VM((images, experts, width), F32),
        VM((images, 1, length), F32),
        VM((width, fan), BF),
        VM((fan, width), BF),
        VM((count, width), BF),
        VM((2, experts) + pair, BF),
        VM((images, experts, width), F32),
        VM((devices * images, width), F32),
        VM((devices,) + pair, BF),
        VM((devices,) + pair, BF),
        VM((devices,) + pair, BF),
        VM((devices,) + pair, BF),
        VM((devices,) + pair, BF),
        VM((devices,) + pair, BF),
        VM((width, count), BF),
        VM((width, count), BF),
        VM((count, width), F32),
        VM((count, width), F32),
        VM((count, width), BF),
        VM((count, width), BF),
        VM((count, 3 * width), BF),
        VM((count, width), BF),
        VM(tokens.shape, BF),
        VM(tokens.shape, BF),
        VM((width, columns), BF),
        VM((4, quarter, columns), BF),
        VM((6, quarter // 2, columns), BF),
        VM((4, 2 * own_rows, columns // 2), BF),
        VM((3, 2 * own_rows, columns // 2), BF),
    ]
    scratch += [dma((3,)), dma((4,)), dma((13,)), dma((13,))]
    scratch += [dma((3 * images,))] * 8
    scratch += [dma((images,)), dma((3,)), dma((4,)), dma((4,))]
    chunks = groups + 1
    scratch += [dma((4 * chunks,))] * 2 + [dma((6 * chunks,))] * 2 + [dma((3 * chunks,))] * 2
    block_out, grad_input, grad_qkv, grad_out_w, grad_small, grad_up, grad_down = pl.pallas_call(
        block_kernel,
        out_shape=outs,
        in_specs=[pl.BlockSpec(memory_space=pltpu.SMEM)] + [vmem] * 3 + [anywhere] * 4,
        out_specs=[anywhere] + [vmem] * 6,
        scratch_shapes=scratch,
        compiler_params=pltpu.CompilerParams(
            collective_id=0, has_side_effects=True, vmem_limit_bytes=63 * 2**20
        ),
        name="block",
    )(lengths, w_qkv, w_out, smalls, tokens, cotangent, w_up, w_down)
    return (
        block_out,
        grad_input,
        grad_qkv,
        grad_out_w,
        grad_small[:, :experts],
        grad_small[:, experts],
        grad_small[:, experts + 1],
        grad_small[:, experts + 2],
        grad_small[:, experts + 3],
        grad_up,
        grad_down,
    )


def solution(mesh):
    plan = kernel_plan if dict(mesh.shape) == {"dp": 8, "seq": 4} else plain_plan
    rows, vector = P(("dp", "seq"), None), P(("dp", "seq"))
    tokens = P("dp", "seq", None)
    up, down = P("dp", None, "seq"), P("dp", "seq", None)
    return jax.shard_map(
        plan,
        mesh=mesh,
        in_specs=(tokens, P("dp"), rows, rows, rows)
        + (vector,) * 4
        + (up, down, tokens),
        out_specs=(tokens, tokens, rows, rows, rows) + (vector,) * 4 + (up, down),
        check_vma=False,
    )
```

```python
import jax
import jax.numpy as jnp
from jax import lax
from jax.experimental import pallas as pl
from jax.experimental.pallas import tpu as pltpu
from jax.sharding import PartitionSpec as P

H = 12
HD = 64
BF = jnp.bfloat16
F32 = jnp.float32


def dot(spec, a, b):
    return jnp.einsum(spec, a, b, preferred_element_type=F32)


def unit_norm(values):
    centred = values - jnp.mean(values, axis=-1, keepdims=True)
    inverse = lax.rsqrt(jnp.mean(centred * centred, axis=-1, keepdims=True) + 1e-06)
    return centred * inverse, inverse


def norm_back(grad_rows, unit_rows, inverse, gain):
    scaled = grad_rows * gain
    centred = scaled - jnp.mean(scaled, axis=-1, keepdims=True)
    correction = unit_rows * jnp.mean(scaled * unit_rows, axis=-1, keepdims=True)
    return (
        inverse * (centred - correction),
        jnp.sum(grad_rows * unit_rows, axis=(0, 1)),
        jnp.sum(grad_rows, axis=(0, 1)),
    )


def gelu_tanh(values):
    return jax.nn.gelu(values, approximate=True)


def to_images(array):
    return lax.all_to_all(array, "seq", split_axis=0, concat_axis=1, tiled=True)


def to_blocks(array):
    return lax.all_to_all(array, "seq", split_axis=1, concat_axis=0, tiled=True)


def to_experts(rows):
    rows = lax.all_to_all(rows, "dp", split_axis=1, concat_axis=0, tiled=True)
    return lax.all_gather(rows, "seq", axis=0, tiled=True)


def from_experts(rows):
    rows = lax.psum_scatter(rows, "seq", scatter_dimension=0, tiled=True).astype(BF)
    return lax.all_to_all(rows, "dp", split_axis=0, concat_axis=1, tiled=True)


def plain_plan(
    tokens, lengths, w_qkv, w_out, router, gain_one, shift_one, gain_two, shift_two,
    w_up, w_down, cotangent,
):
    groups = lax.axis_size("seq")
    model_width, slots_all = w_qkv.shape[1] // 3, router.shape[1]
    packed = jnp.concatenate(
        [w_qkv, w_out, router]
        + [vec[:, None] for vec in (gain_one, shift_one, gain_two, shift_two)],
        axis=1,
    )
    packed = lax.all_gather(packed, ("dp", "seq"), axis=0, tiled=True)
    split = 4 * model_width
    w_qkv, w_out = packed[:, : 3 * model_width], packed[:, 3 * model_width : split]
    router = packed[:, split : split + slots_all]
    gain_one, shift_one, gain_two, shift_two = (
        packed[:, split + slots_all + k].astype(F32) for k in range(4)
    )
    x = to_images(tokens).astype(F32)
    cot = to_images(cotangent)
    images, length_all = x.shape[:2]
    lengths_own = lax.dynamic_slice_in_dim(lengths, lax.axis_index("seq") * images, images)
    valid = jnp.arange(length_all, dtype=jnp.int32)[None, :] < lengths_own[:, None]

    unit_one, inverse_one = unit_norm(x)
    normed_one = (unit_one * gain_one + shift_one).astype(BF)
    qkv = dot("btd,de->bte", normed_one, w_qkv).astype(BF).reshape(images, length_all, 3, H, HD)
    queries, keys_all, values_all = qkv[:, :, 0], qkv[:, :, 1], qkv[:, :, 2]
    scores = dot("bqhd,bkhd->bhqk", queries, keys_all) * HD ** (-0.5)
    probs = jax.nn.softmax(jnp.where(valid[:, None, None, :], scores, -1000000000.0), axis=-1)
    probs_low = probs.astype(BF)
    attended = dot("bhqk,bkhd->bqhd", probs_low, values_all).astype(BF)
    attended = attended.reshape(images, length_all, model_width)
    middle = x + dot("btd,de->bte", attended, w_out)
    unit_two, inverse_two = unit_norm(middle)
    normed_two = (unit_two * gain_two + shift_two).astype(BF)
    logits = dot("btd,de->bte", normed_two, router)
    top = jnp.floor(jnp.max(jnp.where(valid[:, :, None], logits, -1000000000.0), axis=1))
    dispatch = jnp.where(valid[:, :, None], jnp.exp(logits - top[:, None, :]), 0.0)
    dispatch_low = dispatch.astype(BF)
    denominator = jnp.sum(dispatch, axis=1)
    slot_vals = dot("bte,btd->bed", dispatch_low, normed_two) / denominator[:, :, None]
    slot_rows = to_experts(slot_vals.astype(BF))
    hidden = dot("red,edf->ref", slot_rows, w_up)
    active = gelu_tanh(hidden).astype(BF)
    expert_out = from_experts(dot("ref,efd->red", active, w_down))
    combine = jax.nn.softmax(logits, axis=-1)
    combine_low = combine.astype(BF)
    block_out = (middle + dot("bte,bed->btd", combine_low, expert_out)).astype(BF)

    d_combine = dot("btd,bed->bte", cot, expert_out)
    d_expert = dot("bte,btd->bed", combine_low, cot).astype(BF)
    d_rows = to_experts(d_expert)
    d_active = dot("red,efd->ref", d_rows, w_down)
    grad_down = dot("ref,red->efd", active, d_rows)
    d_hidden = jax.vjp(gelu_tanh, hidden)[1](d_active)[0].astype(BF)
    grad_up = dot("red,ref->edf", slot_rows, d_hidden)
    d_slots = from_experts(dot("ref,edf->red", d_hidden, w_up))
    d_slots_wide = d_slots.astype(F32)
    inner = jnp.sum(slot_vals * d_slots_wide, axis=-1)
    projected = dot("btd,bed->bte", normed_two, d_slots)
    d_logits = (projected - inner[:, None, :]) / denominator[:, None, :] * dispatch
    d_logits = d_logits + combine * (
        d_combine - jnp.sum(combine * d_combine, axis=-1, keepdims=True)
    )
    d_logits = d_logits.astype(BF)
    scaled = d_slots_wide / denominator[:, :, None]
    scaled_high = scaled.astype(BF)
    scaled_rest = (scaled - scaled_high.astype(F32)).astype(BF)
    d_normed_two = (
        dot("bte,bed->btd", dispatch_low, scaled_high)
        + dot("bte,bed->btd", dispatch_low, scaled_rest)
        + dot("bte,de->btd", d_logits, router)
    )
    grad_router = dot("btd,bte->de", normed_two, d_logits)
    d_norm, grad_gain_two, grad_shift_two = norm_back(d_normed_two, unit_two, inverse_two, gain_two)
    d_middle = cot.astype(F32) + d_norm
    d_branch = d_middle.astype(BF)
    grad_out_w = dot("btd,bte->de", attended, d_branch)
    d_attended = dot("bte,de->btd", d_branch, w_out).astype(BF)
    d_attended = d_attended.reshape(images, length_all, H, HD)
    d_values = dot("bhqk,bqhd->bkhd", probs_low, d_attended)
    d_probs = dot("bqhd,bkhd->bhqk", d_attended, values_all)
    d_scores = probs * (d_probs - jnp.sum(probs * d_probs, axis=-1, keepdims=True))
    d_scores = d_scores.astype(BF)
    d_queries = dot("bhqk,bkhd->bqhd", d_scores, keys_all) * HD ** (-0.5)
    d_keys = dot("bhqk,bqhd->bkhd", d_scores, queries) * HD ** (-0.5)
    d_qkv = jnp.stack([d_queries, d_keys, d_values], axis=2).astype(BF)
    d_qkv = d_qkv.reshape(images, length_all, 3 * model_width)
    grad_qkv = dot("btd,bte->de", normed_one, d_qkv)
    d_normed_one = dot("bte,de->btd", d_qkv, w_qkv)
    d_norm, grad_gain_one, grad_shift_one = norm_back(d_normed_one, unit_one, inverse_one, gain_one)
    grad_input = to_blocks(d_middle + d_norm)

    vectors = (grad_gain_one, grad_shift_one, grad_gain_two, grad_shift_two)
    packed = jnp.concatenate(
        [grad_qkv, grad_out_w, grad_router] + [vec[:, None] for vec in vectors], axis=1
    )
    packed = lax.psum_scatter(packed, ("dp", "seq"), scatter_dimension=0, tiled=True)
    return (
        to_blocks(block_out),
        grad_input,
        packed[:, : 3 * model_width],
        packed[:, 3 * model_width : split],
        packed[:, split : split + slots_all],
        packed[:, split + slots_all],
        packed[:, split + slots_all + 1],
        packed[:, split + slots_all + 2],
        packed[:, split + slots_all + 3],
        grad_up,
        grad_down,
    )


MESH = pl.DeviceIdType.MESH
VM = pltpu.VMEM
SMALL = 128
ROWS = 64


def nt(a, b):
    return lax.dot_general(a, b, (((1,), (1,)), ((), ())), preferred_element_type=F32)


def tn(a, b):
    return lax.dot_general(a, b, (((0,), (0,)), ((), ())), preferred_element_type=F32)


def mm(a, b):
    return jnp.dot(a, b, preferred_element_type=F32)


def ds(start, size, unit=None):
    return pl.ds(pl.multiple_of(start, unit or size), size)


def remote(src, dst, send, recv, device):
    return pltpu.make_async_remote_copy(
        src_ref=src, dst_ref=dst, send_sem=send, recv_sem=recv, device_id=device,
        device_id_type=MESH,
    )


def other(d, kind):
    core, x, y = lax.rem(d, 2), lax.rem(d // 2, 2), d // 4
    return {"x": d + 2 - 4 * x, "y": d + 4 - 8 * y, "core": d + 1 - 2 * core}[kind]


def gather_steps(stage, full, lo, hi, zsend, zrecv, send, recv, first_sem):
    d, z = lax.axis_index("dp"), lax.axis_index("seq")
    dx, dy, dc = other(d, "x"), other(d, "y"), other(d, "core")
    half = stage.shape[1]
    rows = 2 * half
    over_x, over_y, over_c = (dx, z), (dy, z), (dc, z)

    def block(owner, part):
        if part is None:
            return full.at[ds(owner * rows, rows), lo:hi]
        return full.at[ds(owner * rows + part * half, half), lo:hi]

    mine = stage.at[z]
    first = []
    for k in range(1, 4):
        n = first_sem * 3 + k - 1
        first.append(remote(mine, mine, zsend.at[n], zrecv.at[n], (d, lax.rem(z + k, 4))))

    def copy(n, owner, part, device):
        ref, n = block(owner, part), n + 13 * first_sem
        return remote(ref, ref, send.at[n], recv.at[n], device)

    dd = other(dx, "y")
    plan = [
        copy(0, d, 0, over_x), copy(1, d, 1, over_y), copy(2, d, 1, over_x),
        copy(3, d, 0, over_y), copy(4, d, None, over_c), copy(5, dx, 0, over_y),
        copy(6, dy, 1, over_x), copy(7, dx, 0, over_c), copy(8, dy, 1, over_c),
        copy(9, dx, 1, over_c), copy(10, dy, 0, over_c), copy(11, dd, 0, over_c),
        copy(12, dd, 1, over_c),
    ]
    cx, cy = other(dc, "x"), other(dc, "y")
    cd = other(cx, "y")
    landing = [
        (dx, 0), (dy, 1), (dx, 1), (dy, 0), (dc, None), (dd, 0), (dd, 1),
        (cx, 0), (cy, 1), (cx, 1), (cy, 0), (cd, 0), (cd, 1),
    ]

    def arrived(n):
        ref, n = block(*landing[n]), n + 13 * first_sem
        remote(ref, ref, send.at[n], recv.at[n], over_x).wait_recv()

    def start():
        for one in first:
            one.start()

    def assemble():
        for one in first:
            one.wait_recv()
        quarter, wide = half // 2, stage.shape[2]
        for side in range(2):
            value = jnp.concatenate(
                [
                    stage[k].astype(F32)[side * quarter : (side + 1) * quarter]
                    for k in range(4)
                ],
                axis=0,
            )
            base = lo + side * wide
            full[ds(d * rows, rows), base : base + wide] = value.astype(BF)
        for n in range(5):
            plan[n].start()

    def forward_one():
        arrived(0)
        plan[5].start()
        plan[7].start()
        arrived(1)
        plan[6].start()
        plan[8].start()

    def forward_two():
        arrived(2)
        plan[9].start()
        arrived(3)
        plan[10].start()
        arrived(5)
        plan[11].start()
        arrived(6)
        plan[12].start()

    def finish():
        for n in (4, 7, 8, 9, 10, 11, 12):
            arrived(n)

    def sent():
        for one in first + plan:
            one.wait_send()

    return start, assemble, forward_one, forward_two, finish, sent


def image_steps(blocks, whole, send, recv, local_sem, images, home):
    d, z = lax.axis_index("dp"), lax.axis_index("seq")
    size = blocks.shape[1]
    length = 4 * size

    def make(i, k):
        there = lax.rem(z + k, 4)
        if home:
            src = whole.at[ds(i * length + there * size, size)]
            dst = blocks.at[z * images + i]
        else:
            src = blocks.at[there * images + i]
            dst = whole.at[ds(i * length + z * size, size)]
        if k == 0:
            return pltpu.make_async_copy(src, dst, local_sem.at[i])
        return remote(src, dst, send.at[i * 3 + k - 1], recv.at[i * 3 + k - 1], (d, there))

    table = [[make(i, k) for k in range(4)] for i in range(images)]

    def start(i):
        for one in table[i]:
            one.start()

    def arrived(i):
        table[i][0].wait()
        for one in table[i][1:]:
            one.wait_recv()

    def sent():
        for i in range(images):
            for one in table[i][1:]:
                one.wait_send()

    return start, arrived, sent


def swap_steps(src, dst, send, recv, to_expert):
    d, z = lax.axis_index("dp"), lax.axis_index("seq")
    count = dst.shape[0]
    me = d * 4 + z

    def start():
        def one(k, carry):
            j = lax.rem(me + k, count)
            e = j // 4
            row = src.at[e] if to_expert else src.at[j]
            remote(row, dst.at[me], send, recv, (e, lax.rem(j, 4))).start()
            return carry

        lax.fori_loop(1, count, one, 0)
        pltpu.make_async_copy(src.at[d] if to_expert else src.at[me], dst.at[me], recv).start()

    def arrived():
        pltpu.make_async_copy(dst, dst, recv).wait()

    def sent():
        part = dst.at[pl.ds(0, count - 1)]
        remote(part, part, send, recv, (other(d, "x"), z)).wait_send()

    return start, arrived, sent


def reduce_steps(grads, pairs, inter, out_stage, in_stage, sems, chunk, lo, hi, narrow):
    d, z = lax.axis_index("dp"), lax.axis_index("seq")
    dx, dy, dc = other(d, "x"), other(d, "y"), other(d, "core")
    core = lax.rem(d, 2)
    over_x, over_y, over_c = (dx, z), (dy, z), (dc, z)
    rows = pairs.shape[1]
    half, quarter = rows // 2, rows // 4
    cols = slice(lo, hi)
    send1, recv1, send2, recv2, send3, recv3 = sems
    chips = pairs.shape[0]

    step1 = []
    for m in range(chips):
        block = grads.at[ds((2 * m + 1 - core) * rows, rows), cols]
        n = chunk * chips + m
        step1.append(remote(block, pairs.at[m, :, cols], send1.at[n], recv1.at[n], over_c))
    here, mx, my, md = d // 2, dx // 2, dy // 2, other(dx, "y") // 2

    def part(m, h):
        return pairs.at[m, h * half : (h + 1) * half, cols]

    def hop(k, m, h, device):
        n = chunk * 6 + k
        return remote(part(m, h), inter.at[k, :, cols], send2.at[n], recv2.at[n], device)

    step2 = [
        hop(0, md, 0, over_y), hop(1, md, 1, over_x), hop(2, my, 0, over_y),
        hop(3, mx, 1, over_x), hop(4, mx, 0, over_x), hop(5, my, 1, over_y),
    ]
    local_copy = pltpu.make_async_copy(
        out_stage.at[z, :, narrow], in_stage.at[3, :, narrow], recv3.at[chunk * 4 + 3]
    )
    step3 = []
    for k in range(1, 4):
        n = chunk * 4 + k - 1
        there = lax.rem(z + k, 4)
        step3.append(
            remote(
                out_stage.at[there, :, narrow], in_stage.at[k - 1, :, narrow],
                send3.at[n], recv3.at[n], (d, there),
            )
        )

    def one():
        for c in step1:
            c.start()

    def two():
        for m in range(chips):
            step1[m].wait_recv()
            own = grads[ds((2 * m + core) * rows, rows), cols].astype(F32)
            pairs[m, :, cols] = (own + pairs[m, :, cols].astype(F32)).astype(BF)
        for k in range(4):
            step2[k].start()

    def three():
        for k, m, h in ((0, mx, 0), (1, my, 1)):
            step2[k].wait_recv()
            at = slice(h * half, (h + 1) * half)
            total = pairs[m, at, cols].astype(F32) + inter[k, :, cols].astype(F32)
            pairs[m, at, cols] = total.astype(BF)
            step2[4 + k].start()

    def four():
        for k in (2, 3, 4, 5):
            step2[k].wait_recv()
        own = pairs[here, :, cols].astype(F32)
        top = own[:half] + inter[2, :, cols].astype(F32) + inter[4, :, cols].astype(F32)
        low = own[half:] + inter[3, :, cols].astype(F32) + inter[5, :, cols].astype(F32)
        total = jnp.concatenate([top, low], axis=0)
        middle = narrow.stop - narrow.start
        if 2 * middle > hi - lo:
            filler = jnp.zeros((rows, 2 * middle - (hi - lo)), F32)
            total = jnp.concatenate([total, filler], axis=1)
        for t in range(4):
            shard = total[t * quarter : (t + 1) * quarter]
            both = jnp.concatenate([shard[:, :middle], shard[:, middle:]], axis=0)
            out_stage[t, :, narrow] = both.astype(BF)
        for c in step3:
            c.start()
        local_copy.start()

    def five():
        for c in step3:
            c.wait_recv()
        local_copy.wait()

    def sent():
        for c in step1 + step2 + step3:
            c.wait_send()

    return one, two, three, four, five, sent


def unit_rows(x):
    centred = x - jnp.mean(x, axis=-1, keepdims=True)
    inverse = lax.rsqrt(jnp.mean(centred * centred, axis=-1, keepdims=True) + 1e-06)
    return centred * inverse, inverse


def fold_rows(x):
    total = x[:8]
    for k in range(1, x.shape[0] // 8):
        total = total + x[8 * k : 8 * (k + 1)]
    return total


def norm_rows_back(grad, unit, inverse, gain):
    scaled = grad * gain
    centred = scaled - jnp.mean(scaled, axis=-1, keepdims=True)
    correction = unit * jnp.mean(scaled * unit, axis=-1, keepdims=True)
    return inverse * (centred - correction)


def split_heads(pair):
    lane = lax.broadcasted_iota(jnp.int32, (1, 2 * HD), 1)
    left = jnp.where(lane < HD, 1.0, 0.0)
    return jnp.concatenate([pair * left.astype(BF), pair * (1.0 - left).astype(BF)], axis=0)


def join_heads(pair):
    lane = lax.broadcasted_iota(jnp.int32, (1, 2 * HD), 1)
    rows = pair.shape[0] // 2
    return jnp.where(lane < HD, pair[:rows], pair[rows:])


def gelu_parts(v):
    inner = jnp.tanh(0.7978845608 * (v + 0.044715 * v * v * v))
    slope = 0.5 * (1.0 + inner) + 0.5 * v * (1.0 - inner * inner) * 0.7978845608 * (
        1.0 + 3.0 * 0.044715 * v * v
    )
    return 0.5 * v * (1.0 + inner), slope


def block_kernel(
    lengths, w_qkv, w_out, router_own, gain_a, shift_a, gain_b, shift_b, tokens, cotangent,
    w_up, w_down,
    block_out, g_blocks, in_stage, rows_low, active, d_rows, d_hidden,
    stage_a, stage_b, full, corner, small, xs, cots, qkv, probs, attended, middle, n_one, n_two,
    disp, comb, dcomb, slots, bias, up, down, out_rows, pair_in, pair_out, row_sums,
    recv_a, recv_b, recv_c, recv_d, send_b, send_d, turned_one, turned_att,
    d_norm, d_diff, d_branch, d_attended, d_qkv, g_rows,
    grads, pairs_buf, inter, out_stage,
    zsend, zrecv, wsend, wrecv, tsend, trecv, csend, crecv, bsend, brecv, gsend, grecv,
    t_local, c_local, b_local, g_local, loads, swap_send, swap_recv,
    send1, recv1, send2, recv2, send3, recv3,
):
    d, z = lax.axis_index("dp"), lax.axis_index("seq")
    width = tokens.shape[2]
    images = tokens.shape[0] // 4
    length = 4 * tokens.shape[1]
    count = images * length
    groups = width // 256
    experts = disp.shape[0]
    devices = recv_a.shape[0]
    base_qkv, base_out = SMALL, SMALL + 3 * width

    barrier = pltpu.get_barrier_semaphore()
    partners = [(d, lax.rem(z + k, 4)) for k in range(1, 4)]
    partners += [(other(d, kind), z) for kind in ("x", "y", "core")]
    for partner in partners:
        pl.semaphore_signal(barrier, inc=1, device_id=partner, device_id_type=MESH)
    load_up = pltpu.make_async_copy(w_up.at[0], up, loads.at[0])
    load_down = pltpu.make_async_copy(w_down.at[0], down, loads.at[1])
    load_up.start()
    load_down.start()
    own_rows = w_out.shape[0]
    corner[...] = jnp.zeros_like(corner)
    corner[0:experts, 0:own_rows] = router_own[...].astype(F32)
    for k, vector in enumerate((gain_a, shift_a, gain_b, shift_b)):
        corner[experts + k : experts + k + 1, 0:own_rows] = vector[...].astype(F32)
    own = w_qkv[...].astype(F32)
    pieces = [corner[...].T[:own_rows]]
    for g in range(groups):
        for k in range(3):
            pieces.append(own[:, k * width + g * 256 : k * width + (g + 1) * 256])
    pieces += [w_out[...].astype(F32), jnp.zeros((own_rows, 128), F32)]
    line = jnp.concatenate(pieces, axis=1)
    cut = 2 * stage_a.shape[2]
    for ref, part in ((stage_a, line[:, :cut]), (stage_b, line[:, cut:])):
        wide = ref.shape[2]
        ref[z] = jnp.concatenate([part[:, :wide], part[:, wide:]], axis=0).astype(BF)
    pl.semaphore_wait(barrier, len(partners))

    weight_sems = (zsend, zrecv, wsend, wrecv)
    wa_start, wa_assemble, wa_one, wa_two, wa_finish, wa_sent = gather_steps(
        stage_a, full, 0, cut, *weight_sems, 0
    )
    wb_start, wb_assemble, wb_one, wb_two, wb_finish, wb_sent = gather_steps(
        stage_b, full, cut, base_out + width, *weight_sems, 1
    )
    t_start, t_arrived, t_sent = image_steps(tokens, xs, tsend, trecv, t_local, images, False)
    c_start, c_arrived, c_sent = image_steps(cotangent, cots, csend, crecv, c_local, images, False)
    wa_start()
    wb_start()
    wa_assemble()
    wb_assemble()
    for i in range(images):
        t_start(i)
    wa_one()
    wa_two()
    wb_one()
    wa_finish()
    small[...] = full[:, 0:128].astype(F32).T[:16]
    gains = [small[8 + k : 9 + k, :] for k in range(4)]
    wb_two()

    def norm_one(k, carry):
        at = ds(k * ROWS, ROWS)
        unit, _ = unit_rows(xs[at, :].astype(F32))
        n_one[at, :] = (unit * gains[0] + gains[1]).astype(BF)
        return carry

    per_image = length // ROWS
    for i in range(images):
        t_arrived(i)
        if i == images - 1:
            for k in range(images):
                c_start(k)
        lax.fori_loop(i * per_image, (i + 1) * per_image, norm_one, 0)
    wb_finish()

    def project(k, carry):
        weight = full[:, ds(base_qkv + k * 256, 256, 128)]
        qkv[:, ds(k * 256, 256)] = mm(n_one[...], weight).astype(BF)
        return carry

    lax.fori_loop(0, 3 * groups, project, 0)

    key = lax.broadcasted_iota(jnp.int32, (1, length), 1)
    for i in range(images):
        bias[i] = jnp.where(key < lengths[z * images + i], 0.0, -1000000000.0)
    scale = jnp.asarray(HD ** (-0.5), BF)
    pairs = 2 * groups

    def heads(t):
        i, p = t // pairs, pairs - 1 - lax.rem(t, pairs)
        base = (p // 2) * 768 + lax.rem(p, 2) * 128
        return i, p, ds(i * length, length), base

    def attend(t, carry):
        i, p, at, base = heads(t)
        keys = split_heads(qkv[at, ds(base + 256, 128)])
        values = split_heads(qkv[at, ds(base + 512, 128)])
        scores = nt(qkv[at, ds(base, 128)] * scale, keys)
        for h in range(2):
            part = scores[:, h * length : (h + 1) * length] + bias[i]
            e = jnp.exp(part - jnp.max(part, axis=-1, keepdims=True))
            total = jnp.sum(e, axis=-1, keepdims=True)
            probs[t, :, h * length : (h + 1) * length] = (e * (1.0 / total)).astype(BF)
        attended[at, ds(p * 128, 128)] = mm(probs[t], values).astype(BF)
        return carry

    lax.fori_loop(0, images * pairs, attend, 0)

    def project_out(k, carry):
        at = ds(k * 256, 256)
        weight = full[:, ds(base_out + k * 256, 256, 128)]
        middle[:, at] = xs[:, at].astype(F32) + mm(attended[...], weight)
        return carry

    lax.fori_loop(0, groups, project_out, 0)

    def norm_two(k, carry):
        at = ds(k * ROWS, ROWS)
        unit, _ = unit_rows(middle[at, :])
        n_two[at, :] = (unit * gains[2] + gains[3]).astype(BF)
        return carry

    lax.fori_loop(0, count // ROWS, norm_two, 0)
    router = small[0:8, :].astype(BF)
    spans = [slice(i * length, (i + 1) * length) for i in range(images)]
    denominators = []
    for i, at in enumerate(spans):
        logits = nt(router, n_two[at, :])
        inside = key < lengths[z * images + i]
        top = jnp.floor(
            jnp.max(jnp.where(inside, logits, -1000000000.0), axis=-1, keepdims=True)
        )
        dispatch = jnp.where(inside, jnp.exp(logits - top), 0.0)
        e = jnp.exp(logits - jnp.max(logits, axis=0, keepdims=True))
        disp[:, at] = dispatch
        comb[:, at] = e / jnp.sum(e, axis=0, keepdims=True)
        denominators.append(jnp.sum(dispatch, axis=-1, keepdims=True))
        slots[i] = mm(dispatch.astype(BF), n_two[at, :]) / denominators[i]

    swap_a = swap_steps(pair_in.at[0], recv_a, swap_send.at[0], swap_recv.at[0], True)
    swap_b = swap_steps(send_b, recv_b, swap_send.at[1], swap_recv.at[1], False)
    swap_c = swap_steps(pair_in.at[1], recv_c, swap_send.at[2], swap_recv.at[2], True)
    swap_d = swap_steps(send_d, recv_d, swap_send.at[3], swap_recv.at[3], False)

    def to_pairs(which, values):
        for e in range(experts):
            pair_in[which, e] = jnp.concatenate(
                [value[e : e + 1] for value in values], axis=0
            ).astype(BF)

    def from_pairs(ref):
        for j in range(devices):
            row_sums[images * j : images * (j + 1), :] = ref[j].astype(F32)
        return row_sums[...].astype(BF)

    def spread(ref, value):
        row_sums[...] = value
        for j in range(devices):
            ref[j] = row_sums[images * j : images * (j + 1), :].astype(BF)

    def collect(ref):
        for e in range(experts):
            total = ref[4 * e].astype(F32)
            for k in range(1, 4):
                total = total + ref[4 * e + k].astype(F32)
            for i in range(images):
                pair_out[i, e : e + 1, :] = total[i : i + 1]
        return [pair_out[i].astype(BF) for i in range(images)]

    to_pairs(0, [slots[i] for i in range(images)])
    swap_a[0]()
    for i in range(images):
        c_arrived(i)
    turned_one[...] = n_one[...].T
    load_up.wait()
    load_down.wait()
    swap_a[1]()
    rows_low[...] = from_pairs(recv_a)
    hidden = mm(rows_low[...], up[...])
    act, slope = gelu_parts(hidden)
    active[...] = act.astype(BF)
    spread(send_b, mm(active[...], down[...]))
    swap_b[0]()
    turned_att[...] = attended[...].T
    swap_b[1]()
    outs = collect(recv_b)
    combs = [comb[:, at].astype(BF) for at in spans]
    sends = []
    for i, at in enumerate(spans):
        sends.append(mm(combs[i], cots[at, :]))
        dcomb[:, at] = nt(outs[i], cots[at, :])
    to_pairs(1, sends)
    swap_c[0]()
    b_start, b_arrived, b_sent = image_steps(
        block_out, out_rows, bsend, brecv, b_local, images, True
    )
    for i, at in enumerate(spans):
        for k in range(groups):
            cols = slice(k * 256, (k + 1) * 256)
            moe = tn(combs[i], outs[i][:, cols])
            out_rows[at, cols] = (middle[at, cols] + moe).astype(BF)
    swap_c[1]()
    d_rows[...] = from_pairs(recv_c)
    d_active = nt(d_rows[...], down[...])
    d_hidden[...] = (d_active * slope).astype(BF)
    spread(send_d, nt(d_hidden[...], up[...]))
    swap_d[0]()
    for i in range(images):
        b_start(i)
    swap_d[1]()
    d_slots = collect(recv_d)

    router_grad = jnp.zeros((experts, width), F32)
    for i, at in enumerate(spans):
        wide_slots = d_slots[i].astype(F32)
        inner = jnp.sum(slots[i] * wide_slots, axis=-1, keepdims=True)
        projected = nt(d_slots[i], n_two[at, :])
        weight, change = comb[:, at], dcomb[:, at]
        d_logits = (projected - inner) / denominators[i] * disp[:, at]
        d_logits = d_logits + weight * (
            change - jnp.sum(weight * change, axis=0, keepdims=True)
        )
        router_grad = router_grad + mm(d_logits.astype(BF), n_two[at, :])
        scaled = wide_slots / denominators[i]
        high = scaled.astype(BF).astype(F32)
        left = jnp.concatenate(
            [disp[:, at], disp[:, at], d_logits, jnp.zeros_like(d_logits)], axis=0
        ).astype(BF)
        right = jnp.concatenate(
            [high, scaled - high, small[0:8, :], jnp.zeros_like(scaled)], axis=0
        ).astype(BF)
        for k in range(groups):
            cols = slice(k * 256, (k + 1) * 256)
            d_norm[at, cols] = tn(left, right[:, cols])

    nothing = jnp.zeros((8, width), F32)

    def back_two(k, carry):
        at = ds(k * ROWS, ROWS)
        grad = d_norm[at, :]
        unit, inverse = unit_rows(middle[at, :])
        change = norm_rows_back(grad, unit, inverse, gains[2])
        d_diff[at, :] = change
        d_branch[at, :] = (change + cots[at, :].astype(F32)).astype(BF)
        return carry[0] + fold_rows(grad * unit), carry[1] + fold_rows(grad)

    gain_two, shift_two = lax.fori_loop(0, count // ROWS, back_two, (nothing, nothing))

    sems = (send1, recv1, send2, recv2, send3, recv3)
    chunks = [
        reduce_steps(
            grads, pairs_buf, inter, out_stage, in_stage, sems, c, lo, hi, narrow
        )
        for c, (lo, hi, narrow) in enumerate(chunk_table(width))
    ]
    c_out, c_pos = chunks[groups], chunks[:groups]

    def grad_out(k, carry):
        cols = ds(k * 256, 256)
        to = ds(base_out + k * 256, 256, 128)
        grads[:, to] = mm(turned_att[...], d_branch[:, cols]).astype(BF)
        return carry

    lax.fori_loop(0, groups, grad_out, 0)
    c_out[0]()

    def back_out(k, carry):
        at = ds(k * 256, 256)
        d_attended[:, at] = nt(d_branch[...], full[at, base_out : base_out + width]).astype(BF)
        return carry

    lax.fori_loop(0, groups, back_out, 0)

    def attend_back(t, carry):
        i, p, at, base = heads(t)
        q = qkv[at, ds(base, 128)] * scale
        keys = split_heads(qkv[at, ds(base + 256, 128)])
        values = split_heads(qkv[at, ds(base + 512, 128)])
        grad = d_attended[at, ds(p * 128, 128)]
        d_values = join_heads(tn(probs[t], grad))
        d_probs = nt(grad, values)
        cuts = []
        for h in range(2):
            cut = slice(h * length, (h + 1) * length)
            weight = probs[t, :, cut].astype(F32)
            change = weight * d_probs[:, cut]
            total = jnp.sum(change, axis=-1, keepdims=True)
            cuts.append((change - weight * total).astype(BF))
        d_scores = jnp.concatenate(cuts, axis=1)
        d_qkv[at, ds(base, 128)] = (mm(d_scores, keys) * HD ** (-0.5)).astype(BF)
        d_qkv[at, ds(base + 256, 128)] = join_heads(tn(d_scores, q)).astype(BF)
        d_qkv[at, ds(base + 512, 128)] = d_values.astype(BF)
        return carry

    def group_grads(g):
        def one(k, carry):
            at = ds(g * 768 + k * 256, 256)
            to = ds(base_qkv + g * 768 + k * 256, 256, 128)
            grads[:, to] = mm(turned_one[...], d_qkv[:, at]).astype(BF)
            return carry

        lax.fori_loop(0, 3, one, 0)

    def input_grads(i, carry):
        at = spans[i]

        def back_qkv(k, carry):
            cols = ds(k * 256, 256)
            d_norm[at, cols] = nt(d_qkv[at, :], full[cols, base_qkv : base_qkv + 3 * width])
            return carry

        def back_one(k, carry):
            at = ds(k * ROWS, ROWS)
            grad = d_norm[at, :]
            unit, inverse = unit_rows(xs[at, :].astype(F32))
            change = norm_rows_back(grad, unit, inverse, gains[0])
            g_rows[at, :] = (change + d_diff[at, :]).astype(BF)
            return carry[0] + fold_rows(grad * unit), carry[1] + fold_rows(grad)

        lax.fori_loop(0, groups, back_qkv, 0)
        carry = lax.fori_loop(i * per_image, (i + 1) * per_image, back_one, carry)
        g_start(i)
        return carry

    g_start, g_arrived, g_sent = image_steps(
        g_blocks, g_rows, gsend, grecv, g_local, images, True
    )
    sums_one = (nothing, nothing)
    for i in range(images - 1):
        lax.fori_loop(i * pairs, (i + 1) * pairs, attend_back, 0)
        if i == 0:
            c_out[1]()
        sums_one = input_grads(i, sums_one)
    begin = (images - 1) * pairs
    lax.fori_loop(begin, begin + 2, attend_back, 0)
    c_out[2]()
    group_grads(2)
    c_pos[2][0]()
    lax.fori_loop(begin + 2, begin + 4, attend_back, 0)
    c_out[3]()
    c_pos[2][1]()
    group_grads(1)
    c_pos[1][0]()
    lax.fori_loop(begin + 4, begin + 6, attend_back, 0)
    c_pos[2][2]()
    c_pos[1][1]()
    gain_one, shift_one = input_grads(images - 1, sums_one)
    sums = [
        jnp.sum(value, axis=0, keepdims=True)
        for value in (gain_one, shift_one, gain_two, shift_two)
    ]
    tall = jnp.concatenate(
        [router_grad] + sums + [jnp.zeros((128 - experts - 4, width), F32)], axis=0
    )
    grads[:, 0:SMALL] = tall.T.astype(BF)
    group_grads(0)
    c_pos[0][0]()
    c_pos[1][2]()
    c_pos[2][3]()
    c_pos[0][1]()
    c_pos[1][3]()
    c_pos[0][2]()
    c_pos[0][3]()
    for i in range(images):
        b_arrived(i)
    c_out[4]()
    c_pos[2][4]()
    c_pos[1][4]()
    for i in range(images):
        g_arrived(i)
    c_pos[0][4]()
    for done in (wa_sent, wb_sent, t_sent, c_sent, b_sent, g_sent):
        done()
    for swap in (swap_a, swap_b, swap_c, swap_d):
        swap[2]()
    for chunk in chunks:
        chunk[5]()


def chunk_table(width):
    groups = width // 256
    table = [(0, SMALL + 768, slice(0, 512))]
    for g in range(1, groups):
        table.append((SMALL + g * 768, SMALL + (g + 1) * 768, slice(128 + g * 384, 512 + g * 384)))
    end = 128 + groups * 384
    table.append((SMALL + 3 * width, SMALL + 4 * width, slice(end, end + width // 2)))
    return table


def finish_kernel(
    out_in, diff, cotangent, parts, rows_low, active, d_rows, d_hidden,
    block_out, grad_input, grad_qkv, grad_out_w, grad_small, grad_up, grad_down,
):
    block_out[...] = out_in[...]
    grad_input[...] = diff[...].astype(F32) + cotangent[...].astype(F32)
    grad_up[0] = tn(rows_low[...], d_hidden[...])
    grad_down[0] = tn(active[...], d_rows[...])

    @pl.when(pl.program_id(0) == 0)
    def _():
        width = grad_out_w.shape[1]
        quarter = grad_out_w.shape[0]
        total = parts[0].astype(F32)
        for k in range(1, 4):
            total = total + parts[k].astype(F32)
        for c, (lo, hi, narrow) in enumerate(chunk_table(width)):
            both = jnp.concatenate([total[:quarter, narrow], total[quarter:, narrow]], axis=1)
            if c == width // 256:
                grad_out_w[...] = both
                continue
            if c == 0:
                square = jnp.concatenate(
                    [both[:, :SMALL], jnp.zeros((128 - quarter, SMALL), F32)], axis=0
                )
                grad_small[...] = square.T[:16]
                both = both[:, SMALL:]
            for k in range(3):
                grad_qkv[:, k * width + c * 256 : k * width + (c + 1) * 256] = both[
                    :, k * 256 : (k + 1) * 256
                ]


def kernel_plan(
    tokens, lengths, w_qkv, w_out, router, gain_one, shift_one, gain_two, shift_two,
    w_up, w_down, cotangent,
):
    own_rows, width = w_out.shape
    blocks, size = tokens.shape[:2]
    images, length, experts = blocks // 4, 4 * size, router.shape[1]
    count = images * length
    groups = width // 256
    pairs = 2 * groups
    devices = 4 * experts
    columns = 4 * width + SMALL
    fan = w_up.shape[2]
    wide_a, wide_b = width, width + 128
    quarter = 4 * own_rows
    pair = (images, width)
    rows = devices * images

    def shape(*dims, kind=F32):
        return jax.ShapeDtypeStruct(dims, kind)

    dma = pltpu.SemaphoreType.DMA
    vmem, anywhere = pl.BlockSpec(memory_space=VM), pl.BlockSpec(memory_space=pl.ANY)
    stage_wide = 512 + (groups - 1) * 384 + width // 2
    outs = (
        shape(*tokens.shape, kind=BF),
        shape(*tokens.shape, kind=BF),
        shape(4, 2 * own_rows, stage_wide, kind=BF),
        shape(rows, width, kind=BF),
        shape(rows, fan, kind=BF),
        shape(rows, width, kind=BF),
        shape(rows, fan, kind=BF),
    )
    scratch = [
        VM((4, 2 * own_rows, wide_a), BF),
        VM((4, 2 * own_rows, wide_b), BF),
        VM((width, wide_a * 2 + wide_b * 2), BF),
        VM((128, 128), F32),
        VM((16, width), F32),
        VM((count, width), BF),
        VM((count, width), BF),
        VM((count, 3 * width), BF),
        VM((images * pairs, length, 2 * length), BF),
        VM((count, width), BF),
        VM((count, width), F32),
        VM((count, width), BF),
        VM((count, width), BF),
        VM((experts, count), F32),
        VM((experts, count), F32),
        VM((experts, count), F32),
        VM((images, experts, width), F32),
        VM((images, 1, length), F32),
        VM((width, fan), BF),
        VM((fan, width), BF),
        VM((count, width), BF),
        VM((2, experts) + pair, BF),
        VM((images, experts, width), F32),
        VM((rows, width), F32),
    ]
    scratch += [VM((devices,) + pair, BF)] * 6
    scratch += [
        VM((width, count), BF),
        VM((width, count), BF),
        VM((count, width), F32),
        VM((count, width), F32),
        VM((count, width), BF),
        VM((count, width), BF),
        VM((count, 3 * width), BF),
        VM((count, width), BF),
        VM((width, columns), BF),
        VM((4, quarter, columns), BF),
        VM((6, quarter // 2, columns), BF),
        VM((4, 2 * own_rows, stage_wide), BF),
    ]
    scratch += [dma((6,)), dma((6,)), dma((26,)), dma((26,))]
    scratch += [dma((3 * images,))] * 8
    scratch += [dma((images,))] * 4
    scratch += [dma((2,)), dma((4,)), dma((4,))]
    chunks = groups + 1
    scratch += [dma((4 * chunks,))] * 2 + [dma((6 * chunks,))] * 2 + [dma((4 * chunks,))] * 2
    vectors = [vec[None, :] for vec in (gain_one, shift_one, gain_two, shift_two)]
    out_in, diff, parts, rows_low, active, d_rows, d_hidden = pl.pallas_call(
        block_kernel,
        out_shape=outs,
        in_specs=[pl.BlockSpec(memory_space=pltpu.SMEM)] + [vmem] * 7 + [anywhere] * 4,
        out_specs=[anywhere] * 3 + [vmem] * 4,
        scratch_shapes=scratch,
        compiler_params=pltpu.CompilerParams(
            collective_id=0, has_side_effects=True, vmem_limit_bytes=63 * 2**20
        ),
        name="block",
    )(lengths, w_qkv, w_out, router.T, *vectors, tokens, cotangent, w_up, w_down)

    def by_columns(*dims):
        return pl.BlockSpec(dims + (256,), lambda k: (0,) * len(dims) + (k,))

    def whole(*dims):
        return pl.BlockSpec(dims, lambda k: (0,) * len(dims))

    block_out, grad_input, grad_qkv, grad_out_w, grad_small, grad_up, grad_down = pl.pallas_call(
        finish_kernel,
        grid=(groups,),
        out_shape=(
            shape(*tokens.shape, kind=BF),
            shape(*tokens.shape),
            shape(own_rows, 3 * width),
            shape(own_rows, width),
            shape(16, 128),
            shape(*w_up.shape),
            shape(*w_down.shape),
        ),
        in_specs=[
            by_columns(blocks, size),
            by_columns(blocks, size),
            by_columns(blocks, size),
            whole(4, 2 * own_rows, stage_wide),
            whole(rows, width),
            whole(rows, fan),
            by_columns(rows),
            by_columns(rows),
        ],
        out_specs=[
            by_columns(blocks, size),
            by_columns(blocks, size),
            whole(own_rows, 3 * width),
            whole(own_rows, width),
            whole(16, 128),
            by_columns(1, width),
            by_columns(1, fan),
        ],
        compiler_params=pltpu.CompilerParams(vmem_limit_bytes=63 * 2**20),
        name="finish",
    )(out_in, diff, cotangent, parts, rows_low, active, d_rows, d_hidden)
    return (
        block_out,
        grad_input,
        grad_qkv,
        grad_out_w,
        grad_small[:experts, :own_rows].T,
        grad_small[experts, :own_rows],
        grad_small[experts + 1, :own_rows],
        grad_small[experts + 2, :own_rows],
        grad_small[experts + 3, :own_rows],
        grad_up,
        grad_down,
    )


def solution(mesh):
    plan = kernel_plan if dict(mesh.shape) == {"dp": 8, "seq": 4} else plain_plan
    rows, vector = P(("dp", "seq"), None), P(("dp", "seq"))
    tokens = P("dp", "seq", None)
    up, down = P("dp", None, "seq"), P("dp", "seq", None)
    return jax.shard_map(
        plan,
        mesh=mesh,
        in_specs=(tokens, P("dp"), rows, rows, rows)
        + (vector,) * 4
        + (up, down, tokens),
        out_specs=(tokens, tokens, rows, rows, rows) + (vector,) * 4 + (up, down),
        check_vma=False,
    )
```

```python
import jax
import jax.numpy as jnp
from jax import lax
from jax.experimental import pallas as pl
from jax.experimental.pallas import tpu as pltpu
from jax.sharding import PartitionSpec as P

H = 12
HD = 64
BF = jnp.bfloat16
F32 = jnp.float32


def dot(spec, a, b):
    return jnp.einsum(spec, a, b, preferred_element_type=F32)


def unit_norm(values):
    centred = values - jnp.mean(values, axis=-1, keepdims=True)
    inverse = lax.rsqrt(jnp.mean(centred * centred, axis=-1, keepdims=True) + 1e-06)
    return centred * inverse, inverse


def norm_back(grad_rows, unit_rows, inverse, gain):
    scaled = grad_rows * gain
    centred = scaled - jnp.mean(scaled, axis=-1, keepdims=True)
    correction = unit_rows * jnp.mean(scaled * unit_rows, axis=-1, keepdims=True)
    return (
        inverse * (centred - correction),
        jnp.sum(grad_rows * unit_rows, axis=(0, 1)),
        jnp.sum(grad_rows, axis=(0, 1)),
    )


def gelu_tanh(values):
    return jax.nn.gelu(values, approximate=True)


def to_images(array):
    return lax.all_to_all(array, "seq", split_axis=0, concat_axis=1, tiled=True)


def to_blocks(array):
    return lax.all_to_all(array, "seq", split_axis=1, concat_axis=0, tiled=True)


def to_experts(rows):
    rows = lax.all_to_all(rows, "dp", split_axis=1, concat_axis=0, tiled=True)
    return lax.all_gather(rows, "seq", axis=0, tiled=True)


def from_experts(rows):
    rows = lax.psum_scatter(rows, "seq", scatter_dimension=0, tiled=True).astype(BF)
    return lax.all_to_all(rows, "dp", split_axis=0, concat_axis=1, tiled=True)


def plain_plan(
    tokens, lengths, w_qkv, w_out, router, gain_one, shift_one, gain_two, shift_two,
    w_up, w_down, cotangent,
):
    groups = lax.axis_size("seq")
    model_width, slots_all = w_qkv.shape[1] // 3, router.shape[1]
    packed = jnp.concatenate(
        [w_qkv, w_out, router]
        + [vec[:, None] for vec in (gain_one, shift_one, gain_two, shift_two)],
        axis=1,
    )
    packed = lax.all_gather(packed, ("dp", "seq"), axis=0, tiled=True)
    split = 4 * model_width
    w_qkv, w_out = packed[:, : 3 * model_width], packed[:, 3 * model_width : split]
    router = packed[:, split : split + slots_all]
    gain_one, shift_one, gain_two, shift_two = (
        packed[:, split + slots_all + k].astype(F32) for k in range(4)
    )
    x = to_images(tokens).astype(F32)
    cot = to_images(cotangent)
    images, length_all = x.shape[:2]
    lengths_own = lax.dynamic_slice_in_dim(lengths, lax.axis_index("seq") * images, images)
    valid = jnp.arange(length_all, dtype=jnp.int32)[None, :] < lengths_own[:, None]

    unit_one, inverse_one = unit_norm(x)
    normed_one = (unit_one * gain_one + shift_one).astype(BF)
    qkv = dot("btd,de->bte", normed_one, w_qkv).astype(BF).reshape(images, length_all, 3, H, HD)
    queries, keys_all, values_all = qkv[:, :, 0], qkv[:, :, 1], qkv[:, :, 2]
    scores = dot("bqhd,bkhd->bhqk", queries, keys_all) * HD ** (-0.5)
    probs = jax.nn.softmax(jnp.where(valid[:, None, None, :], scores, -1000000000.0), axis=-1)
    probs_low = probs.astype(BF)
    attended = dot("bhqk,bkhd->bqhd", probs_low, values_all).astype(BF)
    attended = attended.reshape(images, length_all, model_width)
    middle = x + dot("btd,de->bte", attended, w_out)
    unit_two, inverse_two = unit_norm(middle)
    normed_two = (unit_two * gain_two + shift_two).astype(BF)
    logits = dot("btd,de->bte", normed_two, router)
    top = jnp.floor(jnp.max(jnp.where(valid[:, :, None], logits, -1000000000.0), axis=1))
    dispatch = jnp.where(valid[:, :, None], jnp.exp(logits - top[:, None, :]), 0.0)
    dispatch_low = dispatch.astype(BF)
    denominator = jnp.sum(dispatch, axis=1)
    slot_vals = dot("bte,btd->bed", dispatch_low, normed_two) / denominator[:, :, None]
    slot_rows = to_experts(slot_vals.astype(BF))
    hidden = dot("red,edf->ref", slot_rows, w_up)
    active = gelu_tanh(hidden).astype(BF)
    expert_out = from_experts(dot("ref,efd->red", active, w_down))
    combine = jax.nn.softmax(logits, axis=-1)
    combine_low = combine.astype(BF)
    block_out = (middle + dot("bte,bed->btd", combine_low, expert_out)).astype(BF)

    d_combine = dot("btd,bed->bte", cot, expert_out)
    d_expert = dot("bte,btd->bed", combine_low, cot).astype(BF)
    d_rows = to_experts(d_expert)
    d_active = dot("red,efd->ref", d_rows, w_down)
    grad_down = dot("ref,red->efd", active, d_rows)
    d_hidden = jax.vjp(gelu_tanh, hidden)[1](d_active)[0].astype(BF)
    grad_up = dot("red,ref->edf", slot_rows, d_hidden)
    d_slots = from_experts(dot("ref,edf->red", d_hidden, w_up))
    d_slots_wide = d_slots.astype(F32)
    inner = jnp.sum(slot_vals * d_slots_wide, axis=-1)
    projected = dot("btd,bed->bte", normed_two, d_slots)
    d_logits = (projected - inner[:, None, :]) / denominator[:, None, :] * dispatch
    d_logits = d_logits + combine * (
        d_combine - jnp.sum(combine * d_combine, axis=-1, keepdims=True)
    )
    d_logits = d_logits.astype(BF)
    scaled = d_slots_wide / denominator[:, :, None]
    scaled_high = scaled.astype(BF)
    scaled_rest = (scaled - scaled_high.astype(F32)).astype(BF)
    d_normed_two = (
        dot("bte,bed->btd", dispatch_low, scaled_high)
        + dot("bte,bed->btd", dispatch_low, scaled_rest)
        + dot("bte,de->btd", d_logits, router)
    )
    grad_router = dot("btd,bte->de", normed_two, d_logits)
    d_norm, grad_gain_two, grad_shift_two = norm_back(d_normed_two, unit_two, inverse_two, gain_two)
    d_middle = cot.astype(F32) + d_norm
    d_branch = d_middle.astype(BF)
    grad_out_w = dot("btd,bte->de", attended, d_branch)
    d_attended = dot("bte,de->btd", d_branch, w_out).astype(BF)
    d_attended = d_attended.reshape(images, length_all, H, HD)
    d_values = dot("bhqk,bqhd->bkhd", probs_low, d_attended)
    d_probs = dot("bqhd,bkhd->bhqk", d_attended, values_all)
    d_scores = probs * (d_probs - jnp.sum(probs * d_probs, axis=-1, keepdims=True))
    d_scores = d_scores.astype(BF)
    d_queries = dot("bhqk,bkhd->bqhd", d_scores, keys_all) * HD ** (-0.5)
    d_keys = dot("bhqk,bqhd->bkhd", d_scores, queries) * HD ** (-0.5)
    d_qkv = jnp.stack([d_queries, d_keys, d_values], axis=2).astype(BF)
    d_qkv = d_qkv.reshape(images, length_all, 3 * model_width)
    grad_qkv = dot("btd,bte->de", normed_one, d_qkv)
    d_normed_one = dot("bte,de->btd", d_qkv, w_qkv)
    d_norm, grad_gain_one, grad_shift_one = norm_back(d_normed_one, unit_one, inverse_one, gain_one)
    grad_input = to_blocks(d_middle + d_norm)

    vectors = (grad_gain_one, grad_shift_one, grad_gain_two, grad_shift_two)
    packed = jnp.concatenate(
        [grad_qkv, grad_out_w, grad_router] + [vec[:, None] for vec in vectors], axis=1
    )
    packed = lax.psum_scatter(packed, ("dp", "seq"), scatter_dimension=0, tiled=True)
    return (
        to_blocks(block_out),
        grad_input,
        packed[:, : 3 * model_width],
        packed[:, 3 * model_width : split],
        packed[:, split : split + slots_all],
        packed[:, split + slots_all],
        packed[:, split + slots_all + 1],
        packed[:, split + slots_all + 2],
        packed[:, split + slots_all + 3],
        grad_up,
        grad_down,
    )


MESH = pl.DeviceIdType.MESH
VM = pltpu.VMEM
SMALL = 128
ROWS = 64


def nt(a, b):
    return lax.dot_general(a, b, (((1,), (1,)), ((), ())), preferred_element_type=F32)


def tn(a, b):
    return lax.dot_general(a, b, (((0,), (0,)), ((), ())), preferred_element_type=F32)


def mm(a, b):
    return jnp.dot(a, b, preferred_element_type=F32)


def ds(start, size, unit=None):
    return pl.ds(pl.multiple_of(start, unit or size), size)


def remote(src, dst, send, recv, device):
    return pltpu.make_async_remote_copy(
        src_ref=src, dst_ref=dst, send_sem=send, recv_sem=recv, device_id=device,
        device_id_type=MESH,
    )


def other(d, kind):
    core, x, y = lax.rem(d, 2), lax.rem(d // 2, 2), d // 4
    return {"x": d + 2 - 4 * x, "y": d + 4 - 8 * y, "core": d + 1 - 2 * core}[kind]


class Gather:
    def __init__(self, shards, full, zup, zdown, zrecv, xsend, xrecv, ysend, yrecv, csend, crecv, dsend, drecv):
        d, z = lax.axis_index("dp"), lax.axis_index("seq")
        dx, dy, dc = other(d, "x"), other(d, "y"), other(d, "core")
        self.shards, self.full, self.z = shards, full, z
        self.owners = (d, dx, dy, other(dx, "y"))
        self.over = {"x": (dx, z), "y": (dy, z), "core": (dc, z)}
        self.up, self.down = (d, lax.rem(z + 1, 4)), (d, lax.rem(z + 3, 4))
        self.sems = {
            "up": (zup, zrecv), "down": (zdown, zrecv), "x": (xsend, xrecv),
            "y": (ysend, yrecv), "core": (csend, crecv), "d": (dsend, drecv),
        }

    def copy(self, kind, owner, s, device, sem):
        ref = self.shards.at[owner * 4 + s]
        send, recv = self.sems[kind]
        return remote(ref, ref, send.at[sem], recv.at[sem], device)

    def pass_on(self, s, upward, downward):
        d, z = self.owners[0], self.z
        if upward:

            @pl.when(z < 3)
            def _():
                self.copy("up", d, s, self.up, s).start()

        if downward:

            @pl.when(z > 0)
            def _():
                self.copy("down", d, s, self.down, s).start()

        self.copy("x", d, s, self.over["x"], s).start()
        self.copy("y", d, s, self.over["y"], s).start()
        self.copy("core", d, s, self.over["core"], s).start()

    def each(self, h, act):
        if h == 0:
            act(self.z)
            return

        @pl.when(self.z >= h)
        def _():
            act(self.z - h)

        @pl.when(self.z + h <= 3)
        def _():
            act(self.z + h)

    def line(self, h):
        d, z = self.owners[0], self.z
        if h == 0:
            self.pass_on(z, True, True)
            return

        @pl.when(z >= h)
        def _():
            self.copy("up", d, z - h, self.up, z - h).wait_recv()
            self.pass_on(z - h, True, False)

        @pl.when(z + h <= 3)
        def _():
            self.copy("down", d, z + h, self.down, z + h).wait_recv()
            self.pass_on(z + h, False, True)

    def plane(self, h):
        d, dx, dy, dd = self.owners

        def act(s):
            self.copy("x", dx, s, self.over["x"], s).wait_recv()

            @pl.when(lax.rem(s, 2) == 0)
            def _():
                self.copy("d", dx, s, self.over["y"], s).start()

            self.copy("core", dx, s, self.over["core"], 4 + s).start()
            self.copy("y", dy, s, self.over["y"], s).wait_recv()

            @pl.when(lax.rem(s, 2) == 1)
            def _():
                self.copy("d", dy, s, self.over["x"], s).start()

            self.copy("core", dy, s, self.over["core"], 8 + s).start()

        self.each(h, act)

    def diagonal(self, h):
        def act(s):
            self.copy("d", self.owners[3], s, self.over["x"], s).wait_recv()
            self.copy("core", self.owners[3], s, self.over["core"], 12 + s).start()

        self.each(h, act)

    def twin(self, k):
        dc = other(self.owners[k], "core")
        for s in range(4):
            self.copy("core", dc, s, self.over["core"], 4 * k + s).wait_recv()
        self.assemble(dc)

    def assemble(self, owner):
        half, wide = self.shards.shape[1:]
        quarter = half // 2
        for side in range(2):
            value = jnp.concatenate(
                [
                    self.shards[owner * 4 + k].astype(F32)[side * quarter : (side + 1) * quarter]
                    for k in range(4)
                ],
                axis=0,
            )
            self.full[ds(owner * 2 * half, 2 * half), side * wide : (side + 1) * wide] = (
                value.astype(BF)
            )

    def sent(self):
        d, z = self.owners[0], self.z

        def one(s, carry):
            @pl.when((s <= z) & (z < 3))
            def _():
                self.copy("up", d, s, self.up, s).wait_send()

            @pl.when((s >= z) & (z > 0))
            def _():
                self.copy("down", d, s, self.down, s).wait_send()

            self.copy("x", d, s, self.over["x"], s).wait_send()
            self.copy("y", d, s, self.over["y"], s).wait_send()
            self.copy("d", d, s, self.over["x"], s).wait_send()
            for k in range(4):
                self.copy("core", self.owners[k], s, self.over["core"], 4 * k + s).wait_send()
            return carry

        lax.fori_loop(0, 4, one, 0)


def image_steps(blocks, whole, send, recv, local_sem, images, home):
    d, z = lax.axis_index("dp"), lax.axis_index("seq")
    size = blocks.shape[1]
    length = 4 * size

    def make(i, k):
        there = lax.rem(z + k, 4)
        if home:
            src = whole.at[ds(i * length + there * size, size)]
            dst = blocks.at[z * images + i]
        else:
            src = blocks.at[there * images + i]
            dst = whole.at[ds(i * length + z * size, size)]
        if k == 0:
            return pltpu.make_async_copy(src, dst, local_sem.at[i])
        return remote(src, dst, send.at[i * 3 + k - 1], recv.at[i * 3 + k - 1], (d, there))

    table = [[make(i, k) for k in range(4)] for i in range(images)]

    def start(i):
        for one in table[i]:
            one.start()

    def arrived(i):
        table[i][0].wait()
        for one in table[i][1:]:
            one.wait_recv()

    def sent():
        for i in range(images):
            for one in table[i][1:]:
                one.wait_send()

    return start, arrived, sent


def swap_steps(src, dst, send, recv, to_expert):
    d, z = lax.axis_index("dp"), lax.axis_index("seq")
    count = dst.shape[0]
    me = d * 4 + z

    def start():
        def one(k, carry):
            j = lax.rem(me + k, count)
            e = j // 4
            row = src.at[e] if to_expert else src.at[j]
            remote(row, dst.at[me], send, recv, (e, lax.rem(j, 4))).start()
            return carry

        lax.fori_loop(1, count, one, 0)
        pltpu.make_async_copy(src.at[d] if to_expert else src.at[me], dst.at[me], recv).start()

    def arrived():
        pltpu.make_async_copy(dst, dst, recv).wait()

    def sent():
        part = dst.at[pl.ds(0, count - 1)]
        remote(part, part, send, recv, (other(d, "x"), z)).wait_send()

    return start, arrived, sent


def reduce_steps(grads, pairs, inter, out_stage, in_stage, sems, chunk, lo, hi, narrow):
    d, z = lax.axis_index("dp"), lax.axis_index("seq")
    dx, dy, dc = other(d, "x"), other(d, "y"), other(d, "core")
    core = lax.rem(d, 2)
    over_x, over_y, over_c = (dx, z), (dy, z), (dc, z)
    rows = pairs.shape[1]
    half, quarter = rows // 2, rows // 4
    cols = slice(lo, hi)
    send1, recv1, send2, recv2, send3, recv3 = sems
    chips = pairs.shape[0]

    step1 = []
    for m in range(chips):
        block = grads.at[ds((2 * m + 1 - core) * rows, rows), cols]
        n = chunk * chips + m
        step1.append(remote(block, pairs.at[m, :, cols], send1.at[n], recv1.at[n], over_c))
    here, mx, my, md = d // 2, dx // 2, dy // 2, other(dx, "y") // 2

    def part(m, h):
        return pairs.at[m, h * half : (h + 1) * half, cols]

    def hop(k, m, h, device):
        n = chunk * 6 + k
        return remote(part(m, h), inter.at[k, :, cols], send2.at[n], recv2.at[n], device)

    step2 = [
        hop(0, md, 0, over_y), hop(1, md, 1, over_x), hop(2, my, 0, over_y),
        hop(3, mx, 1, over_x), hop(4, mx, 0, over_x), hop(5, my, 1, over_y),
    ]
    local_copy = pltpu.make_async_copy(
        out_stage.at[z, :, narrow], in_stage.at[3, :, narrow], recv3.at[chunk * 4 + 3]
    )
    step3 = []
    for k in range(1, 4):
        n = chunk * 4 + k - 1
        there = lax.rem(z + k, 4)
        step3.append(
            remote(
                out_stage.at[there, :, narrow], in_stage.at[k - 1, :, narrow],
                send3.at[n], recv3.at[n], (d, there),
            )
        )

    def one():
        for c in step1:
            c.start()

    def two():
        for m in range(chips):
            step1[m].wait_recv()
            own = grads[ds((2 * m + core) * rows, rows), cols].astype(F32)
            pairs[m, :, cols] = (own + pairs[m, :, cols].astype(F32)).astype(BF)
        for k in range(4):
            step2[k].start()

    def three():
        for k, m, h in ((0, mx, 0), (1, my, 1)):
            step2[k].wait_recv()
            at = slice(h * half, (h + 1) * half)
            total = pairs[m, at, cols].astype(F32) + inter[k, :, cols].astype(F32)
            pairs[m, at, cols] = total.astype(BF)
            step2[4 + k].start()

    def four():
        for k in (2, 3, 4, 5):
            step2[k].wait_recv()
        own = pairs[here, :, cols].astype(F32)
        top = own[:half] + inter[2, :, cols].astype(F32) + inter[4, :, cols].astype(F32)
        low = own[half:] + inter[3, :, cols].astype(F32) + inter[5, :, cols].astype(F32)
        total = jnp.concatenate([top, low], axis=0)
        middle = narrow.stop - narrow.start
        if 2 * middle > hi - lo:
            filler = jnp.zeros((rows, 2 * middle - (hi - lo)), F32)
            total = jnp.concatenate([total, filler], axis=1)
        for t in range(4):
            shard = total[t * quarter : (t + 1) * quarter]
            both = jnp.concatenate([shard[:, :middle], shard[:, middle:]], axis=0)
            out_stage[t, :, narrow] = both.astype(BF)
        for c in step3:
            c.start()
        local_copy.start()

    def five():
        for c in step3:
            c.wait_recv()
        local_copy.wait()

    def sent():
        for c in step1 + step2 + step3:
            c.wait_send()

    return one, two, three, four, five, sent


def unit_rows(x):
    centred = x - jnp.mean(x, axis=-1, keepdims=True)
    inverse = lax.rsqrt(jnp.mean(centred * centred, axis=-1, keepdims=True) + 1e-06)
    return centred * inverse, inverse


def fold_rows(x):
    total = x[:8]
    for k in range(1, x.shape[0] // 8):
        total = total + x[8 * k : 8 * (k + 1)]
    return total


def norm_rows_back(grad, unit, inverse, gain):
    scaled = grad * gain
    centred = scaled - jnp.mean(scaled, axis=-1, keepdims=True)
    correction = unit * jnp.mean(scaled * unit, axis=-1, keepdims=True)
    return inverse * (centred - correction)


def split_heads(pair):
    lane = lax.broadcasted_iota(jnp.int32, (1, 2 * HD), 1)
    left = jnp.where(lane < HD, 1.0, 0.0)
    return jnp.concatenate([pair * left.astype(BF), pair * (1.0 - left).astype(BF)], axis=0)


def join_heads(pair):
    lane = lax.broadcasted_iota(jnp.int32, (1, 2 * HD), 1)
    rows = pair.shape[0] // 2
    return jnp.where(lane < HD, pair[:rows], pair[rows:])


def gelu_parts(v):
    inner = jnp.tanh(0.7978845608 * (v + 0.044715 * v * v * v))
    slope = 0.5 * (1.0 + inner) + 0.5 * v * (1.0 - inner * inner) * 0.7978845608 * (
        1.0 + 3.0 * 0.044715 * v * v
    )
    return 0.5 * v * (1.0 + inner), slope


def block_kernel(
    lengths, w_qkv, w_out, router_own, gain_a, shift_a, gain_b, shift_b, tokens, cotangent,
    w_up, w_down,
    block_out, g_blocks, in_stage, rows_low, active, d_rows, d_hidden,
    shards, full, corner, small, xs, cots, qkv, probs, attended, middle, n_one, n_two,
    disp, comb, dcomb, slots, bias, up, down, out_rows, pair_in, pair_out, row_sums,
    recv_a, recv_b, recv_c, recv_d, send_b, send_d, turned_one, turned_att,
    d_norm, d_diff, d_branch, d_attended, d_qkv, g_rows,
    grads, pairs_buf, inter, out_stage,
    zup, zdown, zrecv, xsend, xrecv, ysend, yrecv, wsend, wrecv, dsend, drecv, tsend, trecv, csend, crecv, bsend, brecv, gsend, grecv,
    t_local, c_local, b_local, g_local, loads, swap_send, swap_recv,
    send1, recv1, send2, recv2, send3, recv3,
):
    d, z = lax.axis_index("dp"), lax.axis_index("seq")
    width = tokens.shape[2]
    images = tokens.shape[0] // 4
    length = 4 * tokens.shape[1]
    count = images * length
    groups = width // 256
    experts = disp.shape[0]
    devices = recv_a.shape[0]
    base_qkv, base_out = SMALL, SMALL + 3 * width

    barrier = pltpu.get_barrier_semaphore()
    partners = [(d, lax.rem(z + k, 4)) for k in range(1, 4)]
    partners += [(other(d, kind), z) for kind in ("x", "y", "core")]
    for partner in partners:
        pl.semaphore_signal(barrier, inc=1, device_id=partner, device_id_type=MESH)
    load_up = pltpu.make_async_copy(w_up.at[0], up, loads.at[0])
    load_down = pltpu.make_async_copy(w_down.at[0], down, loads.at[1])
    load_up.start()
    load_down.start()
    own_rows = w_out.shape[0]
    corner[...] = jnp.zeros_like(corner)
    corner[0:experts, 0:own_rows] = router_own[...].astype(F32)
    for k, vector in enumerate((gain_a, shift_a, gain_b, shift_b)):
        corner[experts + k : experts + k + 1, 0:own_rows] = vector[...].astype(F32)
    own = w_qkv[...].astype(F32)
    pieces = [corner[...].T[:own_rows]]
    for g in range(groups):
        for k in range(3):
            pieces.append(own[:, k * width + g * 256 : k * width + (g + 1) * 256])
    pieces += [w_out[...].astype(F32), jnp.zeros((own_rows, 128), F32)]
    line = jnp.concatenate(pieces, axis=1)
    wide = shards.shape[2]
    shards[d * 4 + z] = jnp.concatenate([line[:, :wide], line[:, wide:]], axis=0).astype(BF)
    pl.semaphore_wait(barrier, len(partners))

    gather = Gather(
        shards, full, zup, zdown, zrecv, xsend, xrecv, ysend, yrecv, wsend, wrecv, dsend, drecv
    )
    t_start, t_arrived, t_sent = image_steps(tokens, xs, tsend, trecv, t_local, images, False)
    c_start, c_arrived, c_sent = image_steps(cotangent, cots, csend, crecv, c_local, images, False)
    gather.line(0)
    gather.line(1)
    gather.plane(0)
    gather.line(2)
    gather.plane(1)
    gather.diagonal(0)
    gather.line(3)
    for i in range(images):
        t_start(i)
    gather.plane(2)
    gather.diagonal(1)
    gather.assemble(d)
    gather.plane(3)
    gather.diagonal(2)
    gather.twin(0)
    gather.diagonal(3)
    for k in range(1, 4):
        gather.assemble(gather.owners[k])
        gather.twin(k)
    small[...] = full[:, 0:128].astype(F32).T[:16]
    gains = [small[8 + k : 9 + k, :] for k in range(4)]

    def norm_one(k, carry):
        at = ds(k * ROWS, ROWS)
        unit, _ = unit_rows(xs[at, :].astype(F32))
        n_one[at, :] = (unit * gains[0] + gains[1]).astype(BF)
        return carry

    per_image = length // ROWS
    for i in range(images):
        t_arrived(i)
        if i == images - 1:
            for k in range(images):
                c_start(k)
        lax.fori_loop(i * per_image, (i + 1) * per_image, norm_one, 0)

    def project(k, carry):
        weight = full[:, ds(base_qkv + k * 256, 256, 128)]
        qkv[:, ds(k * 256, 256)] = mm(n_one[...], weight).astype(BF)
        return carry

    lax.fori_loop(0, 3 * groups, project, 0)

    key = lax.broadcasted_iota(jnp.int32, (1, length), 1)
    for i in range(images):
        bias[i] = jnp.where(key < lengths[z * images + i], 0.0, -1000000000.0)
    scale = jnp.asarray(HD ** (-0.5), BF)
    pairs = 2 * groups

    def heads(t):
        i, p = t // pairs, pairs - 1 - lax.rem(t, pairs)
        base = (p // 2) * 768 + lax.rem(p, 2) * 128
        return i, p, ds(i * length, length), base

    def attend(t, carry):
        i, p, at, base = heads(t)
        keys = split_heads(qkv[at, ds(base + 256, 128)])
        values = split_heads(qkv[at, ds(base + 512, 128)])
        scores = nt(qkv[at, ds(base, 128)] * scale, keys)
        for h in range(2):
            part = scores[:, h * length : (h + 1) * length] + bias[i]
            e = jnp.exp(part - jnp.max(part, axis=-1, keepdims=True))
            total = jnp.sum(e, axis=-1, keepdims=True)
            probs[t, :, h * length : (h + 1) * length] = (e * (1.0 / total)).astype(BF)
        attended[at, ds(p * 128, 128)] = mm(probs[t], values).astype(BF)
        return carry

    lax.fori_loop(0, images * pairs, attend, 0)

    def project_out(k, carry):
        at = ds(k * 256, 256)
        weight = full[:, ds(base_out + k * 256, 256, 128)]
        middle[:, at] = xs[:, at].astype(F32) + mm(attended[...], weight)
        return carry

    lax.fori_loop(0, groups, project_out, 0)

    def norm_two(k, carry):
        at = ds(k * ROWS, ROWS)
        unit, _ = unit_rows(middle[at, :])
        n_two[at, :] = (unit * gains[2] + gains[3]).astype(BF)
        return carry

    lax.fori_loop(0, count // ROWS, norm_two, 0)
    router = small[0:8, :].astype(BF)
    spans = [slice(i * length, (i + 1) * length) for i in range(images)]
    denominators = []
    for i, at in enumerate(spans):
        logits = nt(router, n_two[at, :])
        inside = key < lengths[z * images + i]
        top = jnp.floor(
            jnp.max(jnp.where(inside, logits, -1000000000.0), axis=-1, keepdims=True)
        )
        dispatch = jnp.where(inside, jnp.exp(logits - top), 0.0)
        e = jnp.exp(logits - jnp.max(logits, axis=0, keepdims=True))
        disp[:, at] = dispatch
        comb[:, at] = e / jnp.sum(e, axis=0, keepdims=True)
        denominators.append(jnp.sum(dispatch, axis=-1, keepdims=True))
        slots[i] = mm(dispatch.astype(BF), n_two[at, :]) / denominators[i]

    swap_a = swap_steps(pair_in.at[0], recv_a, swap_send.at[0], swap_recv.at[0], True)
    swap_b = swap_steps(send_b, recv_b, swap_send.at[1], swap_recv.at[1], False)
    swap_c = swap_steps(pair_in.at[1], recv_c, swap_send.at[2], swap_recv.at[2], True)
    swap_d = swap_steps(send_d, recv_d, swap_send.at[3], swap_recv.at[3], False)

    def to_pairs(which, values):
        for e in range(experts):
            pair_in[which, e] = jnp.concatenate(
                [value[e : e + 1] for value in values], axis=0
            ).astype(BF)

    def from_pairs(ref):
        for j in range(devices):
            row_sums[images * j : images * (j + 1), :] = ref[j].astype(F32)
        return row_sums[...].astype(BF)

    def spread(ref, value):
        row_sums[...] = value
        for j in range(devices):
            ref[j] = row_sums[images * j : images * (j + 1), :].astype(BF)

    def collect(ref):
        for e in range(experts):
            total = ref[4 * e].astype(F32)
            for k in range(1, 4):
                total = total + ref[4 * e + k].astype(F32)
            for i in range(images):
                pair_out[i, e : e + 1, :] = total[i : i + 1]
        return [pair_out[i].astype(BF) for i in range(images)]

    to_pairs(0, [slots[i] for i in range(images)])
    swap_a[0]()
    combs = [comb[:, at].astype(BF) for at in spans]
    sends = []
    for i, at in enumerate(spans):
        c_arrived(i)
        sends.append(mm(combs[i], cots[at, :]))
    to_pairs(1, sends)
    swap_c[0]()
    load_up.wait()
    load_down.wait()
    swap_a[1]()
    rows_low[...] = from_pairs(recv_a)
    hidden = mm(rows_low[...], up[...])
    act, slope = gelu_parts(hidden)
    active[...] = act.astype(BF)
    spread(send_b, mm(active[...], down[...]))
    swap_b[0]()
    swap_c[1]()
    d_rows[...] = from_pairs(recv_c)
    d_active = nt(d_rows[...], down[...])
    d_hidden[...] = (d_active * slope).astype(BF)
    spread(send_d, nt(d_hidden[...], up[...]))
    swap_d[0]()
    turned_one[...] = n_one[...].T
    turned_att[...] = attended[...].T
    swap_b[1]()
    outs = collect(recv_b)
    b_start, b_arrived, b_sent = image_steps(
        block_out, out_rows, bsend, brecv, b_local, images, True
    )
    for i, at in enumerate(spans):
        for k in range(groups):
            cols = slice(k * 256, (k + 1) * 256)
            moe = tn(combs[i], outs[i][:, cols])
            out_rows[at, cols] = (middle[at, cols] + moe).astype(BF)
        dcomb[:, at] = nt(outs[i], cots[at, :])
        b_start(i)
    swap_d[1]()
    d_slots = collect(recv_d)

    router_grad = jnp.zeros((experts, width), F32)
    for i, at in enumerate(spans):
        wide_slots = d_slots[i].astype(F32)
        inner = jnp.sum(slots[i] * wide_slots, axis=-1, keepdims=True)
        projected = nt(d_slots[i], n_two[at, :])
        weight, change = comb[:, at], dcomb[:, at]
        d_logits = (projected - inner) / denominators[i] * disp[:, at]
        d_logits = d_logits + weight * (
            change - jnp.sum(weight * change, axis=0, keepdims=True)
        )
        router_grad = router_grad + mm(d_logits.astype(BF), n_two[at, :])
        scaled = wide_slots / denominators[i]
        high = scaled.astype(BF).astype(F32)
        left = jnp.concatenate(
            [disp[:, at], disp[:, at], d_logits, jnp.zeros_like(d_logits)], axis=0
        ).astype(BF)
        right = jnp.concatenate(
            [high, scaled - high, small[0:8, :], jnp.zeros_like(scaled)], axis=0
        ).astype(BF)
        for k in range(groups):
            cols = slice(k * 256, (k + 1) * 256)
            d_norm[at, cols] = tn(left, right[:, cols])

    nothing = jnp.zeros((8, width), F32)

    def back_two(k, carry):
        at = ds(k * ROWS, ROWS)
        grad = d_norm[at, :]
        unit, inverse = unit_rows(middle[at, :])
        change = norm_rows_back(grad, unit, inverse, gains[2])
        d_diff[at, :] = change
        d_branch[at, :] = (change + cots[at, :].astype(F32)).astype(BF)
        return carry[0] + fold_rows(grad * unit), carry[1] + fold_rows(grad)

    gain_two, shift_two = lax.fori_loop(0, count // ROWS, back_two, (nothing, nothing))

    sems = (send1, recv1, send2, recv2, send3, recv3)
    chunks = [
        reduce_steps(
            grads, pairs_buf, inter, out_stage, in_stage, sems, c, lo, hi, narrow
        )
        for c, (lo, hi, narrow) in enumerate(chunk_table(width))
    ]
    c_out, c_pos = chunks[groups], chunks[:groups]

    def grad_out(k, carry):
        cols = ds(k * 256, 256)
        to = ds(base_out + k * 256, 256, 128)
        grads[:, to] = mm(turned_att[...], d_branch[:, cols]).astype(BF)
        return carry

    lax.fori_loop(0, groups, grad_out, 0)
    c_out[0]()

    def back_out(k, carry):
        at = ds(k * 256, 256)
        d_attended[:, at] = nt(d_branch[...], full[at, base_out : base_out + width]).astype(BF)
        return carry

    lax.fori_loop(0, groups, back_out, 0)

    def attend_back(t, carry):
        i, p, at, base = heads(t)
        q = qkv[at, ds(base, 128)] * scale
        keys = split_heads(qkv[at, ds(base + 256, 128)])
        values = split_heads(qkv[at, ds(base + 512, 128)])
        grad = d_attended[at, ds(p * 128, 128)]
        d_values = join_heads(tn(probs[t], grad))
        d_probs = nt(grad, values)
        cuts = []
        for h in range(2):
            cut = slice(h * length, (h + 1) * length)
            weight = probs[t, :, cut].astype(F32)
            change = weight * d_probs[:, cut]
            total = jnp.sum(change, axis=-1, keepdims=True)
            cuts.append((change - weight * total).astype(BF))
        d_scores = jnp.concatenate(cuts, axis=1)
        d_qkv[at, ds(base, 128)] = (mm(d_scores, keys) * HD ** (-0.5)).astype(BF)
        d_qkv[at, ds(base + 256, 128)] = join_heads(tn(d_scores, q)).astype(BF)
        d_qkv[at, ds(base + 512, 128)] = d_values.astype(BF)
        return carry

    def group_grads(g):
        def one(k, carry):
            at = ds(g * 768 + k * 256, 256)
            to = ds(base_qkv + g * 768 + k * 256, 256, 128)
            grads[:, to] = mm(turned_one[...], d_qkv[:, at]).astype(BF)
            return carry

        lax.fori_loop(0, 3, one, 0)

    def input_grads(i, carry):
        at = spans[i]

        def back_qkv(k, carry):
            cols = ds(k * 256, 256)
            d_norm[at, cols] = nt(d_qkv[at, :], full[cols, base_qkv : base_qkv + 3 * width])
            return carry

        def back_one(k, carry):
            at = ds(k * ROWS, ROWS)
            grad = d_norm[at, :]
            unit, inverse = unit_rows(xs[at, :].astype(F32))
            change = norm_rows_back(grad, unit, inverse, gains[0])
            g_rows[at, :] = (change + d_diff[at, :]).astype(BF)
            return carry[0] + fold_rows(grad * unit), carry[1] + fold_rows(grad)

        lax.fori_loop(0, groups, back_qkv, 0)
        carry = lax.fori_loop(i * per_image, (i + 1) * per_image, back_one, carry)
        g_start(i)
        return carry

    g_start, g_arrived, g_sent = image_steps(
        g_blocks, g_rows, gsend, grecv, g_local, images, True
    )
    sums_one = (nothing, nothing)
    for i in range(images - 1):
        lax.fori_loop(i * pairs, (i + 1) * pairs, attend_back, 0)
        if i == 0:
            c_out[1]()
        sums_one = input_grads(i, sums_one)
    begin = (images - 1) * pairs
    lax.fori_loop(begin, begin + 2, attend_back, 0)
    c_out[2]()
    group_grads(2)
    c_pos[2][0]()
    lax.fori_loop(begin + 2, begin + 4, attend_back, 0)
    c_out[3]()
    c_pos[2][1]()
    group_grads(1)
    c_pos[1][0]()
    lax.fori_loop(begin + 4, begin + 6, attend_back, 0)
    c_pos[2][2]()
    c_pos[1][1]()
    gain_one, shift_one = input_grads(images - 1, sums_one)
    sums = [
        jnp.sum(value, axis=0, keepdims=True)
        for value in (gain_one, shift_one, gain_two, shift_two)
    ]
    tall = jnp.concatenate(
        [router_grad] + sums + [jnp.zeros((128 - experts - 4, width), F32)], axis=0
    )
    grads[:, 0:SMALL] = tall.T.astype(BF)
    group_grads(0)
    c_pos[0][0]()
    c_pos[1][2]()
    c_pos[2][3]()
    c_pos[0][1]()
    c_pos[1][3]()
    c_pos[0][2]()
    c_pos[0][3]()
    for i in range(images):
        b_arrived(i)
    c_out[4]()
    c_pos[2][4]()
    c_pos[1][4]()
    for i in range(images):
        g_arrived(i)
    c_pos[0][4]()
    for done in (gather.sent, t_sent, c_sent, b_sent, g_sent):
        done()
    for swap in (swap_a, swap_b, swap_c, swap_d):
        swap[2]()
    for chunk in chunks:
        chunk[5]()


def chunk_table(width):
    groups = width // 256
    table = [(0, SMALL + 768, slice(0, 512))]
    for g in range(1, groups):
        table.append((SMALL + g * 768, SMALL + (g + 1) * 768, slice(128 + g * 384, 512 + g * 384)))
    end = 128 + groups * 384
    table.append((SMALL + 3 * width, SMALL + 4 * width, slice(end, end + width // 2)))
    return table


def finish_kernel(
    out_in, diff, cotangent, parts, rows_low, active, d_rows, d_hidden,
    block_out, grad_input, grad_qkv, grad_out_w, grad_small, grad_up, grad_down,
):
    block_out[...] = out_in[...]
    grad_input[...] = diff[...].astype(F32) + cotangent[...].astype(F32)
    grad_up[0] = tn(rows_low[...], d_hidden[...])
    grad_down[0] = tn(active[...], d_rows[...])

    @pl.when(pl.program_id(0) == 0)
    def _():
        width = grad_out_w.shape[1]
        quarter = grad_out_w.shape[0]
        total = parts[0].astype(F32)
        for k in range(1, 4):
            total = total + parts[k].astype(F32)
        for c, (lo, hi, narrow) in enumerate(chunk_table(width)):
            both = jnp.concatenate([total[:quarter, narrow], total[quarter:, narrow]], axis=1)
            if c == width // 256:
                grad_out_w[...] = both
                continue
            if c == 0:
                square = jnp.concatenate(
                    [both[:, :SMALL], jnp.zeros((128 - quarter, SMALL), F32)], axis=0
                )
                grad_small[...] = square.T[:16]
                both = both[:, SMALL:]
            for k in range(3):
                grad_qkv[:, k * width + c * 256 : k * width + (c + 1) * 256] = both[
                    :, k * 256 : (k + 1) * 256
                ]


def kernel_plan(
    tokens, lengths, w_qkv, w_out, router, gain_one, shift_one, gain_two, shift_two,
    w_up, w_down, cotangent,
):
    own_rows, width = w_out.shape
    blocks, size = tokens.shape[:2]
    images, length, experts = blocks // 4, 4 * size, router.shape[1]
    count = images * length
    groups = width // 256
    pairs = 2 * groups
    devices = 4 * experts
    columns = 4 * width + SMALL
    fan = w_up.shape[2]
    quarter = 4 * own_rows
    pair = (images, width)
    rows = devices * images

    def shape(*dims, kind=F32):
        return jax.ShapeDtypeStruct(dims, kind)

    dma = pltpu.SemaphoreType.DMA
    vmem, anywhere = pl.BlockSpec(memory_space=VM), pl.BlockSpec(memory_space=pl.ANY)
    stage_wide = 512 + (groups - 1) * 384 + width // 2
    outs = (
        shape(*tokens.shape, kind=BF),
        shape(*tokens.shape, kind=BF),
        shape(4, 2 * own_rows, stage_wide, kind=BF),
        shape(rows, width, kind=BF),
        shape(rows, fan, kind=BF),
        shape(rows, width, kind=BF),
        shape(rows, fan, kind=BF),
    )
    scratch = [
        VM((devices, 2 * own_rows, columns // 2 + 64), BF),
        VM((width, columns + 128), BF),
        VM((128, 128), F32),
        VM((16, width), F32),
        VM((count, width), BF),
        VM((count, width), BF),
        VM((count, 3 * width), BF),
        VM((images * pairs, length, 2 * length), BF),
        VM((count, width), BF),
        VM((count, width), F32),
        VM((count, width), BF),
        VM((count, width), BF),
        VM((experts, count), F32),
        VM((experts, count), F32),
        VM((experts, count), F32),
        VM((images, experts, width), F32),
        VM((images, 1, length), F32),
        VM((width, fan), BF),
        VM((fan, width), BF),
        VM((count, width), BF),
        VM((2, experts) + pair, BF),
        VM((images, experts, width), F32),
        VM((rows, width), F32),
    ]
    scratch += [VM((devices,) + pair, BF)] * 6
    scratch += [
        VM((width, count), BF),
        VM((width, count), BF),
        VM((count, width), F32),
        VM((count, width), F32),
        VM((count, width), BF),
        VM((count, width), BF),
        VM((count, 3 * width), BF),
        VM((count, width), BF),
        VM((width, columns), BF),
        VM((4, quarter, columns), BF),
        VM((6, quarter // 2, columns), BF),
        VM((4, 2 * own_rows, stage_wide), BF),
    ]
    scratch += [dma((4,))] * 7 + [dma((16,))] * 2 + [dma((4,))] * 2
    scratch += [dma((3 * images,))] * 8
    scratch += [dma((images,))] * 4
    scratch += [dma((2,)), dma((4,)), dma((4,))]
    chunks = groups + 1
    scratch += [dma((4 * chunks,))] * 2 + [dma((6 * chunks,))] * 2 + [dma((4 * chunks,))] * 2
    vectors = [vec[None, :] for vec in (gain_one, shift_one, gain_two, shift_two)]
    out_in, diff, parts, rows_low, active, d_rows, d_hidden = pl.pallas_call(
        block_kernel,
        out_shape=outs,
        in_specs=[pl.BlockSpec(memory_space=pltpu.SMEM)] + [vmem] * 7 + [anywhere] * 4,
        out_specs=[anywhere] * 3 + [vmem] * 4,
        scratch_shapes=scratch,
        compiler_params=pltpu.CompilerParams(
            collective_id=0, has_side_effects=True, vmem_limit_bytes=63 * 2**20
        ),
        name="block",
    )(lengths, w_qkv, w_out, router.T, *vectors, tokens, cotangent, w_up, w_down)

    def by_columns(*dims):
        return pl.BlockSpec(dims + (256,), lambda k: (0,) * len(dims) + (k,))

    def whole(*dims):
        return pl.BlockSpec(dims, lambda k: (0,) * len(dims))

    block_out, grad_input, grad_qkv, grad_out_w, grad_small, grad_up, grad_down = pl.pallas_call(
        finish_kernel,
        grid=(groups,),
        out_shape=(
            shape(*tokens.shape, kind=BF),
            shape(*tokens.shape),
            shape(own_rows, 3 * width),
            shape(own_rows, width),
            shape(16, 128),
            shape(*w_up.shape),
            shape(*w_down.shape),
        ),
        in_specs=[
            by_columns(blocks, size),
            by_columns(blocks, size),
            by_columns(blocks, size),
            whole(4, 2 * own_rows, stage_wide),
            whole(rows, width),
            whole(rows, fan),
            by_columns(rows),
            by_columns(rows),
        ],
        out_specs=[
            by_columns(blocks, size),
            by_columns(blocks, size),
            whole(own_rows, 3 * width),
            whole(own_rows, width),
            whole(16, 128),
            by_columns(1, width),
            by_columns(1, fan),
        ],
        compiler_params=pltpu.CompilerParams(vmem_limit_bytes=63 * 2**20),
        name="finish",
    )(out_in, diff, cotangent, parts, rows_low, active, d_rows, d_hidden)
    return (
        block_out,
        grad_input,
        grad_qkv,
        grad_out_w,
        grad_small[:experts, :own_rows].T,
        grad_small[experts, :own_rows],
        grad_small[experts + 1, :own_rows],
        grad_small[experts + 2, :own_rows],
        grad_small[experts + 3, :own_rows],
        grad_up,
        grad_down,
    )


def solution(mesh):
    plan = kernel_plan if dict(mesh.shape) == {"dp": 8, "seq": 4} else plain_plan
    rows, vector = P(("dp", "seq"), None), P(("dp", "seq"))
    tokens = P("dp", "seq", None)
    up, down = P("dp", None, "seq"), P("dp", "seq", None)
    return jax.shard_map(
        plan,
        mesh=mesh,
        in_specs=(tokens, P("dp"), rows, rows, rows)
        + (vector,) * 4
        + (up, down, tokens),
        out_specs=(tokens, tokens, rows, rows, rows) + (vector,) * 4 + (up, down),
        check_vma=False,
    )
```

```python
import jax
import jax.numpy as jnp
from jax import lax
from jax.experimental import pallas as pl
from jax.experimental.pallas import tpu as pltpu
from jax.sharding import PartitionSpec as P

H = 12
HD = 64
BF = jnp.bfloat16
F32 = jnp.float32


def dot(spec, a, b):
    return jnp.einsum(spec, a, b, preferred_element_type=F32)


def unit_norm(values):
    centred = values - jnp.mean(values, axis=-1, keepdims=True)
    inverse = lax.rsqrt(jnp.mean(centred * centred, axis=-1, keepdims=True) + 1e-06)
    return centred * inverse, inverse


def norm_back(grad_rows, unit_rows, inverse, gain):
    scaled = grad_rows * gain
    centred = scaled - jnp.mean(scaled, axis=-1, keepdims=True)
    correction = unit_rows * jnp.mean(scaled * unit_rows, axis=-1, keepdims=True)
    return (
        inverse * (centred - correction),
        jnp.sum(grad_rows * unit_rows, axis=(0, 1)),
        jnp.sum(grad_rows, axis=(0, 1)),
    )


def gelu_tanh(values):
    return jax.nn.gelu(values, approximate=True)


def to_images(array):
    return lax.all_to_all(array, "seq", split_axis=0, concat_axis=1, tiled=True)


def to_blocks(array):
    return lax.all_to_all(array, "seq", split_axis=1, concat_axis=0, tiled=True)


def to_experts(rows):
    rows = lax.all_to_all(rows, "dp", split_axis=1, concat_axis=0, tiled=True)
    return lax.all_gather(rows, "seq", axis=0, tiled=True)


def from_experts(rows):
    rows = lax.psum_scatter(rows, "seq", scatter_dimension=0, tiled=True).astype(BF)
    return lax.all_to_all(rows, "dp", split_axis=0, concat_axis=1, tiled=True)


def plain_plan(
    tokens, lengths, w_qkv, w_out, router, gain_one, shift_one, gain_two, shift_two,
    w_up, w_down, cotangent,
):
    groups = lax.axis_size("seq")
    model_width, slots_all = w_qkv.shape[1] // 3, router.shape[1]
    packed = jnp.concatenate(
        [w_qkv, w_out, router]
        + [vec[:, None] for vec in (gain_one, shift_one, gain_two, shift_two)],
        axis=1,
    )
    packed = lax.all_gather(packed, ("dp", "seq"), axis=0, tiled=True)
    split = 4 * model_width
    w_qkv, w_out = packed[:, : 3 * model_width], packed[:, 3 * model_width : split]
    router = packed[:, split : split + slots_all]
    gain_one, shift_one, gain_two, shift_two = (
        packed[:, split + slots_all + k].astype(F32) for k in range(4)
    )
    x = to_images(tokens).astype(F32)
    cot = to_images(cotangent)
    images, length_all = x.shape[:2]
    lengths_own = lax.dynamic_slice_in_dim(lengths, lax.axis_index("seq") * images, images)
    valid = jnp.arange(length_all, dtype=jnp.int32)[None, :] < lengths_own[:, None]

    unit_one, inverse_one = unit_norm(x)
    normed_one = (unit_one * gain_one + shift_one).astype(BF)
    qkv = dot("btd,de->bte", normed_one, w_qkv).astype(BF).reshape(images, length_all, 3, H, HD)
    queries, keys_all, values_all = qkv[:, :, 0], qkv[:, :, 1], qkv[:, :, 2]
    scores = dot("bqhd,bkhd->bhqk", queries, keys_all) * HD ** (-0.5)
    probs = jax.nn.softmax(jnp.where(valid[:, None, None, :], scores, -1000000000.0), axis=-1)
    probs_low = probs.astype(BF)
    attended = dot("bhqk,bkhd->bqhd", probs_low, values_all).astype(BF)
    attended = attended.reshape(images, length_all, model_width)
    middle = x + dot("btd,de->bte", attended, w_out)
    unit_two, inverse_two = unit_norm(middle)
    normed_two = (unit_two * gain_two + shift_two).astype(BF)
    logits = dot("btd,de->bte", normed_two, router)
    top = jnp.floor(jnp.max(jnp.where(valid[:, :, None], logits, -1000000000.0), axis=1))
    dispatch = jnp.where(valid[:, :, None], jnp.exp(logits - top[:, None, :]), 0.0)
    dispatch_low = dispatch.astype(BF)
    denominator = jnp.sum(dispatch, axis=1)
    slot_vals = dot("bte,btd->bed", dispatch_low, normed_two) / denominator[:, :, None]
    slot_rows = to_experts(slot_vals.astype(BF))
    hidden = dot("red,edf->ref", slot_rows, w_up)
    active = gelu_tanh(hidden).astype(BF)
    expert_out = from_experts(dot("ref,efd->red", active, w_down))
    combine = jax.nn.softmax(logits, axis=-1)
    combine_low = combine.astype(BF)
    block_out = (middle + dot("bte,bed->btd", combine_low, expert_out)).astype(BF)

    d_combine = dot("btd,bed->bte", cot, expert_out)
    d_expert = dot("bte,btd->bed", combine_low, cot).astype(BF)
    d_rows = to_experts(d_expert)
    d_active = dot("red,efd->ref", d_rows, w_down)
    grad_down = dot("ref,red->efd", active, d_rows)
    d_hidden = jax.vjp(gelu_tanh, hidden)[1](d_active)[0].astype(BF)
    grad_up = dot("red,ref->edf", slot_rows, d_hidden)
    d_slots = from_experts(dot("ref,edf->red", d_hidden, w_up))
    d_slots_wide = d_slots.astype(F32)
    inner = jnp.sum(slot_vals * d_slots_wide, axis=-1)
    projected = dot("btd,bed->bte", normed_two, d_slots)
    d_logits = (projected - inner[:, None, :]) / denominator[:, None, :] * dispatch
    d_logits = d_logits + combine * (
        d_combine - jnp.sum(combine * d_combine, axis=-1, keepdims=True)
    )
    d_logits = d_logits.astype(BF)
    scaled = d_slots_wide / denominator[:, :, None]
    scaled_high = scaled.astype(BF)
    scaled_rest = (scaled - scaled_high.astype(F32)).astype(BF)
    d_normed_two = (
        dot("bte,bed->btd", dispatch_low, scaled_high)
        + dot("bte,bed->btd", dispatch_low, scaled_rest)
        + dot("bte,de->btd", d_logits, router)
    )
    grad_router = dot("btd,bte->de", normed_two, d_logits)
    d_norm, grad_gain_two, grad_shift_two = norm_back(d_normed_two, unit_two, inverse_two, gain_two)
    d_middle = cot.astype(F32) + d_norm
    d_branch = d_middle.astype(BF)
    grad_out_w = dot("btd,bte->de", attended, d_branch)
    d_attended = dot("bte,de->btd", d_branch, w_out).astype(BF)
    d_attended = d_attended.reshape(images, length_all, H, HD)
    d_values = dot("bhqk,bqhd->bkhd", probs_low, d_attended)
    d_probs = dot("bqhd,bkhd->bhqk", d_attended, values_all)
    d_scores = probs * (d_probs - jnp.sum(probs * d_probs, axis=-1, keepdims=True))
    d_scores = d_scores.astype(BF)
    d_queries = dot("bhqk,bkhd->bqhd", d_scores, keys_all) * HD ** (-0.5)
    d_keys = dot("bhqk,bqhd->bkhd", d_scores, queries) * HD ** (-0.5)
    d_qkv = jnp.stack([d_queries, d_keys, d_values], axis=2).astype(BF)
    d_qkv = d_qkv.reshape(images, length_all, 3 * model_width)
    grad_qkv = dot("btd,bte->de", normed_one, d_qkv)
    d_normed_one = dot("bte,de->btd", d_qkv, w_qkv)
    d_norm, grad_gain_one, grad_shift_one = norm_back(d_normed_one, unit_one, inverse_one, gain_one)
    grad_input = to_blocks(d_middle + d_norm)

    vectors = (grad_gain_one, grad_shift_one, grad_gain_two, grad_shift_two)
    packed = jnp.concatenate(
        [grad_qkv, grad_out_w, grad_router] + [vec[:, None] for vec in vectors], axis=1
    )
    packed = lax.psum_scatter(packed, ("dp", "seq"), scatter_dimension=0, tiled=True)
    return (
        to_blocks(block_out),
        grad_input,
        packed[:, : 3 * model_width],
        packed[:, 3 * model_width : split],
        packed[:, split : split + slots_all],
        packed[:, split + slots_all],
        packed[:, split + slots_all + 1],
        packed[:, split + slots_all + 2],
        packed[:, split + slots_all + 3],
        grad_up,
        grad_down,
    )


MESH = pl.DeviceIdType.MESH
VM = pltpu.VMEM
SMALL = 128
ROWS = 64


def nt(a, b):
    return lax.dot_general(a, b, (((1,), (1,)), ((), ())), preferred_element_type=F32)


def tn(a, b):
    return lax.dot_general(a, b, (((0,), (0,)), ((), ())), preferred_element_type=F32)


def mm(a, b):
    return jnp.dot(a, b, preferred_element_type=F32)


def ds(start, size, unit=None):
    return pl.ds(pl.multiple_of(start, unit or size), size)


def remote(src, dst, send, recv, device):
    return pltpu.make_async_remote_copy(
        src_ref=src, dst_ref=dst, send_sem=send, recv_sem=recv, device_id=device,
        device_id_type=MESH,
    )


def other(d, kind):
    core, x, y = lax.rem(d, 2), lax.rem(d // 2, 2), d // 4
    return {"x": d + 2 - 4 * x, "y": d + 4 - 8 * y, "core": d + 1 - 2 * core}[kind]


class Gather:
    def __init__(self, shards, full, zup, zdown, zrecv, xsend, xrecv, ysend, yrecv, csend, crecv, dsend, drecv):
        d, z = lax.axis_index("dp"), lax.axis_index("seq")
        dx, dy, dc = other(d, "x"), other(d, "y"), other(d, "core")
        self.shards, self.full, self.z = shards, full, z
        self.owners = (d, dx, dy, other(dx, "y"))
        self.over = {"x": (dx, z), "y": (dy, z), "core": (dc, z)}
        self.up, self.down = (d, lax.rem(z + 1, 4)), (d, lax.rem(z + 3, 4))
        self.sems = {
            "up": (zup, zrecv), "down": (zdown, zrecv), "x": (xsend, xrecv),
            "y": (ysend, yrecv), "core": (csend, crecv), "d": (dsend, drecv),
        }

    def copy(self, kind, owner, s, device, sem):
        ref = self.shards.at[owner * 4 + s]
        send, recv = self.sems[kind]
        return remote(ref, ref, send.at[sem], recv.at[sem], device)

    def pass_on(self, s, upward, downward):
        d, z = self.owners[0], self.z
        if upward:

            @pl.when(z < 3)
            def _():
                self.copy("up", d, s, self.up, s).start()

        if downward:

            @pl.when(z > 0)
            def _():
                self.copy("down", d, s, self.down, s).start()

        self.copy("x", d, s, self.over["x"], s).start()
        self.copy("y", d, s, self.over["y"], s).start()
        self.copy("core", d, s, self.over["core"], s).start()

    def each(self, h, act):
        if h == 0:
            act(self.z)
            return

        @pl.when(self.z >= h)
        def _():
            act(self.z - h)

        @pl.when(self.z + h <= 3)
        def _():
            act(self.z + h)

    def line(self, h):
        d, z = self.owners[0], self.z
        if h == 0:
            self.pass_on(z, True, True)
            return

        @pl.when(z >= h)
        def _():
            self.copy("up", d, z - h, self.up, z - h).wait_recv()
            self.pass_on(z - h, True, False)

        @pl.when(z + h <= 3)
        def _():
            self.copy("down", d, z + h, self.down, z + h).wait_recv()
            self.pass_on(z + h, False, True)

    def plane(self, h):
        d, dx, dy, dd = self.owners

        def act(s):
            self.copy("x", dx, s, self.over["x"], s).wait_recv()

            @pl.when(lax.rem(s, 2) == 0)
            def _():
                self.copy("d", dx, s, self.over["y"], s).start()

            self.copy("core", dx, s, self.over["core"], 4 + s).start()
            self.copy("y", dy, s, self.over["y"], s).wait_recv()

            @pl.when(lax.rem(s, 2) == 1)
            def _():
                self.copy("d", dy, s, self.over["x"], s).start()

            self.copy("core", dy, s, self.over["core"], 8 + s).start()

        self.each(h, act)

    def diagonal(self, h):
        def act(s):
            self.copy("d", self.owners[3], s, self.over["x"], s).wait_recv()
            self.copy("core", self.owners[3], s, self.over["core"], 12 + s).start()

        self.each(h, act)

    def twin(self, k):
        dc = other(self.owners[k], "core")
        for s in range(4):
            self.copy("core", dc, s, self.over["core"], 4 * k + s).wait_recv()
        self.assemble(dc)

    def assemble(self, owner):
        half, wide = self.shards.shape[1:]
        quarter = half // 2
        for side in range(2):
            value = jnp.concatenate(
                [
                    self.shards[owner * 4 + k].astype(F32)[side * quarter : (side + 1) * quarter]
                    for k in range(4)
                ],
                axis=0,
            )
            self.full[ds(owner * 2 * half, 2 * half), side * wide : (side + 1) * wide] = (
                value.astype(BF)
            )

    def sent(self):
        d, z = self.owners[0], self.z

        def one(s, carry):
            @pl.when((s <= z) & (z < 3))
            def _():
                self.copy("up", d, s, self.up, s).wait_send()

            @pl.when((s >= z) & (z > 0))
            def _():
                self.copy("down", d, s, self.down, s).wait_send()

            self.copy("x", d, s, self.over["x"], s).wait_send()
            self.copy("y", d, s, self.over["y"], s).wait_send()
            self.copy("d", d, s, self.over["x"], s).wait_send()
            for k in range(4):
                self.copy("core", self.owners[k], s, self.over["core"], 4 * k + s).wait_send()
            return carry

        lax.fori_loop(0, 4, one, 0)


def image_steps(blocks, whole, send, recv, local_sem, images, home):
    d, z = lax.axis_index("dp"), lax.axis_index("seq")
    size = blocks.shape[1]
    length = 4 * size

    def make(i, k):
        there = lax.rem(z + k, 4)
        if home:
            src = whole.at[ds(i * length + there * size, size)]
            dst = blocks.at[z * images + i]
        else:
            src = blocks.at[there * images + i]
            dst = whole.at[ds(i * length + z * size, size)]
        if k == 0:
            return pltpu.make_async_copy(src, dst, local_sem.at[i])
        return remote(src, dst, send.at[i * 3 + k - 1], recv.at[i * 3 + k - 1], (d, there))

    table = [[make(i, k) for k in range(4)] for i in range(images)]

    def start(i):
        for one in table[i]:
            one.start()

    def arrived(i):
        table[i][0].wait()
        for one in table[i][1:]:
            one.wait_recv()

    def sent():
        for i in range(images):
            for one in table[i][1:]:
                one.wait_send()

    return start, arrived, sent


def swap_steps(src, dst, send, recv, to_expert):
    d, z = lax.axis_index("dp"), lax.axis_index("seq")
    count = dst.shape[0]
    me = d * 4 + z

    def start():
        def one(k, carry):
            j = lax.rem(me + k, count)
            e = j // 4
            row = src.at[e] if to_expert else src.at[j]
            remote(row, dst.at[me], send, recv, (e, lax.rem(j, 4))).start()
            return carry

        lax.fori_loop(1, count, one, 0)
        pltpu.make_async_copy(src.at[d] if to_expert else src.at[me], dst.at[me], recv).start()

    def arrived():
        pltpu.make_async_copy(dst, dst, recv).wait()

    def sent():
        part = dst.at[pl.ds(0, count - 1)]
        remote(part, part, send, recv, (other(d, "x"), z)).wait_send()

    return start, arrived, sent


def reduce_steps(grads, pairs, inter, out_stage, in_stage, sems, chunk, lo, hi, narrow):
    d, z = lax.axis_index("dp"), lax.axis_index("seq")
    dx, dy, dc = other(d, "x"), other(d, "y"), other(d, "core")
    core = lax.rem(d, 2)
    over_x, over_y, over_c = (dx, z), (dy, z), (dc, z)
    rows = pairs.shape[1]
    half, quarter = rows // 2, rows // 4
    cols = slice(lo, hi)
    send1, recv1, send2, recv2, send3, recv3 = sems
    chips = pairs.shape[0]

    step1 = []
    for m in range(chips):
        block = grads.at[ds((2 * m + 1 - core) * rows, rows), cols]
        n = chunk * chips + m
        step1.append(remote(block, pairs.at[m, :, cols], send1.at[n], recv1.at[n], over_c))
    here, mx, my, md = d // 2, dx // 2, dy // 2, other(dx, "y") // 2

    def part(m, h):
        return pairs.at[m, h * half : (h + 1) * half, cols]

    def hop(k, m, h, device):
        n = chunk * 6 + k
        return remote(part(m, h), inter.at[k, :, cols], send2.at[n], recv2.at[n], device)

    step2 = [
        hop(0, md, 0, over_y), hop(1, md, 1, over_x), hop(2, my, 0, over_y),
        hop(3, mx, 1, over_x), hop(4, mx, 0, over_x), hop(5, my, 1, over_y),
    ]
    local_copy = pltpu.make_async_copy(
        out_stage.at[z, :, narrow], in_stage.at[3, :, narrow], recv3.at[chunk * 4 + 3]
    )
    step3 = []
    for k in range(1, 4):
        n = chunk * 4 + k - 1
        there = lax.rem(z + k, 4)
        step3.append(
            remote(
                out_stage.at[there, :, narrow], in_stage.at[k - 1, :, narrow],
                send3.at[n], recv3.at[n], (d, there),
            )
        )

    def one():
        for c in step1:
            c.start()

    def two():
        for m in range(chips):
            step1[m].wait_recv()
            own = grads[ds((2 * m + core) * rows, rows), cols].astype(F32)
            pairs[m, :, cols] = (own + pairs[m, :, cols].astype(F32)).astype(BF)
        for k in range(4):
            step2[k].start()

    def three():
        for k, m, h in ((0, mx, 0), (1, my, 1)):
            step2[k].wait_recv()
            at = slice(h * half, (h + 1) * half)
            total = pairs[m, at, cols].astype(F32) + inter[k, :, cols].astype(F32)
            pairs[m, at, cols] = total.astype(BF)
            step2[4 + k].start()

    def four():
        for k in (2, 3, 4, 5):
            step2[k].wait_recv()
        own = pairs[here, :, cols].astype(F32)
        top = own[:half] + inter[2, :, cols].astype(F32) + inter[4, :, cols].astype(F32)
        low = own[half:] + inter[3, :, cols].astype(F32) + inter[5, :, cols].astype(F32)
        total = jnp.concatenate([top, low], axis=0)
        middle = narrow.stop - narrow.start
        if 2 * middle > hi - lo:
            filler = jnp.zeros((rows, 2 * middle - (hi - lo)), F32)
            total = jnp.concatenate([total, filler], axis=1)
        for t in range(4):
            shard = total[t * quarter : (t + 1) * quarter]
            both = jnp.concatenate([shard[:, :middle], shard[:, middle:]], axis=0)
            out_stage[t, :, narrow] = both.astype(BF)
        for c in step3:
            c.start()
        local_copy.start()

    def five():
        for c in step3:
            c.wait_recv()
        local_copy.wait()

    def sent():
        for c in step1 + step2 + step3:
            c.wait_send()

    return one, two, three, four, five, sent


def unit_rows(x):
    centred = x - jnp.mean(x, axis=-1, keepdims=True)
    inverse = lax.rsqrt(jnp.mean(centred * centred, axis=-1, keepdims=True) + 1e-06)
    return centred * inverse, inverse


def fold_rows(x):
    total = x[:8]
    for k in range(1, x.shape[0] // 8):
        total = total + x[8 * k : 8 * (k + 1)]
    return total


def norm_rows_back(grad, unit, inverse, gain):
    scaled = grad * gain
    centred = scaled - jnp.mean(scaled, axis=-1, keepdims=True)
    correction = unit * jnp.mean(scaled * unit, axis=-1, keepdims=True)
    return inverse * (centred - correction)


def split_heads(pair):
    lane = lax.broadcasted_iota(jnp.int32, (1, 2 * HD), 1)
    left = jnp.where(lane < HD, 1.0, 0.0)
    return jnp.concatenate([pair * left.astype(BF), pair * (1.0 - left).astype(BF)], axis=0)


def join_heads(pair):
    lane = lax.broadcasted_iota(jnp.int32, (1, 2 * HD), 1)
    rows = pair.shape[0] // 2
    return jnp.where(lane < HD, pair[:rows], pair[rows:])


def gelu_parts(v):
    inner = jnp.tanh(0.7978845608 * (v + 0.044715 * v * v * v))
    slope = 0.5 * (1.0 + inner) + 0.5 * v * (1.0 - inner * inner) * 0.7978845608 * (
        1.0 + 3.0 * 0.044715 * v * v
    )
    return 0.5 * v * (1.0 + inner), slope


def block_kernel(
    lengths, w_qkv, w_out, router_own, gain_a, shift_a, gain_b, shift_b, tokens, cotangent,
    w_up, w_down,
    block_out, g_blocks, in_stage, rows_low, active, d_rows, d_hidden,
    shards, full, corner, small, xs, cots, qkv, probs, attended, middle, n_one, n_two,
    disp, comb, dcomb, slots, bias, up, down, out_rows, pair_in, pair_out, row_sums,
    recv_a, recv_b, recv_c, recv_d, send_b, send_d, turned_one, turned_att,
    d_norm, d_diff, d_branch, d_attended, d_qkv, g_rows,
    grads, pairs_buf, inter, out_stage,
    zup, zdown, zrecv, xsend, xrecv, ysend, yrecv, wsend, wrecv, dsend, drecv, tsend, trecv, csend, crecv, bsend, brecv, gsend, grecv,
    t_local, c_local, b_local, g_local, loads, swap_send, swap_recv,
    send1, recv1, send2, recv2, send3, recv3,
):
    d, z = lax.axis_index("dp"), lax.axis_index("seq")
    width = tokens.shape[2]
    images = tokens.shape[0] // 4
    length = 4 * tokens.shape[1]
    count = images * length
    groups = width // 256
    experts = disp.shape[0]
    devices = recv_a.shape[0]
    base_qkv, base_out = SMALL, SMALL + 3 * width

    barrier = pltpu.get_barrier_semaphore()
    partners = [(d, lax.rem(z + k, 4)) for k in range(1, 4)]
    partners += [(other(d, kind), z) for kind in ("x", "y", "core")]
    for partner in partners:
        pl.semaphore_signal(barrier, inc=1, device_id=partner, device_id_type=MESH)
    load_up = pltpu.make_async_copy(w_up.at[0], up, loads.at[0])
    load_down = pltpu.make_async_copy(w_down.at[0], down, loads.at[1])
    load_up.start()
    load_down.start()
    own_rows = w_out.shape[0]
    corner[...] = jnp.zeros_like(corner)
    corner[0:experts, 0:own_rows] = router_own[...].astype(F32)
    for k, vector in enumerate((gain_a, shift_a, gain_b, shift_b)):
        corner[experts + k : experts + k + 1, 0:own_rows] = vector[...].astype(F32)
    own = w_qkv[...].astype(F32)
    pieces = [corner[...].T[:own_rows]]
    for g in range(groups):
        for k in range(3):
            pieces.append(own[:, k * width + g * 256 : k * width + (g + 1) * 256])
    pieces += [w_out[...].astype(F32), jnp.zeros((own_rows, 128), F32)]
    line = jnp.concatenate(pieces, axis=1)
    wide = shards.shape[2]
    shards[d * 4 + z] = jnp.concatenate([line[:, :wide], line[:, wide:]], axis=0).astype(BF)
    pl.semaphore_wait(barrier, len(partners))

    gather = Gather(
        shards, full, zup, zdown, zrecv, xsend, xrecv, ysend, yrecv, wsend, wrecv, dsend, drecv
    )
    t_start, t_arrived, t_sent = image_steps(tokens, xs, tsend, trecv, t_local, images, False)
    c_start, c_arrived, c_sent = image_steps(cotangent, cots, csend, crecv, c_local, images, False)
    gather.line(0)
    gather.line(1)
    gather.plane(0)
    gather.line(2)
    for i in range(images):
        t_start(i)
    gather.plane(1)
    gather.diagonal(0)
    gather.line(3)
    gather.plane(2)
    gather.diagonal(1)
    gather.assemble(d)
    gather.plane(3)
    gather.diagonal(2)
    gather.twin(0)
    gather.diagonal(3)
    for k in range(1, 4):
        gather.assemble(gather.owners[k])
        gather.twin(k)
    small[...] = full[:, 0:128].astype(F32).T[:16]
    gains = [small[8 + k : 9 + k, :] for k in range(4)]

    def norm_one(k, carry):
        at = ds(k * ROWS, ROWS)
        unit, _ = unit_rows(xs[at, :].astype(F32))
        n_one[at, :] = (unit * gains[0] + gains[1]).astype(BF)
        return carry

    per_image = length // ROWS
    for i in range(images):
        t_arrived(i)
        if i == images - 1:
            for k in range(images):
                c_start(k)
        lax.fori_loop(i * per_image, (i + 1) * per_image, norm_one, 0)

    def project(k, carry):
        weight = full[:, ds(base_qkv + k * 256, 256, 128)]
        qkv[:, ds(k * 256, 256)] = mm(n_one[...], weight).astype(BF)
        return carry

    lax.fori_loop(0, 3 * groups, project, 0)

    key = lax.broadcasted_iota(jnp.int32, (1, length), 1)
    for i in range(images):
        bias[i] = jnp.where(key < lengths[z * images + i], 0.0, -1000000000.0)
    scale = jnp.asarray(HD ** (-0.5), BF)
    pairs = 2 * groups

    def heads(t):
        i, p = t // pairs, pairs - 1 - lax.rem(t, pairs)
        base = (p // 2) * 768 + lax.rem(p, 2) * 128
        return i, p, ds(i * length, length), base

    def attend(t, carry):
        i, p, at, base = heads(t)
        keys = split_heads(qkv[at, ds(base + 256, 128)])
        values = split_heads(qkv[at, ds(base + 512, 128)])
        scores = nt(qkv[at, ds(base, 128)] * scale, keys)
        for h in range(2):
            part = scores[:, h * length : (h + 1) * length] + bias[i]
            e = jnp.exp(part - jnp.max(part, axis=-1, keepdims=True))
            total = jnp.sum(e, axis=-1, keepdims=True)
            probs[t, :, h * length : (h + 1) * length] = (e * (1.0 / total)).astype(BF)
        attended[at, ds(p * 128, 128)] = mm(probs[t], values).astype(BF)
        return carry

    lax.fori_loop(0, images * pairs, attend, 0)

    def project_out(k, carry):
        at = ds(k * 256, 256)
        weight = full[:, ds(base_out + k * 256, 256, 128)]
        middle[:, at] = xs[:, at].astype(F32) + mm(attended[...], weight)
        return carry

    lax.fori_loop(0, groups, project_out, 0)

    def norm_two(k, carry):
        at = ds(k * ROWS, ROWS)
        unit, _ = unit_rows(middle[at, :])
        n_two[at, :] = (unit * gains[2] + gains[3]).astype(BF)
        return carry

    lax.fori_loop(0, count // ROWS, norm_two, 0)
    router = small[0:8, :].astype(BF)
    spans = [slice(i * length, (i + 1) * length) for i in range(images)]
    denominators = []
    for i, at in enumerate(spans):
        logits = nt(router, n_two[at, :])
        inside = key < lengths[z * images + i]
        top = jnp.floor(
            jnp.max(jnp.where(inside, logits, -1000000000.0), axis=-1, keepdims=True)
        )
        dispatch = jnp.where(inside, jnp.exp(logits - top), 0.0)
        e = jnp.exp(logits - jnp.max(logits, axis=0, keepdims=True))
        disp[:, at] = dispatch
        comb[:, at] = e / jnp.sum(e, axis=0, keepdims=True)
        denominators.append(jnp.sum(dispatch, axis=-1, keepdims=True))
        slots[i] = mm(dispatch.astype(BF), n_two[at, :]) / denominators[i]

    swap_a = swap_steps(pair_in.at[0], recv_a, swap_send.at[0], swap_recv.at[0], True)
    swap_b = swap_steps(send_b, recv_b, swap_send.at[1], swap_recv.at[1], False)
    swap_c = swap_steps(pair_in.at[1], recv_c, swap_send.at[2], swap_recv.at[2], True)
    swap_d = swap_steps(send_d, recv_d, swap_send.at[3], swap_recv.at[3], False)

    def to_pairs(which, values):
        for e in range(experts):
            pair_in[which, e] = jnp.concatenate(
                [value[e : e + 1] for value in values], axis=0
            ).astype(BF)

    def from_pairs(ref):
        for j in range(devices):
            row_sums[images * j : images * (j + 1), :] = ref[j].astype(F32)
        return row_sums[...].astype(BF)

    def spread(ref, value):
        row_sums[...] = value
        for j in range(devices):
            ref[j] = row_sums[images * j : images * (j + 1), :].astype(BF)

    def collect(ref):
        for e in range(experts):
            total = ref[4 * e].astype(F32)
            for k in range(1, 4):
                total = total + ref[4 * e + k].astype(F32)
            for i in range(images):
                pair_out[i, e : e + 1, :] = total[i : i + 1]
        return [pair_out[i].astype(BF) for i in range(images)]

    to_pairs(0, [slots[i] for i in range(images)])
    swap_a[0]()
    combs = [comb[:, at].astype(BF) for at in spans]
    sends = []
    for i, at in enumerate(spans):
        c_arrived(i)
        sends.append(mm(combs[i], cots[at, :]))
    to_pairs(1, sends)
    swap_c[0]()
    load_up.wait()
    load_down.wait()
    swap_a[1]()
    rows_low[...] = from_pairs(recv_a)
    hidden = mm(rows_low[...], up[...])
    act, slope = gelu_parts(hidden)
    active[...] = act.astype(BF)
    spread(send_b, mm(active[...], down[...]))
    swap_b[0]()
    swap_c[1]()
    d_rows[...] = from_pairs(recv_c)
    d_active = nt(d_rows[...], down[...])
    d_hidden[...] = (d_active * slope).astype(BF)
    spread(send_d, nt(d_hidden[...], up[...]))
    swap_d[0]()
    turned_one[...] = n_one[...].T
    turned_att[...] = attended[...].T
    swap_b[1]()
    outs = collect(recv_b)
    b_start, b_arrived, b_sent = image_steps(
        block_out, out_rows, bsend, brecv, b_local, images, True
    )
    for i, at in enumerate(spans):
        for k in range(groups):
            cols = slice(k * 256, (k + 1) * 256)
            moe = tn(combs[i], outs[i][:, cols])
            out_rows[at, cols] = (middle[at, cols] + moe).astype(BF)
        dcomb[:, at] = nt(outs[i], cots[at, :])
        b_start(i)
    swap_d[1]()
    d_slots = collect(recv_d)

    router_grad = jnp.zeros((experts, width), F32)
    for i, at in enumerate(spans):
        wide_slots = d_slots[i].astype(F32)
        inner = jnp.sum(slots[i] * wide_slots, axis=-1, keepdims=True)
        projected = nt(d_slots[i], n_two[at, :])
        weight, change = comb[:, at], dcomb[:, at]
        d_logits = (projected - inner) / denominators[i] * disp[:, at]
        d_logits = d_logits + weight * (
            change - jnp.sum(weight * change, axis=0, keepdims=True)
        )
        router_grad = router_grad + mm(d_logits.astype(BF), n_two[at, :])
        scaled = wide_slots / denominators[i]
        high = scaled.astype(BF).astype(F32)
        left = jnp.concatenate(
            [disp[:, at], disp[:, at], d_logits, jnp.zeros_like(d_logits)], axis=0
        ).astype(BF)
        right = jnp.concatenate(
            [high, scaled - high, small[0:8, :], jnp.zeros_like(scaled)], axis=0
        ).astype(BF)
        for k in range(groups):
            cols = slice(k * 256, (k + 1) * 256)
            d_norm[at, cols] = tn(left, right[:, cols])

    nothing = jnp.zeros((8, width), F32)

    def back_two(k, carry):
        at = ds(k * ROWS, ROWS)
        grad = d_norm[at, :]
        unit, inverse = unit_rows(middle[at, :])
        change = norm_rows_back(grad, unit, inverse, gains[2])
        d_diff[at, :] = change
        d_branch[at, :] = (change + cots[at, :].astype(F32)).astype(BF)
        return carry[0] + fold_rows(grad * unit), carry[1] + fold_rows(grad)

    gain_two, shift_two = lax.fori_loop(0, count // ROWS, back_two, (nothing, nothing))

    sems = (send1, recv1, send2, recv2, send3, recv3)
    chunks = [
        reduce_steps(
            grads, pairs_buf, inter, out_stage, in_stage, sems, c, lo, hi, narrow
        )
        for c, (lo, hi, narrow) in enumerate(chunk_table(width))
    ]
    c_out, c_pos = chunks[groups], chunks[:groups]

    def grad_out(k, carry):
        cols = ds(k * 256, 256)
        to = ds(base_out + k * 256, 256, 128)
        grads[:, to] = mm(turned_att[...], d_branch[:, cols]).astype(BF)
        return carry

    lax.fori_loop(0, groups, grad_out, 0)
    c_out[0]()

    def back_out(k, carry):
        at = ds(k * 256, 256)
        d_attended[:, at] = nt(d_branch[...], full[at, base_out : base_out + width]).astype(BF)
        return carry

    lax.fori_loop(0, groups, back_out, 0)

    def attend_back(t, carry):
        i, p, at, base = heads(t)
        q = qkv[at, ds(base, 128)] * scale
        keys = split_heads(qkv[at, ds(base + 256, 128)])
        values = split_heads(qkv[at, ds(base + 512, 128)])
        grad = d_attended[at, ds(p * 128, 128)]
        d_values = join_heads(tn(probs[t], grad))
        d_probs = nt(grad, values)
        cuts = []
        for h in range(2):
            cut = slice(h * length, (h + 1) * length)
            weight = probs[t, :, cut].astype(F32)
            change = weight * d_probs[:, cut]
            total = jnp.sum(change, axis=-1, keepdims=True)
            cuts.append((change - weight * total).astype(BF))
        d_scores = jnp.concatenate(cuts, axis=1)
        d_qkv[at, ds(base, 128)] = (mm(d_scores, keys) * HD ** (-0.5)).astype(BF)
        d_qkv[at, ds(base + 256, 128)] = join_heads(tn(d_scores, q)).astype(BF)
        d_qkv[at, ds(base + 512, 128)] = d_values.astype(BF)
        return carry

    def group_grads(g):
        def one(k, carry):
            at = ds(g * 768 + k * 256, 256)
            to = ds(base_qkv + g * 768 + k * 256, 256, 128)
            grads[:, to] = mm(turned_one[...], d_qkv[:, at]).astype(BF)
            return carry

        lax.fori_loop(0, 3, one, 0)

    def input_grads(i, carry):
        at = spans[i]

        def back_qkv(k, carry):
            cols = ds(k * 256, 256)
            d_norm[at, cols] = nt(d_qkv[at, :], full[cols, base_qkv : base_qkv + 3 * width])
            return carry

        def back_one(k, carry):
            at = ds(k * ROWS, ROWS)
            grad = d_norm[at, :]
            unit, inverse = unit_rows(xs[at, :].astype(F32))
            change = norm_rows_back(grad, unit, inverse, gains[0])
            g_rows[at, :] = (change + d_diff[at, :]).astype(BF)
            return carry[0] + fold_rows(grad * unit), carry[1] + fold_rows(grad)

        lax.fori_loop(0, groups, back_qkv, 0)
        carry = lax.fori_loop(i * per_image, (i + 1) * per_image, back_one, carry)
        g_start(i)
        return carry

    g_start, g_arrived, g_sent = image_steps(
        g_blocks, g_rows, gsend, grecv, g_local, images, True
    )
    sums_one = (nothing, nothing)
    for i in range(images - 1):
        lax.fori_loop(i * pairs, (i + 1) * pairs, attend_back, 0)
        if i == 0:
            c_out[1]()
        sums_one = input_grads(i, sums_one)
    begin = (images - 1) * pairs
    lax.fori_loop(begin, begin + 2, attend_back, 0)
    c_out[2]()
    group_grads(2)
    c_pos[2][0]()
    lax.fori_loop(begin + 2, begin + 4, attend_back, 0)
    c_out[3]()
    c_pos[2][1]()
    group_grads(1)
    c_pos[1][0]()
    lax.fori_loop(begin + 4, begin + 6, attend_back, 0)
    c_pos[2][2]()
    c_pos[1][1]()
    gain_one, shift_one = input_grads(images - 1, sums_one)
    sums = [
        jnp.sum(value, axis=0, keepdims=True)
        for value in (gain_one, shift_one, gain_two, shift_two)
    ]
    tall = jnp.concatenate(
        [router_grad] + sums + [jnp.zeros((128 - experts - 4, width), F32)], axis=0
    )
    grads[:, 0:SMALL] = tall.T.astype(BF)
    group_grads(0)
    c_pos[0][0]()
    c_pos[1][2]()
    c_pos[2][3]()
    c_pos[0][1]()
    c_pos[1][3]()
    c_pos[0][2]()
    c_pos[0][3]()
    for i in range(images):
        b_arrived(i)
    c_out[4]()
    c_pos[2][4]()
    c_pos[1][4]()
    for i in range(images):
        g_arrived(i)
    c_pos[0][4]()
    for done in (gather.sent, t_sent, c_sent, b_sent, g_sent):
        done()
    for swap in (swap_a, swap_b, swap_c, swap_d):
        swap[2]()
    for chunk in chunks:
        chunk[5]()


def chunk_table(width):
    groups = width // 256
    table = [(0, SMALL + 768, slice(0, 512))]
    for g in range(1, groups):
        table.append((SMALL + g * 768, SMALL + (g + 1) * 768, slice(128 + g * 384, 512 + g * 384)))
    end = 128 + groups * 384
    table.append((SMALL + 3 * width, SMALL + 4 * width, slice(end, end + width // 2)))
    return table


def finish_kernel(
    out_in, diff, cotangent, parts, rows_low, active, d_rows, d_hidden,
    block_out, grad_input, grad_qkv, grad_out_w, grad_small, grad_up, grad_down,
):
    block_out[...] = out_in[...]
    grad_input[...] = diff[...].astype(F32) + cotangent[...].astype(F32)
    grad_up[0] = tn(rows_low[...], d_hidden[...])
    grad_down[0] = tn(active[...], d_rows[...])

    @pl.when(pl.program_id(0) == 0)
    def _():
        width = grad_out_w.shape[1]
        quarter = grad_out_w.shape[0]
        total = parts[0].astype(F32)
        for k in range(1, 4):
            total = total + parts[k].astype(F32)
        for c, (lo, hi, narrow) in enumerate(chunk_table(width)):
            both = jnp.concatenate([total[:quarter, narrow], total[quarter:, narrow]], axis=1)
            if c == width // 256:
                grad_out_w[...] = both
                continue
            if c == 0:
                square = jnp.concatenate(
                    [both[:, :SMALL], jnp.zeros((128 - quarter, SMALL), F32)], axis=0
                )
                grad_small[...] = square.T[:16]
                both = both[:, SMALL:]
            for k in range(3):
                grad_qkv[:, k * width + c * 256 : k * width + (c + 1) * 256] = both[
                    :, k * 256 : (k + 1) * 256
                ]


def kernel_plan(
    tokens, lengths, w_qkv, w_out, router, gain_one, shift_one, gain_two, shift_two,
    w_up, w_down, cotangent,
):
    own_rows, width = w_out.shape
    blocks, size = tokens.shape[:2]
    images, length, experts = blocks // 4, 4 * size, router.shape[1]
    count = images * length
    groups = width // 256
    pairs = 2 * groups
    devices = 4 * experts
    columns = 4 * width + SMALL
    fan = w_up.shape[2]
    quarter = 4 * own_rows
    pair = (images, width)
    rows = devices * images

    def shape(*dims, kind=F32):
        return jax.ShapeDtypeStruct(dims, kind)

    dma = pltpu.SemaphoreType.DMA
    vmem, anywhere = pl.BlockSpec(memory_space=VM), pl.BlockSpec(memory_space=pl.ANY)
    stage_wide = 512 + (groups - 1) * 384 + width // 2
    outs = (
        shape(*tokens.shape, kind=BF),
        shape(*tokens.shape, kind=BF),
        shape(4, 2 * own_rows, stage_wide, kind=BF),
        shape(rows, width, kind=BF),
        shape(rows, fan, kind=BF),
        shape(rows, width, kind=BF),
        shape(rows, fan, kind=BF),
    )
    scratch = [
        VM((devices, 2 * own_rows, columns // 2 + 64), BF),
        VM((width, columns + 128), BF),
        VM((128, 128), F32),
        VM((16, width), F32),
        VM((count, width), BF),
        VM((count, width), BF),
        VM((count, 3 * width), BF),
        VM((images * pairs, length, 2 * length), BF),
        VM((count, width), BF),
        VM((count, width), F32),
        VM((count, width), BF),
        VM((count, width), BF),
        VM((experts, count), F32),
        VM((experts, count), F32),
        VM((experts, count), F32),
        VM((images, experts, width), F32),
        VM((images, 1, length), F32),
        VM((width, fan), BF),
        VM((fan, width), BF),
        VM((count, width), BF),
        VM((2, experts) + pair, BF),
        VM((images, experts, width), F32),
        VM((rows, width), F32),
    ]
    scratch += [VM((devices,) + pair, BF)] * 6
    scratch += [
        VM((width, count), BF),
        VM((width, count), BF),
        VM((count, width), F32),
        VM((count, width), F32),
        VM((count, width), BF),
        VM((count, width), BF),
        VM((count, 3 * width), BF),
        VM((count, width), BF),
        VM((width, columns), BF),
        VM((4, quarter, columns), BF),
        VM((6, quarter // 2, columns), BF),
        VM((4, 2 * own_rows, stage_wide), BF),
    ]
    scratch += [dma((4,))] * 7 + [dma((16,))] * 2 + [dma((4,))] * 2
    scratch += [dma((3 * images,))] * 8
    scratch += [dma((images,))] * 4
    scratch += [dma((2,)), dma((4,)), dma((4,))]
    chunks = groups + 1
    scratch += [dma((4 * chunks,))] * 2 + [dma((6 * chunks,))] * 2 + [dma((4 * chunks,))] * 2
    vectors = [vec[None, :] for vec in (gain_one, shift_one, gain_two, shift_two)]
    out_in, diff, parts, rows_low, active, d_rows, d_hidden = pl.pallas_call(
        block_kernel,
        out_shape=outs,
        in_specs=[pl.BlockSpec(memory_space=pltpu.SMEM)] + [vmem] * 7 + [anywhere] * 4,
        out_specs=[anywhere] * 3 + [vmem] * 4,
        scratch_shapes=scratch,
        compiler_params=pltpu.CompilerParams(
            collective_id=0, has_side_effects=True, vmem_limit_bytes=63 * 2**20
        ),
        name="block",
    )(lengths, w_qkv, w_out, router.T, *vectors, tokens, cotangent, w_up, w_down)

    def by_columns(*dims):
        return pl.BlockSpec(dims + (256,), lambda k: (0,) * len(dims) + (k,))

    def whole(*dims):
        return pl.BlockSpec(dims, lambda k: (0,) * len(dims))

    block_out, grad_input, grad_qkv, grad_out_w, grad_small, grad_up, grad_down = pl.pallas_call(
        finish_kernel,
        grid=(groups,),
        out_shape=(
            shape(*tokens.shape, kind=BF),
            shape(*tokens.shape),
            shape(own_rows, 3 * width),
            shape(own_rows, width),
            shape(16, 128),
            shape(*w_up.shape),
            shape(*w_down.shape),
        ),
        in_specs=[
            by_columns(blocks, size),
            by_columns(blocks, size),
            by_columns(blocks, size),
            whole(4, 2 * own_rows, stage_wide),
            whole(rows, width),
            whole(rows, fan),
            by_columns(rows),
            by_columns(rows),
        ],
        out_specs=[
            by_columns(blocks, size),
            by_columns(blocks, size),
            whole(own_rows, 3 * width),
            whole(own_rows, width),
            whole(16, 128),
            by_columns(1, width),
            by_columns(1, fan),
        ],
        compiler_params=pltpu.CompilerParams(vmem_limit_bytes=63 * 2**20),
        name="finish",
    )(out_in, diff, cotangent, parts, rows_low, active, d_rows, d_hidden)
    return (
        block_out,
        grad_input,
        grad_qkv,
        grad_out_w,
        grad_small[:experts, :own_rows].T,
        grad_small[experts, :own_rows],
        grad_small[experts + 1, :own_rows],
        grad_small[experts + 2, :own_rows],
        grad_small[experts + 3, :own_rows],
        grad_up,
        grad_down,
    )


def solution(mesh):
    plan = kernel_plan if dict(mesh.shape) == {"dp": 8, "seq": 4} else plain_plan
    rows, vector = P(("dp", "seq"), None), P(("dp", "seq"))
    tokens = P("dp", "seq", None)
    up, down = P("dp", None, "seq"), P("dp", "seq", None)
    return jax.shard_map(
        plan,
        mesh=mesh,
        in_specs=(tokens, P("dp"), rows, rows, rows)
        + (vector,) * 4
        + (up, down, tokens),
        out_specs=(tokens, tokens, rows, rows, rows) + (vector,) * 4 + (up, down),
        check_vma=False,
    )
```

```python
import jax
import jax.numpy as jnp
from jax import lax
from jax.experimental import pallas as pl
from jax.experimental.pallas import tpu as pltpu
from jax.sharding import PartitionSpec as P

H = 12
HD = 64
BF = jnp.bfloat16
F32 = jnp.float32


def dot(spec, a, b):
    return jnp.einsum(spec, a, b, preferred_element_type=F32)


def unit_norm(values):
    centred = values - jnp.mean(values, axis=-1, keepdims=True)
    inverse = lax.rsqrt(jnp.mean(centred * centred, axis=-1, keepdims=True) + 1e-06)
    return centred * inverse, inverse


def norm_back(grad_rows, unit_rows, inverse, gain):
    scaled = grad_rows * gain
    centred = scaled - jnp.mean(scaled, axis=-1, keepdims=True)
    correction = unit_rows * jnp.mean(scaled * unit_rows, axis=-1, keepdims=True)
    return (
        inverse * (centred - correction),
        jnp.sum(grad_rows * unit_rows, axis=(0, 1)),
        jnp.sum(grad_rows, axis=(0, 1)),
    )


def gelu_tanh(values):
    return jax.nn.gelu(values, approximate=True)


def to_images(array):
    return lax.all_to_all(array, "seq", split_axis=0, concat_axis=1, tiled=True)


def to_blocks(array):
    return lax.all_to_all(array, "seq", split_axis=1, concat_axis=0, tiled=True)


def to_experts(rows):
    rows = lax.all_to_all(rows, "dp", split_axis=1, concat_axis=0, tiled=True)
    return lax.all_gather(rows, "seq", axis=0, tiled=True)


def from_experts(rows):
    rows = lax.psum_scatter(rows, "seq", scatter_dimension=0, tiled=True).astype(BF)
    return lax.all_to_all(rows, "dp", split_axis=0, concat_axis=1, tiled=True)


def plain_plan(
    tokens, lengths, w_qkv, w_out, router, gain_one, shift_one, gain_two, shift_two,
    w_up, w_down, cotangent,
):
    groups = lax.axis_size("seq")
    model_width, slots_all = w_qkv.shape[1] // 3, router.shape[1]
    packed = jnp.concatenate(
        [w_qkv, w_out, router]
        + [vec[:, None] for vec in (gain_one, shift_one, gain_two, shift_two)],
        axis=1,
    )
    packed = lax.all_gather(packed, ("dp", "seq"), axis=0, tiled=True)
    split = 4 * model_width
    w_qkv, w_out = packed[:, : 3 * model_width], packed[:, 3 * model_width : split]
    router = packed[:, split : split + slots_all]
    gain_one, shift_one, gain_two, shift_two = (
        packed[:, split + slots_all + k].astype(F32) for k in range(4)
    )
    x = to_images(tokens).astype(F32)
    cot = to_images(cotangent)
    images, length_all = x.shape[:2]
    lengths_own = lax.dynamic_slice_in_dim(lengths, lax.axis_index("seq") * images, images)
    valid = jnp.arange(length_all, dtype=jnp.int32)[None, :] < lengths_own[:, None]

    unit_one, inverse_one = unit_norm(x)
    normed_one = (unit_one * gain_one + shift_one).astype(BF)
    qkv = dot("btd,de->bte", normed_one, w_qkv).astype(BF).reshape(images, length_all, 3, H, HD)
    queries, keys_all, values_all = qkv[:, :, 0], qkv[:, :, 1], qkv[:, :, 2]
    scores = dot("bqhd,bkhd->bhqk", queries, keys_all) * HD ** (-0.5)
    probs = jax.nn.softmax(jnp.where(valid[:, None, None, :], scores, -1000000000.0), axis=-1)
    probs_low = probs.astype(BF)
    attended = dot("bhqk,bkhd->bqhd", probs_low, values_all).astype(BF)
    attended = attended.reshape(images, length_all, model_width)
    middle = x + dot("btd,de->bte", attended, w_out)
    unit_two, inverse_two = unit_norm(middle)
    normed_two = (unit_two * gain_two + shift_two).astype(BF)
    logits = dot("btd,de->bte", normed_two, router)
    top = jnp.floor(jnp.max(jnp.where(valid[:, :, None], logits, -1000000000.0), axis=1))
    dispatch = jnp.where(valid[:, :, None], jnp.exp(logits - top[:, None, :]), 0.0)
    dispatch_low = dispatch.astype(BF)
    denominator = jnp.sum(dispatch, axis=1)
    slot_vals = dot("bte,btd->bed", dispatch_low, normed_two) / denominator[:, :, None]
    slot_rows = to_experts(slot_vals.astype(BF))
    hidden = dot("red,edf->ref", slot_rows, w_up)
    active = gelu_tanh(hidden).astype(BF)
    expert_out = from_experts(dot("ref,efd->red", active, w_down))
    combine = jax.nn.softmax(logits, axis=-1)
    combine_low = combine.astype(BF)
    block_out = (middle + dot("bte,bed->btd", combine_low, expert_out)).astype(BF)

    d_combine = dot("btd,bed->bte", cot, expert_out)
    d_expert = dot("bte,btd->bed", combine_low, cot).astype(BF)
    d_rows = to_experts(d_expert)
    d_active = dot("red,efd->ref", d_rows, w_down)
    grad_down = dot("ref,red->efd", active, d_rows)
    d_hidden = jax.vjp(gelu_tanh, hidden)[1](d_active)[0].astype(BF)
    grad_up = dot("red,ref->edf", slot_rows, d_hidden)
    d_slots = from_experts(dot("ref,edf->red", d_hidden, w_up))
    d_slots_wide = d_slots.astype(F32)
    inner = jnp.sum(slot_vals * d_slots_wide, axis=-1)
    projected = dot("btd,bed->bte", normed_two, d_slots)
    d_logits = (projected - inner[:, None, :]) / denominator[:, None, :] * dispatch
    d_logits = d_logits + combine * (
        d_combine - jnp.sum(combine * d_combine, axis=-1, keepdims=True)
    )
    d_logits = d_logits.astype(BF)
    scaled = d_slots_wide / denominator[:, :, None]
    scaled_high = scaled.astype(BF)
    scaled_rest = (scaled - scaled_high.astype(F32)).astype(BF)
    d_normed_two = (
        dot("bte,bed->btd", dispatch_low, scaled_high)
        + dot("bte,bed->btd", dispatch_low, scaled_rest)
        + dot("bte,de->btd", d_logits, router)
    )
    grad_router = dot("btd,bte->de", normed_two, d_logits)
    d_norm, grad_gain_two, grad_shift_two = norm_back(d_normed_two, unit_two, inverse_two, gain_two)
    d_middle = cot.astype(F32) + d_norm
    d_branch = d_middle.astype(BF)
    grad_out_w = dot("btd,bte->de", attended, d_branch)
    d_attended = dot("bte,de->btd", d_branch, w_out).astype(BF)
    d_attended = d_attended.reshape(images, length_all, H, HD)
    d_values = dot("bhqk,bqhd->bkhd", probs_low, d_attended)
    d_probs = dot("bqhd,bkhd->bhqk", d_attended, values_all)
    d_scores = probs * (d_probs - jnp.sum(probs * d_probs, axis=-1, keepdims=True))
    d_scores = d_scores.astype(BF)
    d_queries = dot("bhqk,bkhd->bqhd", d_scores, keys_all) * HD ** (-0.5)
    d_keys = dot("bhqk,bqhd->bkhd", d_scores, queries) * HD ** (-0.5)
    d_qkv = jnp.stack([d_queries, d_keys, d_values], axis=2).astype(BF)
    d_qkv = d_qkv.reshape(images, length_all, 3 * model_width)
    grad_qkv = dot("btd,bte->de", normed_one, d_qkv)
    d_normed_one = dot("bte,de->btd", d_qkv, w_qkv)
    d_norm, grad_gain_one, grad_shift_one = norm_back(d_normed_one, unit_one, inverse_one, gain_one)
    grad_input = to_blocks(d_middle + d_norm)

    vectors = (grad_gain_one, grad_shift_one, grad_gain_two, grad_shift_two)
    packed = jnp.concatenate(
        [grad_qkv, grad_out_w, grad_router] + [vec[:, None] for vec in vectors], axis=1
    )
    packed = lax.psum_scatter(packed, ("dp", "seq"), scatter_dimension=0, tiled=True)
    return (
        to_blocks(block_out),
        grad_input,
        packed[:, : 3 * model_width],
        packed[:, 3 * model_width : split],
        packed[:, split : split + slots_all],
        packed[:, split + slots_all],
        packed[:, split + slots_all + 1],
        packed[:, split + slots_all + 2],
        packed[:, split + slots_all + 3],
        grad_up,
        grad_down,
    )


MESH = pl.DeviceIdType.MESH
VM = pltpu.VMEM
SMALL = 128
ROWS = 64


def nt(a, b):
    return lax.dot_general(a, b, (((1,), (1,)), ((), ())), preferred_element_type=F32)


def tn(a, b):
    return lax.dot_general(a, b, (((0,), (0,)), ((), ())), preferred_element_type=F32)


def mm(a, b):
    return jnp.dot(a, b, preferred_element_type=F32)


def ds(start, size, unit=None):
    return pl.ds(pl.multiple_of(start, unit or size), size)


def remote(src, dst, send, recv, device):
    return pltpu.make_async_remote_copy(
        src_ref=src, dst_ref=dst, send_sem=send, recv_sem=recv, device_id=device,
        device_id_type=MESH,
    )


def other(d, kind):
    core, x, y = lax.rem(d, 2), lax.rem(d // 2, 2), d // 4
    return {"x": d + 2 - 4 * x, "y": d + 4 - 8 * y, "core": d + 1 - 2 * core}[kind]


class Gather:
    def __init__(self, shards, full, zup, zdown, zrecv, xsend, xrecv, ysend, yrecv, csend, crecv, dsend, drecv):
        d, z = lax.axis_index("dp"), lax.axis_index("seq")
        dx, dy, dc = other(d, "x"), other(d, "y"), other(d, "core")
        self.shards, self.full, self.z = shards, full, z
        self.owners = (d, dx, dy, other(dx, "y"))
        self.over = {"x": (dx, z), "y": (dy, z), "core": (dc, z)}
        self.up, self.down = (d, lax.rem(z + 1, 4)), (d, lax.rem(z + 3, 4))
        self.sems = {
            "up": (zup, zrecv), "down": (zdown, zrecv), "x": (xsend, xrecv),
            "y": (ysend, yrecv), "core": (csend, crecv), "d": (dsend, drecv),
        }

    def copy(self, kind, owner, s, device, sem):
        ref = self.shards.at[owner * 4 + s]
        send, recv = self.sems[kind]
        return remote(ref, ref, send.at[sem], recv.at[sem], device)

    def pass_on(self, s, upward, downward):
        d, z = self.owners[0], self.z
        if upward:

            @pl.when(z < 3)
            def _():
                self.copy("up", d, s, self.up, s).start()

        if downward:

            @pl.when(z > 0)
            def _():
                self.copy("down", d, s, self.down, s).start()

        self.copy("x", d, s, self.over["x"], s).start()
        self.copy("y", d, s, self.over["y"], s).start()
        self.copy("core", d, s, self.over["core"], s).start()

    def each(self, h, act):
        if h == 0:
            act(self.z)
            return

        @pl.when(self.z >= h)
        def _():
            act(self.z - h)

        @pl.when(self.z + h <= 3)
        def _():
            act(self.z + h)

    def line(self, h):
        d, z = self.owners[0], self.z
        if h == 0:
            self.pass_on(z, True, True)
            return

        @pl.when(z >= h)
        def _():
            self.copy("up", d, z - h, self.up, z - h).wait_recv()
            self.pass_on(z - h, True, False)

        @pl.when(z + h <= 3)
        def _():
            self.copy("down", d, z + h, self.down, z + h).wait_recv()
            self.pass_on(z + h, False, True)

    def plane(self, h):
        d, dx, dy, dd = self.owners

        def act(s):
            self.copy("x", dx, s, self.over["x"], s).wait_recv()

            @pl.when(lax.rem(s, 2) == 0)
            def _():
                self.copy("d", dx, s, self.over["y"], s).start()

            self.copy("core", dx, s, self.over["core"], 4 + s).start()
            self.copy("y", dy, s, self.over["y"], s).wait_recv()

            @pl.when(lax.rem(s, 2) == 1)
            def _():
                self.copy("d", dy, s, self.over["x"], s).start()

            self.copy("core", dy, s, self.over["core"], 8 + s).start()

        self.each(h, act)

    def diagonal(self, h):
        def act(s):
            self.copy("d", self.owners[3], s, self.over["x"], s).wait_recv()
            self.copy("core", self.owners[3], s, self.over["core"], 12 + s).start()

        self.each(h, act)

    def twin(self, k):
        dc = other(self.owners[k], "core")
        for s in range(4):
            self.copy("core", dc, s, self.over["core"], 4 * k + s).wait_recv()
        self.assemble(dc)

    def assemble(self, owner):
        half, wide = self.shards.shape[1:]
        quarter = half // 2
        for side in range(2):
            value = jnp.concatenate(
                [
                    self.shards[owner * 4 + k].astype(F32)[side * quarter : (side + 1) * quarter]
                    for k in range(4)
                ],
                axis=0,
            )
            self.full[ds(owner * 2 * half, 2 * half), side * wide : (side + 1) * wide] = (
                value.astype(BF)
            )

    def sent(self):
        d, z = self.owners[0], self.z

        def one(s, carry):
            @pl.when((s <= z) & (z < 3))
            def _():
                self.copy("up", d, s, self.up, s).wait_send()

            @pl.when((s >= z) & (z > 0))
            def _():
                self.copy("down", d, s, self.down, s).wait_send()

            self.copy("x", d, s, self.over["x"], s).wait_send()
            self.copy("y", d, s, self.over["y"], s).wait_send()
            self.copy("d", d, s, self.over["x"], s).wait_send()
            for k in range(4):
                self.copy("core", self.owners[k], s, self.over["core"], 4 * k + s).wait_send()
            return carry

        lax.fori_loop(0, 4, one, 0)


def image_steps(blocks, whole, send, recv, local_sem, images, home):
    d, z = lax.axis_index("dp"), lax.axis_index("seq")
    size = blocks.shape[1]
    length = 4 * size

    def make(i, k):
        there = lax.rem(z + k, 4)
        if home:
            src = whole.at[ds(i * length + there * size, size)]
            dst = blocks.at[z * images + i]
        else:
            src = blocks.at[there * images + i]
            dst = whole.at[ds(i * length + z * size, size)]
        if k == 0:
            return pltpu.make_async_copy(src, dst, local_sem.at[i])
        return remote(src, dst, send.at[i * 3 + k - 1], recv.at[i * 3 + k - 1], (d, there))

    table = [[make(i, k) for k in range(4)] for i in range(images)]

    def start(i):
        for one in table[i]:
            one.start()

    def arrived(i):
        table[i][0].wait()
        for one in table[i][1:]:
            one.wait_recv()

    def sent():
        for i in range(images):
            for one in table[i][1:]:
                one.wait_send()

    return start, arrived, sent


def swap_steps(src, dst, send, recv, to_expert):
    d, z = lax.axis_index("dp"), lax.axis_index("seq")
    count = dst.shape[0]
    me = d * 4 + z

    def start():
        def one(k, carry):
            j = lax.rem(me + k, count)
            e = j // 4
            row = src.at[e] if to_expert else src.at[j]
            remote(row, dst.at[me], send, recv, (e, lax.rem(j, 4))).start()
            return carry

        lax.fori_loop(1, count, one, 0)
        pltpu.make_async_copy(src.at[d] if to_expert else src.at[me], dst.at[me], recv).start()

    def arrived():
        pltpu.make_async_copy(dst, dst, recv).wait()

    def sent():
        part = dst.at[pl.ds(0, count - 1)]
        remote(part, part, send, recv, (other(d, "x"), z)).wait_send()

    return start, arrived, sent


def reduce_steps(grads, pairs, inter, out_stage, in_stage, sems, chunk, lo, hi, narrow):
    d, z = lax.axis_index("dp"), lax.axis_index("seq")
    dx, dy, dc = other(d, "x"), other(d, "y"), other(d, "core")
    core = lax.rem(d, 2)
    over_x, over_y, over_c = (dx, z), (dy, z), (dc, z)
    rows = pairs.shape[1]
    half, quarter = rows // 2, rows // 4
    cols = slice(lo, hi)
    send1, recv1, send2, recv2, send3, recv3 = sems
    chips = pairs.shape[0]

    step1 = []
    for m in range(chips):
        block = grads.at[ds((2 * m + 1 - core) * rows, rows), cols]
        n = chunk * chips + m
        step1.append(remote(block, pairs.at[m, :, cols], send1.at[n], recv1.at[n], over_c))
    here, mx, my, md = d // 2, dx // 2, dy // 2, other(dx, "y") // 2

    def part(m, h):
        return pairs.at[m, h * half : (h + 1) * half, cols]

    def hop(k, m, h, device):
        n = chunk * 6 + k
        return remote(part(m, h), inter.at[k, :, cols], send2.at[n], recv2.at[n], device)

    step2 = [
        hop(0, md, 0, over_y), hop(1, md, 1, over_x), hop(2, my, 0, over_y),
        hop(3, mx, 1, over_x), hop(4, mx, 0, over_x), hop(5, my, 1, over_y),
    ]
    local_copy = pltpu.make_async_copy(
        out_stage.at[z, :, narrow], in_stage.at[3, :, narrow], recv3.at[chunk * 4 + 3]
    )
    step3 = []
    for k in range(1, 4):
        n = chunk * 4 + k - 1
        there = lax.rem(z + k, 4)
        step3.append(
            remote(
                out_stage.at[there, :, narrow], in_stage.at[k - 1, :, narrow],
                send3.at[n], recv3.at[n], (d, there),
            )
        )

    def one():
        for c in step1:
            c.start()

    def two():
        for m in range(chips):
            step1[m].wait_recv()
            own = grads[ds((2 * m + core) * rows, rows), cols].astype(F32)
            pairs[m, :, cols] = (own + pairs[m, :, cols].astype(F32)).astype(BF)
        for k in range(4):
            step2[k].start()

    def three():
        for k, m, h in ((0, mx, 0), (1, my, 1)):
            step2[k].wait_recv()
            at = slice(h * half, (h + 1) * half)
            total = pairs[m, at, cols].astype(F32) + inter[k, :, cols].astype(F32)
            pairs[m, at, cols] = total.astype(BF)
            step2[4 + k].start()

    def four():
        for k in (2, 3, 4, 5):
            step2[k].wait_recv()
        own = pairs[here, :, cols].astype(F32)
        top = own[:half] + inter[2, :, cols].astype(F32) + inter[4, :, cols].astype(F32)
        low = own[half:] + inter[3, :, cols].astype(F32) + inter[5, :, cols].astype(F32)
        total = jnp.concatenate([top, low], axis=0)
        middle = narrow.stop - narrow.start
        if 2 * middle > hi - lo:
            filler = jnp.zeros((rows, 2 * middle - (hi - lo)), F32)
            total = jnp.concatenate([total, filler], axis=1)
        for t in range(4):
            shard = total[t * quarter : (t + 1) * quarter]
            both = jnp.concatenate([shard[:, :middle], shard[:, middle:]], axis=0)
            out_stage[t, :, narrow] = both.astype(BF)
        for c in step3:
            c.start()
        local_copy.start()

    def five():
        for c in step3:
            c.wait_recv()
        local_copy.wait()

    def sent():
        for c in step1 + step2 + step3:
            c.wait_send()

    return one, two, three, four, five, sent


def unit_rows(x):
    centred = x - jnp.mean(x, axis=-1, keepdims=True)
    inverse = lax.rsqrt(jnp.mean(centred * centred, axis=-1, keepdims=True) + 1e-06)
    return centred * inverse, inverse


def fold_rows(x):
    total = x[:8]
    for k in range(1, x.shape[0] // 8):
        total = total + x[8 * k : 8 * (k + 1)]
    return total


def norm_rows_back(grad, unit, inverse, gain):
    scaled = grad * gain
    centred = scaled - jnp.mean(scaled, axis=-1, keepdims=True)
    correction = unit * jnp.mean(scaled * unit, axis=-1, keepdims=True)
    return inverse * (centred - correction)


def split_heads(pair):
    lane = lax.broadcasted_iota(jnp.int32, (1, 2 * HD), 1)
    left = jnp.where(lane < HD, 1.0, 0.0)
    return jnp.concatenate([pair * left.astype(BF), pair * (1.0 - left).astype(BF)], axis=0)


def join_heads(pair):
    lane = lax.broadcasted_iota(jnp.int32, (1, 2 * HD), 1)
    rows = pair.shape[0] // 2
    return jnp.where(lane < HD, pair[:rows], pair[rows:])


def gelu_parts(v):
    inner = jnp.tanh(0.7978845608 * (v + 0.044715 * v * v * v))
    slope = 0.5 * (1.0 + inner) + 0.5 * v * (1.0 - inner * inner) * 0.7978845608 * (
        1.0 + 3.0 * 0.044715 * v * v
    )
    return 0.5 * v * (1.0 + inner), slope


def block_kernel(
    lengths, w_qkv, w_out, router_own, gain_a, shift_a, gain_b, shift_b, tokens, cotangent,
    w_up, w_down,
    block_out, g_blocks, in_stage, rows_low, active, d_rows, d_hidden,
    shards, full, corner, small, xs, cots, qkv, probs, attended, middle, n_one, n_two,
    disp, comb, dcomb, slots, bias, up, down, out_rows, pair_in, pair_out, row_sums,
    recv_a, recv_b, recv_c, recv_d, send_b, send_d, turned_one, turned_att,
    d_norm, d_diff, d_branch, d_attended, d_qkv, g_rows,
    grads, pairs_buf, inter, out_stage,
    zup, zdown, zrecv, xsend, xrecv, ysend, yrecv, wsend, wrecv, dsend, drecv, tsend, trecv, csend, crecv, bsend, brecv, gsend, grecv,
    t_local, c_local, b_local, g_local, loads, swap_send, swap_recv,
    send1, recv1, send2, recv2, send3, recv3,
):
    d, z = lax.axis_index("dp"), lax.axis_index("seq")
    width = tokens.shape[2]
    images = tokens.shape[0] // 4
    length = 4 * tokens.shape[1]
    count = images * length
    groups = width // 256
    experts = disp.shape[0]
    devices = recv_a.shape[0]
    base_qkv, base_out = SMALL, SMALL + 3 * width

    barrier = pltpu.get_barrier_semaphore()
    partners = [(d, lax.rem(z + k, 4)) for k in range(1, 4)]
    partners += [(other(d, kind), z) for kind in ("x", "y", "core")]
    for partner in partners:
        pl.semaphore_signal(barrier, inc=1, device_id=partner, device_id_type=MESH)
    load_up = pltpu.make_async_copy(w_up.at[0], up, loads.at[0])
    load_down = pltpu.make_async_copy(w_down.at[0], down, loads.at[1])
    load_up.start()
    load_down.start()
    own_rows = w_out.shape[0]
    corner[...] = jnp.zeros_like(corner)
    corner[0:experts, 0:own_rows] = router_own[...].astype(F32)
    for k, vector in enumerate((gain_a, shift_a, gain_b, shift_b)):
        corner[experts + k : experts + k + 1, 0:own_rows] = vector[...].astype(F32)
    own = w_qkv[...].astype(F32)
    pieces = [corner[...].T[:own_rows]]
    for g in range(groups):
        for k in range(3):
            pieces.append(own[:, k * width + g * 256 : k * width + (g + 1) * 256])
    pieces += [w_out[...].astype(F32), jnp.zeros((own_rows, 128), F32)]
    line = jnp.concatenate(pieces, axis=1)
    wide = shards.shape[2]
    shards[d * 4 + z] = jnp.concatenate([line[:, :wide], line[:, wide:]], axis=0).astype(BF)
    pl.semaphore_wait(barrier, len(partners))

    gather = Gather(
        shards, full, zup, zdown, zrecv, xsend, xrecv, ysend, yrecv, wsend, wrecv, dsend, drecv
    )
    t_start, t_arrived, t_sent = image_steps(tokens, xs, tsend, trecv, t_local, images, False)
    c_start, c_arrived, c_sent = image_steps(cotangent, cots, csend, crecv, c_local, images, False)
    gather.line(0)
    gather.line(1)
    gather.plane(0)
    gather.line(2)
    t_start(0)
    gather.plane(1)
    gather.diagonal(0)
    gather.line(3)
    for i in range(1, images):
        t_start(i)
    gather.plane(2)
    gather.diagonal(1)
    gather.assemble(d)
    gather.plane(3)
    gather.diagonal(2)
    gather.twin(0)
    gather.diagonal(3)
    for k in range(1, 4):
        gather.assemble(gather.owners[k])
        gather.twin(k)
    small[...] = full[:, 0:128].astype(F32).T[:16]
    gains = [small[8 + k : 9 + k, :] for k in range(4)]

    def norm_one(k, carry):
        at = ds(k * ROWS, ROWS)
        unit, _ = unit_rows(xs[at, :].astype(F32))
        n_one[at, :] = (unit * gains[0] + gains[1]).astype(BF)
        return carry

    per_image = length // ROWS
    for i in range(images):
        t_arrived(i)
        if i == images - 1:
            for k in range(images):
                c_start(k)
        lax.fori_loop(i * per_image, (i + 1) * per_image, norm_one, 0)

    def project(k, carry):
        weight = full[:, ds(base_qkv + k * 256, 256, 128)]
        qkv[:, ds(k * 256, 256)] = mm(n_one[...], weight).astype(BF)
        return carry

    lax.fori_loop(0, 3 * groups, project, 0)

    key = lax.broadcasted_iota(jnp.int32, (1, length), 1)
    for i in range(images):
        bias[i] = jnp.where(key < lengths[z * images + i], 0.0, -1000000000.0)
    scale = jnp.asarray(HD ** (-0.5), BF)
    pairs = 2 * groups

    def heads(t):
        i, p = t // pairs, pairs - 1 - lax.rem(t, pairs)
        base = (p // 2) * 768 + lax.rem(p, 2) * 128
        return i, p, ds(i * length, length), base

    def attend(t, carry):
        i, p, at, base = heads(t)
        keys = split_heads(qkv[at, ds(base + 256, 128)])
        values = split_heads(qkv[at, ds(base + 512, 128)])
        scores = nt(qkv[at, ds(base, 128)] * scale, keys)
        for h in range(2):
            part = scores[:, h * length : (h + 1) * length] + bias[i]
            e = jnp.exp(part - jnp.max(part, axis=-1, keepdims=True))
            total = jnp.sum(e, axis=-1, keepdims=True)
            probs[t, :, h * length : (h + 1) * length] = (e * (1.0 / total)).astype(BF)
        attended[at, ds(p * 128, 128)] = mm(probs[t], values).astype(BF)
        return carry

    lax.fori_loop(0, images * pairs, attend, 0, unroll=2)

    def project_out(k, carry):
        at = ds(k * 256, 256)
        weight = full[:, ds(base_out + k * 256, 256, 128)]
        middle[:, at] = xs[:, at].astype(F32) + mm(attended[...], weight)
        return carry

    lax.fori_loop(0, groups, project_out, 0)

    def norm_two(k, carry):
        at = ds(k * ROWS, ROWS)
        unit, _ = unit_rows(middle[at, :])
        n_two[at, :] = (unit * gains[2] + gains[3]).astype(BF)
        return carry

    lax.fori_loop(0, count // ROWS, norm_two, 0)
    router = small[0:8, :].astype(BF)
    spans = [slice(i * length, (i + 1) * length) for i in range(images)]
    denominators = []
    for i, at in enumerate(spans):
        logits = nt(router, n_two[at, :])
        inside = key < lengths[z * images + i]
        top = jnp.floor(
            jnp.max(jnp.where(inside, logits, -1000000000.0), axis=-1, keepdims=True)
        )
        dispatch = jnp.where(inside, jnp.exp(logits - top), 0.0)
        e = jnp.exp(logits - jnp.max(logits, axis=0, keepdims=True))
        disp[:, at] = dispatch
        comb[:, at] = e / jnp.sum(e, axis=0, keepdims=True)
        denominators.append(jnp.sum(dispatch, axis=-1, keepdims=True))
        slots[i] = mm(dispatch.astype(BF), n_two[at, :]) / denominators[i]

    swap_a = swap_steps(pair_in.at[0], recv_a, swap_send.at[0], swap_recv.at[0], True)
    swap_b = swap_steps(send_b, recv_b, swap_send.at[1], swap_recv.at[1], False)
    swap_c = swap_steps(pair_in.at[1], recv_c, swap_send.at[2], swap_recv.at[2], True)
    swap_d = swap_steps(send_d, recv_d, swap_send.at[3], swap_recv.at[3], False)

    def to_pairs(which, values):
        for e in range(experts):
            pair_in[which, e] = jnp.concatenate(
                [value[e : e + 1] for value in values], axis=0
            ).astype(BF)

    def from_pairs(ref):
        for j in range(devices):
            row_sums[images * j : images * (j + 1), :] = ref[j].astype(F32)
        return row_sums[...].astype(BF)

    def spread(ref, value):
        row_sums[...] = value
        for j in range(devices):
            ref[j] = row_sums[images * j : images * (j + 1), :].astype(BF)

    def collect(ref):
        for e in range(experts):
            total = ref[4 * e].astype(F32)
            for k in range(1, 4):
                total = total + ref[4 * e + k].astype(F32)
            for i in range(images):
                pair_out[i, e : e + 1, :] = total[i : i + 1]
        return [pair_out[i].astype(BF) for i in range(images)]

    to_pairs(0, [slots[i] for i in range(images)])
    swap_a[0]()
    combs = [comb[:, at].astype(BF) for at in spans]
    sends = []
    for i, at in enumerate(spans):
        c_arrived(i)
        sends.append(mm(combs[i], cots[at, :]))
    to_pairs(1, sends)
    swap_c[0]()
    load_up.wait()
    load_down.wait()
    swap_a[1]()
    rows_low[...] = from_pairs(recv_a)
    hidden = mm(rows_low[...], up[...])
    act, slope = gelu_parts(hidden)
    active[...] = act.astype(BF)
    spread(send_b, mm(active[...], down[...]))
    swap_b[0]()
    swap_c[1]()
    d_rows[...] = from_pairs(recv_c)
    d_active = nt(d_rows[...], down[...])
    d_hidden[...] = (d_active * slope).astype(BF)
    spread(send_d, nt(d_hidden[...], up[...]))
    swap_d[0]()
    turned_one[...] = n_one[...].T
    turned_att[...] = attended[...].T
    swap_b[1]()
    outs = collect(recv_b)
    b_start, b_arrived, b_sent = image_steps(
        block_out, out_rows, bsend, brecv, b_local, images, True
    )
    for i, at in enumerate(spans):
        for k in range(groups):
            cols = slice(k * 256, (k + 1) * 256)
            moe = tn(combs[i], outs[i][:, cols])
            out_rows[at, cols] = (middle[at, cols] + moe).astype(BF)
        dcomb[:, at] = nt(outs[i], cots[at, :])
        b_start(i)
    swap_d[1]()
    d_slots = collect(recv_d)

    router_grad = jnp.zeros((experts, width), F32)
    for i, at in enumerate(spans):
        wide_slots = d_slots[i].astype(F32)
        inner = jnp.sum(slots[i] * wide_slots, axis=-1, keepdims=True)
        projected = nt(d_slots[i], n_two[at, :])
        weight, change = comb[:, at], dcomb[:, at]
        d_logits = (projected - inner) / denominators[i] * disp[:, at]
        d_logits = d_logits + weight * (
            change - jnp.sum(weight * change, axis=0, keepdims=True)
        )
        router_grad = router_grad + mm(d_logits.astype(BF), n_two[at, :])
        scaled = wide_slots / denominators[i]
        high = scaled.astype(BF).astype(F32)
        left = jnp.concatenate(
            [disp[:, at], disp[:, at], d_logits, jnp.zeros_like(d_logits)], axis=0
        ).astype(BF)
        right = jnp.concatenate(
            [high, scaled - high, small[0:8, :], jnp.zeros_like(scaled)], axis=0
        ).astype(BF)
        for k in range(groups):
            cols = slice(k * 256, (k + 1) * 256)
            d_norm[at, cols] = tn(left, right[:, cols])

    nothing = jnp.zeros((8, width), F32)

    def back_two(k, carry):
        at = ds(k * ROWS, ROWS)
        grad = d_norm[at, :]
        unit, inverse = unit_rows(middle[at, :])
        change = norm_rows_back(grad, unit, inverse, gains[2])
        d_diff[at, :] = change
        d_branch[at, :] = (change + cots[at, :].astype(F32)).astype(BF)
        return carry[0] + fold_rows(grad * unit), carry[1] + fold_rows(grad)

    gain_two, shift_two = lax.fori_loop(0, count // ROWS, back_two, (nothing, nothing))

    sems = (send1, recv1, send2, recv2, send3, recv3)
    chunks = [
        reduce_steps(
            grads, pairs_buf, inter, out_stage, in_stage, sems, c, lo, hi, narrow
        )
        for c, (lo, hi, narrow) in enumerate(chunk_table(width))
    ]
    c_out, c_pos = chunks[groups], chunks[:groups]

    def grad_out(k, carry):
        cols = ds(k * 256, 256)
        to = ds(base_out + k * 256, 256, 128)
        grads[:, to] = mm(turned_att[...], d_branch[:, cols]).astype(BF)
        return carry

    lax.fori_loop(0, groups, grad_out, 0)
    c_out[0]()

    def back_out(k, carry):
        at = ds(k * 256, 256)
        d_attended[:, at] = nt(d_branch[...], full[at, base_out : base_out + width]).astype(BF)
        return carry

    lax.fori_loop(0, groups, back_out, 0)

    def attend_back(t, carry):
        i, p, at, base = heads(t)
        q = qkv[at, ds(base, 128)] * scale
        keys = split_heads(qkv[at, ds(base + 256, 128)])
        values = split_heads(qkv[at, ds(base + 512, 128)])
        grad = d_attended[at, ds(p * 128, 128)]
        d_values = join_heads(tn(probs[t], grad))
        d_probs = nt(grad, values)
        cuts = []
        for h in range(2):
            cut = slice(h * length, (h + 1) * length)
            weight = probs[t, :, cut].astype(F32)
            change = weight * d_probs[:, cut]
            total = jnp.sum(change, axis=-1, keepdims=True)
            cuts.append((change - weight * total).astype(BF))
        d_scores = jnp.concatenate(cuts, axis=1)
        d_qkv[at, ds(base, 128)] = (mm(d_scores, keys) * HD ** (-0.5)).astype(BF)
        d_qkv[at, ds(base + 256, 128)] = join_heads(tn(d_scores, q)).astype(BF)
        d_qkv[at, ds(base + 512, 128)] = d_values.astype(BF)
        return carry

    def group_grads(g):
        def one(k, carry):
            at = ds(g * 768 + k * 256, 256)
            to = ds(base_qkv + g * 768 + k * 256, 256, 128)
            grads[:, to] = mm(turned_one[...], d_qkv[:, at]).astype(BF)
            return carry

        lax.fori_loop(0, 3, one, 0)

    def input_grads(i, carry):
        at = spans[i]

        def back_qkv(k, carry):
            cols = ds(k * 256, 256)
            d_norm[at, cols] = nt(d_qkv[at, :], full[cols, base_qkv : base_qkv + 3 * width])
            return carry

        def back_one(k, carry):
            at = ds(k * ROWS, ROWS)
            grad = d_norm[at, :]
            unit, inverse = unit_rows(xs[at, :].astype(F32))
            change = norm_rows_back(grad, unit, inverse, gains[0])
            g_rows[at, :] = (change + d_diff[at, :]).astype(BF)
            return carry[0] + fold_rows(grad * unit), carry[1] + fold_rows(grad)

        lax.fori_loop(0, groups, back_qkv, 0)
        carry = lax.fori_loop(i * per_image, (i + 1) * per_image, back_one, carry)
        g_start(i)
        return carry

    g_start, g_arrived, g_sent = image_steps(
        g_blocks, g_rows, gsend, grecv, g_local, images, True
    )
    sums_one = (nothing, nothing)
    for i in range(images - 1):
        lax.fori_loop(i * pairs, (i + 1) * pairs, attend_back, 0, unroll=2)
        if i == 0:
            c_out[1]()
        sums_one = input_grads(i, sums_one)
    begin = (images - 1) * pairs
    lax.fori_loop(begin, begin + 2, attend_back, 0, unroll=2)
    c_out[2]()
    group_grads(2)
    c_pos[2][0]()
    lax.fori_loop(begin + 2, begin + 4, attend_back, 0, unroll=2)
    c_out[3]()
    c_pos[2][1]()
    group_grads(1)
    c_pos[1][0]()
    lax.fori_loop(begin + 4, begin + 6, attend_back, 0, unroll=2)
    c_pos[2][2]()
    c_pos[1][1]()
    gain_one, shift_one = input_grads(images - 1, sums_one)
    sums = [
        jnp.sum(value, axis=0, keepdims=True)
        for value in (gain_one, shift_one, gain_two, shift_two)
    ]
    tall = jnp.concatenate(
        [router_grad] + sums + [jnp.zeros((128 - experts - 4, width), F32)], axis=0
    )
    grads[:, 0:SMALL] = tall.T.astype(BF)
    group_grads(0)
    c_pos[0][0]()
    c_pos[1][2]()
    c_pos[2][3]()
    c_pos[0][1]()
    c_pos[1][3]()
    c_pos[0][2]()
    c_pos[0][3]()
    for i in range(images):
        b_arrived(i)
    c_out[4]()
    c_pos[2][4]()
    c_pos[1][4]()
    for i in range(images):
        g_arrived(i)
    c_pos[0][4]()
    for done in (gather.sent, t_sent, c_sent, b_sent, g_sent):
        done()
    for swap in (swap_a, swap_b, swap_c, swap_d):
        swap[2]()
    for chunk in chunks:
        chunk[5]()


def chunk_table(width):
    groups = width // 256
    table = [(0, SMALL + 768, slice(0, 512))]
    for g in range(1, groups):
        table.append((SMALL + g * 768, SMALL + (g + 1) * 768, slice(128 + g * 384, 512 + g * 384)))
    end = 128 + groups * 384
    table.append((SMALL + 3 * width, SMALL + 4 * width, slice(end, end + width // 2)))
    return table


def finish_kernel(
    out_in, diff, cotangent, parts, rows_low, active, d_rows, d_hidden,
    block_out, grad_input, grad_qkv, grad_out_w, grad_small, grad_up, grad_down,
):
    block_out[...] = out_in[...]
    grad_input[...] = diff[...].astype(F32) + cotangent[...].astype(F32)
    grad_up[0] = tn(rows_low[...], d_hidden[...])
    grad_down[0] = tn(active[...], d_rows[...])

    @pl.when(pl.program_id(0) == 0)
    def _():
        width = grad_out_w.shape[1]
        quarter = grad_out_w.shape[0]
        total = parts[0].astype(F32)
        for k in range(1, 4):
            total = total + parts[k].astype(F32)
        for c, (lo, hi, narrow) in enumerate(chunk_table(width)):
            both = jnp.concatenate([total[:quarter, narrow], total[quarter:, narrow]], axis=1)
            if c == width // 256:
                grad_out_w[...] = both
                continue
            if c == 0:
                square = jnp.concatenate(
                    [both[:, :SMALL], jnp.zeros((128 - quarter, SMALL), F32)], axis=0
                )
                grad_small[...] = square.T[:16]
                both = both[:, SMALL:]
            for k in range(3):
                grad_qkv[:, k * width + c * 256 : k * width + (c + 1) * 256] = both[
                    :, k * 256 : (k + 1) * 256
                ]


def kernel_plan(
    tokens, lengths, w_qkv, w_out, router, gain_one, shift_one, gain_two, shift_two,
    w_up, w_down, cotangent,
):
    own_rows, width = w_out.shape
    blocks, size = tokens.shape[:2]
    images, length, experts = blocks // 4, 4 * size, router.shape[1]
    count = images * length
    groups = width // 256
    pairs = 2 * groups
    devices = 4 * experts
    columns = 4 * width + SMALL
    fan = w_up.shape[2]
    quarter = 4 * own_rows
    pair = (images, width)
    rows = devices * images

    def shape(*dims, kind=F32):
        return jax.ShapeDtypeStruct(dims, kind)

    dma = pltpu.SemaphoreType.DMA
    vmem, anywhere = pl.BlockSpec(memory_space=VM), pl.BlockSpec(memory_space=pl.ANY)
    stage_wide = 512 + (groups - 1) * 384 + width // 2
    outs = (
        shape(*tokens.shape, kind=BF),
        shape(*tokens.shape, kind=BF),
        shape(4, 2 * own_rows, stage_wide, kind=BF),
        shape(rows, width, kind=BF),
        shape(rows, fan, kind=BF),
        shape(rows, width, kind=BF),
        shape(rows, fan, kind=BF),
    )
    scratch = [
        VM((devices, 2 * own_rows, columns // 2 + 64), BF),
        VM((width, columns + 128), BF),
        VM((128, 128), F32),
        VM((16, width), F32),
        VM((count, width), BF),
        VM((count, width), BF),
        VM((count, 3 * width), BF),
        VM((images * pairs, length, 2 * length), BF),
        VM((count, width), BF),
        VM((count, width), F32),
        VM((count, width), BF),
        VM((count, width), BF),
        VM((experts, count), F32),
        VM((experts, count), F32),
        VM((experts, count), F32),
        VM((images, experts, width), F32),
        VM((images, 1, length), F32),
        VM((width, fan), BF),
        VM((fan, width), BF),
        VM((count, width), BF),
        VM((2, experts) + pair, BF),
        VM((images, experts, width), F32),
        VM((rows, width), F32),
    ]
    scratch += [VM((devices,) + pair, BF)] * 6
    scratch += [
        VM((width, count), BF),
        VM((width, count), BF),
        VM((count, width), F32),
        VM((count, width), F32),
        VM((count, width), BF),
        VM((count, width), BF),
        VM((count, 3 * width), BF),
        VM((count, width), BF),
        VM((width, columns), BF),
        VM((4, quarter, columns), BF),
        VM((6, quarter // 2, columns), BF),
        VM((4, 2 * own_rows, stage_wide), BF),
    ]
    scratch += [dma((4,))] * 7 + [dma((16,))] * 2 + [dma((4,))] * 2
    scratch += [dma((3 * images,))] * 8
    scratch += [dma((images,))] * 4
    scratch += [dma((2,)), dma((4,)), dma((4,))]
    chunks = groups + 1
    scratch += [dma((4 * chunks,))] * 2 + [dma((6 * chunks,))] * 2 + [dma((4 * chunks,))] * 2
    vectors = [vec[None, :] for vec in (gain_one, shift_one, gain_two, shift_two)]
    out_in, diff, parts, rows_low, active, d_rows, d_hidden = pl.pallas_call(
        block_kernel,
        out_shape=outs,
        in_specs=[pl.BlockSpec(memory_space=pltpu.SMEM)] + [vmem] * 7 + [anywhere] * 4,
        out_specs=[anywhere] * 3 + [vmem] * 4,
        scratch_shapes=scratch,
        compiler_params=pltpu.CompilerParams(
            collective_id=0, has_side_effects=True, vmem_limit_bytes=63 * 2**20
        ),
        name="block",
    )(lengths, w_qkv, w_out, router.T, *vectors, tokens, cotangent, w_up, w_down)

    def by_columns(*dims):
        return pl.BlockSpec(dims + (256,), lambda k: (0,) * len(dims) + (k,))

    def whole(*dims):
        return pl.BlockSpec(dims, lambda k: (0,) * len(dims))

    block_out, grad_input, grad_qkv, grad_out_w, grad_small, grad_up, grad_down = pl.pallas_call(
        finish_kernel,
        grid=(groups,),
        out_shape=(
            shape(*tokens.shape, kind=BF),
            shape(*tokens.shape),
            shape(own_rows, 3 * width),
            shape(own_rows, width),
            shape(16, 128),
            shape(*w_up.shape),
            shape(*w_down.shape),
        ),
        in_specs=[
            by_columns(blocks, size),
            by_columns(blocks, size),
            by_columns(blocks, size),
            whole(4, 2 * own_rows, stage_wide),
            whole(rows, width),
            whole(rows, fan),
            by_columns(rows),
            by_columns(rows),
        ],
        out_specs=[
            by_columns(blocks, size),
            by_columns(blocks, size),
            whole(own_rows, 3 * width),
            whole(own_rows, width),
            whole(16, 128),
            by_columns(1, width),
            by_columns(1, fan),
        ],
        compiler_params=pltpu.CompilerParams(vmem_limit_bytes=63 * 2**20),
        name="finish",
    )(out_in, diff, cotangent, parts, rows_low, active, d_rows, d_hidden)
    return (
        block_out,
        grad_input,
        grad_qkv,
        grad_out_w,
        grad_small[:experts, :own_rows].T,
        grad_small[experts, :own_rows],
        grad_small[experts + 1, :own_rows],
        grad_small[experts + 2, :own_rows],
        grad_small[experts + 3, :own_rows],
        grad_up,
        grad_down,
    )


def solution(mesh):
    plan = kernel_plan if dict(mesh.shape) == {"dp": 8, "seq": 4} else plain_plan
    rows, vector = P(("dp", "seq"), None), P(("dp", "seq"))
    tokens = P("dp", "seq", None)
    up, down = P("dp", None, "seq"), P("dp", "seq", None)
    return jax.shard_map(
        plan,
        mesh=mesh,
        in_specs=(tokens, P("dp"), rows, rows, rows)
        + (vector,) * 4
        + (up, down, tokens),
        out_specs=(tokens, tokens, rows, rows, rows) + (vector,) * 4 + (up, down),
        check_vma=False,
    )
```

```python
import jax
import jax.numpy as jnp
from jax import lax
from jax.experimental import pallas as pl
from jax.experimental.pallas import tpu as pltpu
from jax.sharding import PartitionSpec as P

H = 12
HD = 64
BF = jnp.bfloat16
F32 = jnp.float32


def dot(spec, a, b):
    return jnp.einsum(spec, a, b, preferred_element_type=F32)


def unit_norm(values):
    centred = values - jnp.mean(values, axis=-1, keepdims=True)
    inverse = lax.rsqrt(jnp.mean(centred * centred, axis=-1, keepdims=True) + 1e-06)
    return centred * inverse, inverse


def norm_back(grad_rows, unit_rows, inverse, gain):
    scaled = grad_rows * gain
    centred = scaled - jnp.mean(scaled, axis=-1, keepdims=True)
    correction = unit_rows * jnp.mean(scaled * unit_rows, axis=-1, keepdims=True)
    return (
        inverse * (centred - correction),
        jnp.sum(grad_rows * unit_rows, axis=(0, 1)),
        jnp.sum(grad_rows, axis=(0, 1)),
    )


def gelu_tanh(values):
    return jax.nn.gelu(values, approximate=True)


def to_images(array):
    return lax.all_to_all(array, "seq", split_axis=0, concat_axis=1, tiled=True)


def to_blocks(array):
    return lax.all_to_all(array, "seq", split_axis=1, concat_axis=0, tiled=True)


def to_experts(rows):
    rows = lax.all_to_all(rows, "dp", split_axis=1, concat_axis=0, tiled=True)
    return lax.all_gather(rows, "seq", axis=0, tiled=True)


def from_experts(rows):
    rows = lax.psum_scatter(rows, "seq", scatter_dimension=0, tiled=True).astype(BF)
    return lax.all_to_all(rows, "dp", split_axis=0, concat_axis=1, tiled=True)


def plain_plan(
    tokens, lengths, w_qkv, w_out, router, gain_one, shift_one, gain_two, shift_two,
    w_up, w_down, cotangent,
):
    groups = lax.axis_size("seq")
    model_width, slots_all = w_qkv.shape[1] // 3, router.shape[1]
    packed = jnp.concatenate(
        [w_qkv, w_out, router]
        + [vec[:, None] for vec in (gain_one, shift_one, gain_two, shift_two)],
        axis=1,
    )
    packed = lax.all_gather(packed, ("dp", "seq"), axis=0, tiled=True)
    split = 4 * model_width
    w_qkv, w_out = packed[:, : 3 * model_width], packed[:, 3 * model_width : split]
    router = packed[:, split : split + slots_all]
    gain_one, shift_one, gain_two, shift_two = (
        packed[:, split + slots_all + k].astype(F32) for k in range(4)
    )
    x = to_images(tokens).astype(F32)
    cot = to_images(cotangent)
    images, length_all = x.shape[:2]
    lengths_own = lax.dynamic_slice_in_dim(lengths, lax.axis_index("seq") * images, images)
    valid = jnp.arange(length_all, dtype=jnp.int32)[None, :] < lengths_own[:, None]

    unit_one, inverse_one = unit_norm(x)
    normed_one = (unit_one * gain_one + shift_one).astype(BF)
    qkv = dot("btd,de->bte", normed_one, w_qkv).astype(BF).reshape(images, length_all, 3, H, HD)
    queries, keys_all, values_all = qkv[:, :, 0], qkv[:, :, 1], qkv[:, :, 2]
    scores = dot("bqhd,bkhd->bhqk", queries, keys_all) * HD ** (-0.5)
    probs = jax.nn.softmax(jnp.where(valid[:, None, None, :], scores, -1000000000.0), axis=-1)
    probs_low = probs.astype(BF)
    attended = dot("bhqk,bkhd->bqhd", probs_low, values_all).astype(BF)
    attended = attended.reshape(images, length_all, model_width)
    middle = x + dot("btd,de->bte", attended, w_out)
    unit_two, inverse_two = unit_norm(middle)
    normed_two = (unit_two * gain_two + shift_two).astype(BF)
    logits = dot("btd,de->bte", normed_two, router)
    top = jnp.floor(jnp.max(jnp.where(valid[:, :, None], logits, -1000000000.0), axis=1))
    dispatch = jnp.where(valid[:, :, None], jnp.exp(logits - top[:, None, :]), 0.0)
    dispatch_low = dispatch.astype(BF)
    denominator = jnp.sum(dispatch, axis=1)
    slot_vals = dot("bte,btd->bed", dispatch_low, normed_two) / denominator[:, :, None]
    slot_rows = to_experts(slot_vals.astype(BF))
    hidden = dot("red,edf->ref", slot_rows, w_up)
    active = gelu_tanh(hidden).astype(BF)
    expert_out = from_experts(dot("ref,efd->red", active, w_down))
    combine = jax.nn.softmax(logits, axis=-1)
    combine_low = combine.astype(BF)
    block_out = (middle + dot("bte,bed->btd", combine_low, expert_out)).astype(BF)

    d_combine = dot("btd,bed->bte", cot, expert_out)
    d_expert = dot("bte,btd->bed", combine_low, cot).astype(BF)
    d_rows = to_experts(d_expert)
    d_active = dot("red,efd->ref", d_rows, w_down)
    grad_down = dot("ref,red->efd", active, d_rows)
    d_hidden = jax.vjp(gelu_tanh, hidden)[1](d_active)[0].astype(BF)
    grad_up = dot("red,ref->edf", slot_rows, d_hidden)
    d_slots = from_experts(dot("ref,edf->red", d_hidden, w_up))
    d_slots_wide = d_slots.astype(F32)
    inner = jnp.sum(slot_vals * d_slots_wide, axis=-1)
    projected = dot("btd,bed->bte", normed_two, d_slots)
    d_logits = (projected - inner[:, None, :]) / denominator[:, None, :] * dispatch
    d_logits = d_logits + combine * (
        d_combine - jnp.sum(combine * d_combine, axis=-1, keepdims=True)
    )
    d_logits = d_logits.astype(BF)
    scaled = d_slots_wide / denominator[:, :, None]
    scaled_high = scaled.astype(BF)
    scaled_rest = (scaled - scaled_high.astype(F32)).astype(BF)
    d_normed_two = (
        dot("bte,bed->btd", dispatch_low, scaled_high)
        + dot("bte,bed->btd", dispatch_low, scaled_rest)
        + dot("bte,de->btd", d_logits, router)
    )
    grad_router = dot("btd,bte->de", normed_two, d_logits)
    d_norm, grad_gain_two, grad_shift_two = norm_back(d_normed_two, unit_two, inverse_two, gain_two)
    d_middle = cot.astype(F32) + d_norm
    d_branch = d_middle.astype(BF)
    grad_out_w = dot("btd,bte->de", attended, d_branch)
    d_attended = dot("bte,de->btd", d_branch, w_out).astype(BF)
    d_attended = d_attended.reshape(images, length_all, H, HD)
    d_values = dot("bhqk,bqhd->bkhd", probs_low, d_attended)
    d_probs = dot("bqhd,bkhd->bhqk", d_attended, values_all)
    d_scores = probs * (d_probs - jnp.sum(probs * d_probs, axis=-1, keepdims=True))
    d_scores = d_scores.astype(BF)
    d_queries = dot("bhqk,bkhd->bqhd", d_scores, keys_all) * HD ** (-0.5)
    d_keys = dot("bhqk,bqhd->bkhd", d_scores, queries) * HD ** (-0.5)
    d_qkv = jnp.stack([d_queries, d_keys, d_values], axis=2).astype(BF)
    d_qkv = d_qkv.reshape(images, length_all, 3 * model_width)
    grad_qkv = dot("btd,bte->de", normed_one, d_qkv)
    d_normed_one = dot("bte,de->btd", d_qkv, w_qkv)
    d_norm, grad_gain_one, grad_shift_one = norm_back(d_normed_one, unit_one, inverse_one, gain_one)
    grad_input = to_blocks(d_middle + d_norm)

    vectors = (grad_gain_one, grad_shift_one, grad_gain_two, grad_shift_two)
    packed = jnp.concatenate(
        [grad_qkv, grad_out_w, grad_router] + [vec[:, None] for vec in vectors], axis=1
    )
    packed = lax.psum_scatter(packed, ("dp", "seq"), scatter_dimension=0, tiled=True)
    return (
        to_blocks(block_out),
        grad_input,
        packed[:, : 3 * model_width],
        packed[:, 3 * model_width : split],
        packed[:, split : split + slots_all],
        packed[:, split + slots_all],
        packed[:, split + slots_all + 1],
        packed[:, split + slots_all + 2],
        packed[:, split + slots_all + 3],
        grad_up,
        grad_down,
    )


MESH = pl.DeviceIdType.MESH
VM = pltpu.VMEM
SMALL = 128
ROWS = 64


def nt(a, b):
    return lax.dot_general(a, b, (((1,), (1,)), ((), ())), preferred_element_type=F32)


def tn(a, b):
    return lax.dot_general(a, b, (((0,), (0,)), ((), ())), preferred_element_type=F32)


def mm(a, b):
    return jnp.dot(a, b, preferred_element_type=F32)


def ds(start, size, unit=None):
    return pl.ds(pl.multiple_of(start, unit or size), size)


def remote(src, dst, send, recv, device):
    return pltpu.make_async_remote_copy(
        src_ref=src, dst_ref=dst, send_sem=send, recv_sem=recv, device_id=device,
        device_id_type=MESH,
    )


def other(d, kind):
    core, x, y = lax.rem(d, 2), lax.rem(d // 2, 2), d // 4
    return {"x": d + 2 - 4 * x, "y": d + 4 - 8 * y, "core": d + 1 - 2 * core}[kind]


class Gather:
    def __init__(self, shards, full, zup, zdown, zrecv, xsend, xrecv, ysend, yrecv, csend, crecv, dsend, drecv):
        d, z = lax.axis_index("dp"), lax.axis_index("seq")
        dx, dy, dc = other(d, "x"), other(d, "y"), other(d, "core")
        self.shards, self.full, self.z = shards, full, z
        self.owners = (d, dx, dy, other(dx, "y"))
        self.over = {"x": (dx, z), "y": (dy, z), "core": (dc, z)}
        self.up, self.down = (d, lax.rem(z + 1, 4)), (d, lax.rem(z + 3, 4))
        self.sems = {
            "up": (zup, zrecv), "down": (zdown, zrecv), "x": (xsend, xrecv),
            "y": (ysend, yrecv), "core": (csend, crecv), "d": (dsend, drecv),
        }

    def copy(self, kind, owner, s, device, sem):
        ref = self.shards.at[owner * 4 + s]
        send, recv = self.sems[kind]
        return remote(ref, ref, send.at[sem], recv.at[sem], device)

    def pass_on(self, s, upward, downward):
        d, z = self.owners[0], self.z
        if upward:

            @pl.when(z < 3)
            def _():
                self.copy("up", d, s, self.up, s).start()

        if downward:

            @pl.when(z > 0)
            def _():
                self.copy("down", d, s, self.down, s).start()

        self.copy("x", d, s, self.over["x"], s).start()
        self.copy("y", d, s, self.over["y"], s).start()
        self.copy("core", d, s, self.over["core"], s).start()

    def each(self, h, act):
        if h == 0:
            act(self.z)
            return

        @pl.when(self.z >= h)
        def _():
            act(self.z - h)

        @pl.when(self.z + h <= 3)
        def _():
            act(self.z + h)

    def line(self, h):
        d, z = self.owners[0], self.z
        if h == 0:
            self.pass_on(z, True, True)
            return

        @pl.when(z >= h)
        def _():
            self.copy("up", d, z - h, self.up, z - h).wait_recv()
            self.pass_on(z - h, True, False)

        @pl.when(z + h <= 3)
        def _():
            self.copy("down", d, z + h, self.down, z + h).wait_recv()
            self.pass_on(z + h, False, True)

    def plane(self, h):
        d, dx, dy, dd = self.owners

        def act(s):
            self.copy("x", dx, s, self.over["x"], s).wait_recv()

            @pl.when(lax.rem(s, 2) == 0)
            def _():
                self.copy("d", dx, s, self.over["y"], s).start()

            self.copy("core", dx, s, self.over["core"], 4 + s).start()
            self.copy("y", dy, s, self.over["y"], s).wait_recv()

            @pl.when(lax.rem(s, 2) == 1)
            def _():
                self.copy("d", dy, s, self.over["x"], s).start()

            self.copy("core", dy, s, self.over["core"], 8 + s).start()

        self.each(h, act)

    def diagonal(self, h):
        def act(s):
            self.copy("d", self.owners[3], s, self.over["x"], s).wait_recv()
            self.copy("core", self.owners[3], s, self.over["core"], 12 + s).start()

        self.each(h, act)

    def twin(self, k):
        dc = other(self.owners[k], "core")
        for s in range(4):
            self.copy("core", dc, s, self.over["core"], 4 * k + s).wait_recv()
        self.assemble(dc)

    def assemble(self, owner):
        half, wide = self.shards.shape[1:]
        quarter = half // 2
        for side in range(2):
            value = jnp.concatenate(
                [
                    self.shards[owner * 4 + k].astype(F32)[side * quarter : (side + 1) * quarter]
                    for k in range(4)
                ],
                axis=0,
            )
            self.full[ds(owner * 2 * half, 2 * half), side * wide : (side + 1) * wide] = (
                value.astype(BF)
            )

    def sent(self):
        d, z = self.owners[0], self.z

        def one(s, carry):
            @pl.when((s <= z) & (z < 3))
            def _():
                self.copy("up", d, s, self.up, s).wait_send()

            @pl.when((s >= z) & (z > 0))
            def _():
                self.copy("down", d, s, self.down, s).wait_send()

            self.copy("x", d, s, self.over["x"], s).wait_send()
            self.copy("y", d, s, self.over["y"], s).wait_send()
            self.copy("d", d, s, self.over["x"], s).wait_send()
            for k in range(4):
                self.copy("core", self.owners[k], s, self.over["core"], 4 * k + s).wait_send()
            return carry

        lax.fori_loop(0, 4, one, 0)


def image_steps(blocks, whole, send, recv, local_sem, images, home):
    d, z = lax.axis_index("dp"), lax.axis_index("seq")
    size = blocks.shape[1]
    length = 4 * size

    def make(i, k):
        there = lax.rem(z + k, 4)
        if home:
            src = whole.at[ds(i * length + there * size, size)]
            dst = blocks.at[z * images + i]
        else:
            src = blocks.at[there * images + i]
            dst = whole.at[ds(i * length + z * size, size)]
        if k == 0:
            return pltpu.make_async_copy(src, dst, local_sem.at[i])
        return remote(src, dst, send.at[i * 3 + k - 1], recv.at[i * 3 + k - 1], (d, there))

    table = [[make(i, k) for k in range(4)] for i in range(images)]

    def start(i):
        for one in table[i]:
            one.start()

    def arrived(i):
        table[i][0].wait()
        for one in table[i][1:]:
            one.wait_recv()

    def sent():
        for i in range(images):
            for one in table[i][1:]:
                one.wait_send()

    return start, arrived, sent


def swap_steps(src, dst, send, recv, to_expert):
    d, z = lax.axis_index("dp"), lax.axis_index("seq")
    count = dst.shape[0]
    me = d * 4 + z

    def start():
        def one(k, carry):
            j = lax.rem(me + k, count)
            e = j // 4
            row = src.at[e] if to_expert else src.at[j]
            remote(row, dst.at[me], send, recv, (e, lax.rem(j, 4))).start()
            return carry

        lax.fori_loop(1, count, one, 0)
        pltpu.make_async_copy(src.at[d] if to_expert else src.at[me], dst.at[me], recv).start()

    def arrived():
        pltpu.make_async_copy(dst, dst, recv).wait()

    def sent():
        part = dst.at[pl.ds(0, count - 1)]
        remote(part, part, send, recv, (other(d, "x"), z)).wait_send()

    return start, arrived, sent


def reduce_steps(grads, pairs, inter, out_stage, in_stage, sems, chunk, lo, hi, narrow):
    d, z = lax.axis_index("dp"), lax.axis_index("seq")
    dx, dy, dc = other(d, "x"), other(d, "y"), other(d, "core")
    core = lax.rem(d, 2)
    over_x, over_y, over_c = (dx, z), (dy, z), (dc, z)
    rows = pairs.shape[1]
    half, quarter = rows // 2, rows // 4
    cols = slice(lo, hi)
    send1, recv1, send2, recv2, send3, recv3 = sems
    chips = pairs.shape[0]

    step1 = []
    for m in range(chips):
        block = grads.at[ds((2 * m + 1 - core) * rows, rows), cols]
        n = chunk * chips + m
        step1.append(remote(block, pairs.at[m, :, cols], send1.at[n], recv1.at[n], over_c))
    here, mx, my, md = d // 2, dx // 2, dy // 2, other(dx, "y") // 2

    def part(m, h):
        return pairs.at[m, h * half : (h + 1) * half, cols]

    def hop(k, m, h, device):
        n = chunk * 6 + k
        return remote(part(m, h), inter.at[k, :, cols], send2.at[n], recv2.at[n], device)

    step2 = [
        hop(0, md, 0, over_y), hop(1, md, 1, over_x), hop(2, my, 0, over_y),
        hop(3, mx, 1, over_x), hop(4, mx, 0, over_x), hop(5, my, 1, over_y),
    ]
    local_copy = pltpu.make_async_copy(
        out_stage.at[z, :, narrow], in_stage.at[3, :, narrow], recv3.at[chunk * 4 + 3]
    )
    step3 = []
    for k in range(1, 4):
        n = chunk * 4 + k - 1
        there = lax.rem(z + k, 4)
        step3.append(
            remote(
                out_stage.at[there, :, narrow], in_stage.at[k - 1, :, narrow],
                send3.at[n], recv3.at[n], (d, there),
            )
        )

    def one():
        for c in step1:
            c.start()

    def two():
        for m in range(chips):
            step1[m].wait_recv()
            own = grads[ds((2 * m + core) * rows, rows), cols].astype(F32)
            pairs[m, :, cols] = (own + pairs[m, :, cols].astype(F32)).astype(BF)
        for k in range(4):
            step2[k].start()

    def three():
        for k, m, h in ((0, mx, 0), (1, my, 1)):
            step2[k].wait_recv()
            at = slice(h * half, (h + 1) * half)
            total = pairs[m, at, cols].astype(F32) + inter[k, :, cols].astype(F32)
            pairs[m, at, cols] = total.astype(BF)
            step2[4 + k].start()

    def four():
        for k in (2, 3, 4, 5):
            step2[k].wait_recv()
        own = pairs[here, :, cols].astype(F32)
        top = own[:half] + inter[2, :, cols].astype(F32) + inter[4, :, cols].astype(F32)
        low = own[half:] + inter[3, :, cols].astype(F32) + inter[5, :, cols].astype(F32)
        total = jnp.concatenate([top, low], axis=0)
        middle = narrow.stop - narrow.start
        if 2 * middle > hi - lo:
            filler = jnp.zeros((rows, 2 * middle - (hi - lo)), F32)
            total = jnp.concatenate([total, filler], axis=1)
        for t in range(4):
            shard = total[t * quarter : (t + 1) * quarter]
            both = jnp.concatenate([shard[:, :middle], shard[:, middle:]], axis=0)
            out_stage[t, :, narrow] = both.astype(BF)
        for c in step3:
            c.start()
        local_copy.start()

    def five():
        for c in step3:
            c.wait_recv()
        local_copy.wait()

    def sent():
        for c in step1 + step2 + step3:
            c.wait_send()

    return one, two, three, four, five, sent


def unit_rows(x):
    centred = x - jnp.mean(x, axis=-1, keepdims=True)
    inverse = lax.rsqrt(jnp.mean(centred * centred, axis=-1, keepdims=True) + 1e-06)
    return centred * inverse, inverse


def fold_rows(x):
    total = x[:8]
    for k in range(1, x.shape[0] // 8):
        total = total + x[8 * k : 8 * (k + 1)]
    return total


def norm_rows_back(grad, unit, inverse, gain):
    scaled = grad * gain
    centred = scaled - jnp.mean(scaled, axis=-1, keepdims=True)
    correction = unit * jnp.mean(scaled * unit, axis=-1, keepdims=True)
    return inverse * (centred - correction)


def split_heads(pair):
    lane = lax.broadcasted_iota(jnp.int32, (1, 2 * HD), 1)
    left = jnp.where(lane < HD, 1.0, 0.0)
    return jnp.concatenate([pair * left.astype(BF), pair * (1.0 - left).astype(BF)], axis=0)


def join_heads(pair):
    lane = lax.broadcasted_iota(jnp.int32, (1, 2 * HD), 1)
    rows = pair.shape[0] // 2
    return jnp.where(lane < HD, pair[:rows], pair[rows:])


def gelu_parts(v):
    inner = jnp.tanh(0.7978845608 * (v + 0.044715 * v * v * v))
    slope = 0.5 * (1.0 + inner) + 0.5 * v * (1.0 - inner * inner) * 0.7978845608 * (
        1.0 + 3.0 * 0.044715 * v * v
    )
    return 0.5 * v * (1.0 + inner), slope


def block_kernel(
    lengths, w_qkv, w_out, router_own, gain_a, shift_a, gain_b, shift_b, tokens, cotangent,
    w_up, w_down,
    block_out, g_blocks, in_stage, rows_low, active, d_rows, d_hidden,
    shards, full, corner, small, xs, cots, qkv, probs, attended, middle, n_one, n_two,
    disp, comb, dcomb, slots, bias, up, down, out_rows, pair_in, pair_out, row_sums,
    recv_a, recv_b, recv_c, recv_d, send_b, send_d, turned_one, turned_att,
    d_norm, d_diff, d_branch, d_attended, d_qkv, g_rows,
    grads, pairs_buf, inter, out_stage,
    zup, zdown, zrecv, xsend, xrecv, ysend, yrecv, wsend, wrecv, dsend, drecv, tsend, trecv, csend, crecv, bsend, brecv, gsend, grecv,
    t_local, c_local, b_local, g_local, loads, swap_send, swap_recv,
    send1, recv1, send2, recv2, send3, recv3,
):
    d, z = lax.axis_index("dp"), lax.axis_index("seq")
    width = tokens.shape[2]
    images = tokens.shape[0] // 4
    length = 4 * tokens.shape[1]
    count = images * length
    groups = width // 256
    experts = disp.shape[0]
    devices = recv_a.shape[0]
    base_qkv, base_out = SMALL, SMALL + 3 * width

    barrier = pltpu.get_barrier_semaphore()
    partners = [(d, lax.rem(z + k, 4)) for k in range(1, 4)]
    partners += [(other(d, kind), z) for kind in ("x", "y", "core")]
    for partner in partners:
        pl.semaphore_signal(barrier, inc=1, device_id=partner, device_id_type=MESH)
    load_up = pltpu.make_async_copy(w_up.at[0], up, loads.at[0])
    load_down = pltpu.make_async_copy(w_down.at[0], down, loads.at[1])
    load_up.start()
    load_down.start()
    own_rows = w_out.shape[0]
    corner[...] = jnp.zeros_like(corner)
    corner[0:experts, 0:own_rows] = router_own[...].astype(F32)
    for k, vector in enumerate((gain_a, shift_a, gain_b, shift_b)):
        corner[experts + k : experts + k + 1, 0:own_rows] = vector[...].astype(F32)
    own = w_qkv[...].astype(F32)
    pieces = [corner[...].T[:own_rows]]
    for g in range(groups):
        for k in range(3):
            pieces.append(own[:, k * width + g * 256 : k * width + (g + 1) * 256])
    pieces += [w_out[...].astype(F32), jnp.zeros((own_rows, 128), F32)]
    line = jnp.concatenate(pieces, axis=1)
    wide = shards.shape[2]
    shards[d * 4 + z] = jnp.concatenate([line[:, :wide], line[:, wide:]], axis=0).astype(BF)
    pl.semaphore_wait(barrier, len(partners))

    gather = Gather(
        shards, full, zup, zdown, zrecv, xsend, xrecv, ysend, yrecv, wsend, wrecv, dsend, drecv
    )
    t_start, t_arrived, t_sent = image_steps(tokens, xs, tsend, trecv, t_local, images, False)
    c_start, c_arrived, c_sent = image_steps(cotangent, cots, csend, crecv, c_local, images, False)
    gather.line(0)
    gather.line(1)
    gather.plane(0)
    gather.line(2)
    t_start(0)
    gather.plane(1)
    gather.diagonal(0)
    gather.line(3)
    for i in range(1, images):
        t_start(i)
    gather.plane(2)
    gather.diagonal(1)
    gather.assemble(d)
    gather.plane(3)
    gather.diagonal(2)
    gather.twin(0)
    gather.diagonal(3)
    for k in range(1, 4):
        gather.assemble(gather.owners[k])
        gather.twin(k)
    small[...] = full[:, 0:128].astype(F32).T[:16]
    gains = [small[8 + k : 9 + k, :] for k in range(4)]

    def norm_one(k, carry):
        at = ds(k * ROWS, ROWS)
        unit, _ = unit_rows(xs[at, :].astype(F32))
        n_one[at, :] = (unit * gains[0] + gains[1]).astype(BF)
        return carry

    per_image = length // ROWS
    for i in range(images):
        t_arrived(i)
        if i == images - 1:
            for k in range(images):
                c_start(k)
        lax.fori_loop(i * per_image, (i + 1) * per_image, norm_one, 0)

    def project(k, carry):
        weight = full[:, ds(base_qkv + k * 256, 256, 128)]
        qkv[:, ds(k * 256, 256)] = mm(n_one[...], weight).astype(BF)
        return carry

    lax.fori_loop(0, 3 * groups, project, 0)

    key = lax.broadcasted_iota(jnp.int32, (1, length), 1)
    for i in range(images):
        bias[i] = jnp.where(key < lengths[z * images + i], 0.0, -1000000000.0)
    scale = jnp.asarray(HD ** (-0.5), BF)
    pairs = 2 * groups

    def heads(t):
        i, p = t // pairs, pairs - 1 - lax.rem(t, pairs)
        base = (p // 2) * 768 + lax.rem(p, 2) * 128
        return i, p, ds(i * length, length), base

    def attend(t, carry):
        i, p, at, base = heads(t)
        keys = split_heads(qkv[at, ds(base + 256, 128)])
        values = split_heads(qkv[at, ds(base + 512, 128)])
        scores = nt(qkv[at, ds(base, 128)] * scale, keys)
        for h in range(2):
            part = scores[:, h * length : (h + 1) * length] + bias[i]
            e = jnp.exp(part - jnp.max(part, axis=-1, keepdims=True))
            total = jnp.sum(e, axis=-1, keepdims=True)
            probs[t, :, h * length : (h + 1) * length] = (e * (1.0 / total)).astype(BF)
        attended[at, ds(p * 128, 128)] = mm(probs[t], values).astype(BF)
        return carry

    lax.fori_loop(0, images * pairs, attend, 0, unroll=3)

    def project_out(k, carry):
        at = ds(k * 256, 256)
        weight = full[:, ds(base_out + k * 256, 256, 128)]
        middle[:, at] = xs[:, at].astype(F32) + mm(attended[...], weight)
        return carry

    lax.fori_loop(0, groups, project_out, 0)

    def norm_two(k, carry):
        at = ds(k * ROWS, ROWS)
        unit, _ = unit_rows(middle[at, :])
        n_two[at, :] = (unit * gains[2] + gains[3]).astype(BF)
        return carry

    lax.fori_loop(0, count // ROWS, norm_two, 0)
    router = small[0:8, :].astype(BF)
    spans = [slice(i * length, (i + 1) * length) for i in range(images)]
    denominators = []
    for i, at in enumerate(spans):
        logits = nt(router, n_two[at, :])
        inside = key < lengths[z * images + i]
        top = jnp.floor(
            jnp.max(jnp.where(inside, logits, -1000000000.0), axis=-1, keepdims=True)
        )
        dispatch = jnp.where(inside, jnp.exp(logits - top), 0.0)
        e = jnp.exp(logits - jnp.max(logits, axis=0, keepdims=True))
        disp[:, at] = dispatch
        comb[:, at] = e / jnp.sum(e, axis=0, keepdims=True)
        denominators.append(jnp.sum(dispatch, axis=-1, keepdims=True))
        slots[i] = mm(dispatch.astype(BF), n_two[at, :]) / denominators[i]

    swap_a = swap_steps(pair_in.at[0], recv_a, swap_send.at[0], swap_recv.at[0], True)
    swap_b = swap_steps(send_b, recv_b, swap_send.at[1], swap_recv.at[1], False)
    swap_c = swap_steps(pair_in.at[1], recv_c, swap_send.at[2], swap_recv.at[2], True)
    swap_d = swap_steps(send_d, recv_d, swap_send.at[3], swap_recv.at[3], False)

    def to_pairs(which, values):
        for e in range(experts):
            pair_in[which, e] = jnp.concatenate(
                [value[e : e + 1] for value in values], axis=0
            ).astype(BF)

    def from_pairs(ref):
        for j in range(devices):
            row_sums[images * j : images * (j + 1), :] = ref[j].astype(F32)
        return row_sums[...].astype(BF)

    def spread(ref, value):
        row_sums[...] = value
        for j in range(devices):
            ref[j] = row_sums[images * j : images * (j + 1), :].astype(BF)

    def collect(ref):
        for e in range(experts):
            total = ref[4 * e].astype(F32)
            for k in range(1, 4):
                total = total + ref[4 * e + k].astype(F32)
            for i in range(images):
                pair_out[i, e : e + 1, :] = total[i : i + 1]
        return [pair_out[i].astype(BF) for i in range(images)]

    to_pairs(0, [slots[i] for i in range(images)])
    swap_a[0]()
    combs = [comb[:, at].astype(BF) for at in spans]
    sends = []
    for i, at in enumerate(spans):
        c_arrived(i)
        sends.append(mm(combs[i], cots[at, :]))
    to_pairs(1, sends)
    swap_c[0]()
    load_up.wait()
    load_down.wait()
    swap_a[1]()
    rows_low[...] = from_pairs(recv_a)
    hidden = mm(rows_low[...], up[...])
    act, slope = gelu_parts(hidden)
    active[...] = act.astype(BF)
    spread(send_b, mm(active[...], down[...]))
    swap_b[0]()
    swap_c[1]()
    d_rows[...] = from_pairs(recv_c)
    d_active = nt(d_rows[...], down[...])
    d_hidden[...] = (d_active * slope).astype(BF)
    spread(send_d, nt(d_hidden[...], up[...]))
    swap_d[0]()
    turned_one[...] = n_one[...].T
    turned_att[...] = attended[...].T
    swap_b[1]()
    outs = collect(recv_b)
    b_start, b_arrived, b_sent = image_steps(
        block_out, out_rows, bsend, brecv, b_local, images, True
    )
    for i, at in enumerate(spans):
        for k in range(groups):
            cols = slice(k * 256, (k + 1) * 256)
            moe = tn(combs[i], outs[i][:, cols])
            out_rows[at, cols] = (middle[at, cols] + moe).astype(BF)
        dcomb[:, at] = nt(outs[i], cots[at, :])
        b_start(i)
    swap_d[1]()
    d_slots = collect(recv_d)

    router_grad = jnp.zeros((experts, width), F32)
    for i, at in enumerate(spans):
        wide_slots = d_slots[i].astype(F32)
        inner = jnp.sum(slots[i] * wide_slots, axis=-1, keepdims=True)
        projected = nt(d_slots[i], n_two[at, :])
        weight, change = comb[:, at], dcomb[:, at]
        d_logits = (projected - inner) / denominators[i] * disp[:, at]
        d_logits = d_logits + weight * (
            change - jnp.sum(weight * change, axis=0, keepdims=True)
        )
        router_grad = router_grad + mm(d_logits.astype(BF), n_two[at, :])
        scaled = wide_slots / denominators[i]
        high = scaled.astype(BF).astype(F32)
        left = jnp.concatenate(
            [disp[:, at], disp[:, at], d_logits, jnp.zeros_like(d_logits)], axis=0
        ).astype(BF)
        right = jnp.concatenate(
            [high, scaled - high, small[0:8, :], jnp.zeros_like(scaled)], axis=0
        ).astype(BF)
        for k in range(groups):
            cols = slice(k * 256, (k + 1) * 256)
            d_norm[at, cols] = tn(left, right[:, cols])

    nothing = jnp.zeros((8, width), F32)

    def back_two(k, carry):
        at = ds(k * ROWS, ROWS)
        grad = d_norm[at, :]
        unit, inverse = unit_rows(middle[at, :])
        change = norm_rows_back(grad, unit, inverse, gains[2])
        d_diff[at, :] = change
        d_branch[at, :] = (change + cots[at, :].astype(F32)).astype(BF)
        return carry[0] + fold_rows(grad * unit), carry[1] + fold_rows(grad)

    gain_two, shift_two = lax.fori_loop(0, count // ROWS, back_two, (nothing, nothing))

    sems = (send1, recv1, send2, recv2, send3, recv3)
    chunks = [
        reduce_steps(
            grads, pairs_buf, inter, out_stage, in_stage, sems, c, lo, hi, narrow
        )
        for c, (lo, hi, narrow) in enumerate(chunk_table(width))
    ]
    c_out, c_pos = chunks[groups], chunks[:groups]

    def grad_out(k, carry):
        cols = ds(k * 256, 256)
        to = ds(base_out + k * 256, 256, 128)
        grads[:, to] = mm(turned_att[...], d_branch[:, cols]).astype(BF)
        return carry

    lax.fori_loop(0, groups, grad_out, 0)
    c_out[0]()

    def back_out(k, carry):
        at = ds(k * 256, 256)
        d_attended[:, at] = nt(d_branch[...], full[at, base_out : base_out + width]).astype(BF)
        return carry

    lax.fori_loop(0, groups, back_out, 0)

    def attend_back(t, carry):
        i, p, at, base = heads(t)
        q = qkv[at, ds(base, 128)] * scale
        keys = split_heads(qkv[at, ds(base + 256, 128)])
        values = split_heads(qkv[at, ds(base + 512, 128)])
        grad = d_attended[at, ds(p * 128, 128)]
        d_values = join_heads(tn(probs[t], grad))
        d_probs = nt(grad, values)
        cuts = []
        for h in range(2):
            cut = slice(h * length, (h + 1) * length)
            weight = probs[t, :, cut].astype(F32)
            change = weight * d_probs[:, cut]
            total = jnp.sum(change, axis=-1, keepdims=True)
            cuts.append((change - weight * total).astype(BF))
        d_scores = jnp.concatenate(cuts, axis=1)
        d_qkv[at, ds(base, 128)] = (mm(d_scores, keys) * HD ** (-0.5)).astype(BF)
        d_qkv[at, ds(base + 256, 128)] = join_heads(tn(d_scores, q)).astype(BF)
        d_qkv[at, ds(base + 512, 128)] = d_values.astype(BF)
        return carry

    def group_grads(g):
        def one(k, carry):
            at = ds(g * 768 + k * 256, 256)
            to = ds(base_qkv + g * 768 + k * 256, 256, 128)
            grads[:, to] = mm(turned_one[...], d_qkv[:, at]).astype(BF)
            return carry

        lax.fori_loop(0, 3, one, 0)

    def input_grads(i, carry):
        at = spans[i]

        def back_qkv(k, carry):
            cols = ds(k * 256, 256)
            d_norm[at, cols] = nt(d_qkv[at, :], full[cols, base_qkv : base_qkv + 3 * width])
            return carry

        def back_one(k, carry):
            at = ds(k * ROWS, ROWS)
            grad = d_norm[at, :]
            unit, inverse = unit_rows(xs[at, :].astype(F32))
            change = norm_rows_back(grad, unit, inverse, gains[0])
            g_rows[at, :] = (change + d_diff[at, :]).astype(BF)
            return carry[0] + fold_rows(grad * unit), carry[1] + fold_rows(grad)

        lax.fori_loop(0, groups, back_qkv, 0)
        carry = lax.fori_loop(i * per_image, (i + 1) * per_image, back_one, carry)
        g_start(i)
        return carry

    g_start, g_arrived, g_sent = image_steps(
        g_blocks, g_rows, gsend, grecv, g_local, images, True
    )
    sums_one = (nothing, nothing)
    for i in range(images - 1):
        lax.fori_loop(i * pairs, (i + 1) * pairs, attend_back, 0, unroll=3)
        if i == 0:
            c_out[1]()
        sums_one = input_grads(i, sums_one)
    begin = (images - 1) * pairs
    lax.fori_loop(begin, begin + 2, attend_back, 0, unroll=2)
    c_out[2]()
    group_grads(2)
    c_pos[2][0]()
    lax.fori_loop(begin + 2, begin + 4, attend_back, 0, unroll=2)
    c_out[3]()
    c_pos[2][1]()
    group_grads(1)
    c_pos[1][0]()
    lax.fori_loop(begin + 4, begin + 6, attend_back, 0, unroll=2)
    c_pos[2][2]()
    c_pos[1][1]()
    gain_one, shift_one = input_grads(images - 1, sums_one)
    sums = [
        jnp.sum(value, axis=0, keepdims=True)
        for value in (gain_one, shift_one, gain_two, shift_two)
    ]
    tall = jnp.concatenate(
        [router_grad] + sums + [jnp.zeros((128 - experts - 4, width), F32)], axis=0
    )
    grads[:, 0:SMALL] = tall.T.astype(BF)
    group_grads(0)
    c_pos[0][0]()
    c_pos[1][2]()
    c_pos[2][3]()
    c_pos[0][1]()
    c_pos[1][3]()
    c_pos[0][2]()
    c_pos[0][3]()
    for i in range(images):
        b_arrived(i)
    c_out[4]()
    c_pos[2][4]()
    c_pos[1][4]()
    for i in range(images):
        g_arrived(i)
    c_pos[0][4]()
    for done in (gather.sent, t_sent, c_sent, b_sent, g_sent):
        done()
    for swap in (swap_a, swap_b, swap_c, swap_d):
        swap[2]()
    for chunk in chunks:
        chunk[5]()


def chunk_table(width):
    groups = width // 256
    table = [(0, SMALL + 768, slice(0, 512))]
    for g in range(1, groups):
        table.append((SMALL + g * 768, SMALL + (g + 1) * 768, slice(128 + g * 384, 512 + g * 384)))
    end = 128 + groups * 384
    table.append((SMALL + 3 * width, SMALL + 4 * width, slice(end, end + width // 2)))
    return table


def finish_kernel(
    out_in, diff, cotangent, parts, rows_low, active, d_rows, d_hidden,
    block_out, grad_input, grad_qkv, grad_out_w, grad_small, grad_up, grad_down,
):
    block_out[...] = out_in[...]
    grad_input[...] = diff[...].astype(F32) + cotangent[...].astype(F32)
    grad_up[0] = tn(rows_low[...], d_hidden[...])
    grad_down[0] = tn(active[...], d_rows[...])

    @pl.when(pl.program_id(0) == 0)
    def _():
        width = grad_out_w.shape[1]
        quarter = grad_out_w.shape[0]
        total = parts[0].astype(F32)
        for k in range(1, 4):
            total = total + parts[k].astype(F32)
        for c, (lo, hi, narrow) in enumerate(chunk_table(width)):
            both = jnp.concatenate([total[:quarter, narrow], total[quarter:, narrow]], axis=1)
            if c == width // 256:
                grad_out_w[...] = both
                continue
            if c == 0:
                square = jnp.concatenate(
                    [both[:, :SMALL], jnp.zeros((128 - quarter, SMALL), F32)], axis=0
                )
                grad_small[...] = square.T[:16]
                both = both[:, SMALL:]
            for k in range(3):
                grad_qkv[:, k * width + c * 256 : k * width + (c + 1) * 256] = both[
                    :, k * 256 : (k + 1) * 256
                ]


def kernel_plan(
    tokens, lengths, w_qkv, w_out, router, gain_one, shift_one, gain_two, shift_two,
    w_up, w_down, cotangent,
):
    own_rows, width = w_out.shape
    blocks, size = tokens.shape[:2]
    images, length, experts = blocks // 4, 4 * size, router.shape[1]
    count = images * length
    groups = width // 256
    pairs = 2 * groups
    devices = 4 * experts
    columns = 4 * width + SMALL
    fan = w_up.shape[2]
    quarter = 4 * own_rows
    pair = (images, width)
    rows = devices * images

    def shape(*dims, kind=F32):
        return jax.ShapeDtypeStruct(dims, kind)

    dma = pltpu.SemaphoreType.DMA
    vmem, anywhere = pl.BlockSpec(memory_space=VM), pl.BlockSpec(memory_space=pl.ANY)
    stage_wide = 512 + (groups - 1) * 384 + width // 2
    outs = (
        shape(*tokens.shape, kind=BF),
        shape(*tokens.shape, kind=BF),
        shape(4, 2 * own_rows, stage_wide, kind=BF),
        shape(rows, width, kind=BF),
        shape(rows, fan, kind=BF),
        shape(rows, width, kind=BF),
        shape(rows, fan, kind=BF),
    )
    scratch = [
        VM((devices, 2 * own_rows, columns // 2 + 64), BF),
        VM((width, columns + 128), BF),
        VM((128, 128), F32),
        VM((16, width), F32),
        VM((count, width), BF),
        VM((count, width), BF),
        VM((count, 3 * width), BF),
        VM((images * pairs, length, 2 * length), BF),
        VM((count, width), BF),
        VM((count, width), F32),
        VM((count, width), BF),
        VM((count, width), BF),
        VM((experts, count), F32),
        VM((experts, count), F32),
        VM((experts, count), F32),
        VM((images, experts, width), F32),
        VM((images, 1, length), F32),
        VM((width, fan), BF),
        VM((fan, width), BF),
        VM((count, width), BF),
        VM((2, experts) + pair, BF),
        VM((images, experts, width), F32),
        VM((rows, width), F32),
    ]
    scratch += [VM((devices,) + pair, BF)] * 6
    scratch += [
        VM((width, count), BF),
        VM((width, count), BF),
        VM((count, width), F32),
        VM((count, width), F32),
        VM((count, width), BF),
        VM((count, width), BF),
        VM((count, 3 * width), BF),
        VM((count, width), BF),
        VM((width, columns), BF),
        VM((4, quarter, columns), BF),
        VM((6, quarter // 2, columns), BF),
        VM((4, 2 * own_rows, stage_wide), BF),
    ]
    scratch += [dma((4,))] * 7 + [dma((16,))] * 2 + [dma((4,))] * 2
    scratch += [dma((3 * images,))] * 8
    scratch += [dma((images,))] * 4
    scratch += [dma((2,)), dma((4,)), dma((4,))]
    chunks = groups + 1
    scratch += [dma((4 * chunks,))] * 2 + [dma((6 * chunks,))] * 2 + [dma((4 * chunks,))] * 2
    vectors = [vec[None, :] for vec in (gain_one, shift_one, gain_two, shift_two)]
    out_in, diff, parts, rows_low, active, d_rows, d_hidden = pl.pallas_call(
        block_kernel,
        out_shape=outs,
        in_specs=[pl.BlockSpec(memory_space=pltpu.SMEM)] + [vmem] * 7 + [anywhere] * 4,
        out_specs=[anywhere] * 3 + [vmem] * 4,
        scratch_shapes=scratch,
        compiler_params=pltpu.CompilerParams(
            collective_id=0, has_side_effects=True, vmem_limit_bytes=63 * 2**20
        ),
        name="block",
    )(lengths, w_qkv, w_out, router.T, *vectors, tokens, cotangent, w_up, w_down)

    def by_columns(*dims):
        return pl.BlockSpec(dims + (256,), lambda k: (0,) * len(dims) + (k,))

    def whole(*dims):
        return pl.BlockSpec(dims, lambda k: (0,) * len(dims))

    block_out, grad_input, grad_qkv, grad_out_w, grad_small, grad_up, grad_down = pl.pallas_call(
        finish_kernel,
        grid=(groups,),
        out_shape=(
            shape(*tokens.shape, kind=BF),
            shape(*tokens.shape),
            shape(own_rows, 3 * width),
            shape(own_rows, width),
            shape(16, 128),
            shape(*w_up.shape),
            shape(*w_down.shape),
        ),
        in_specs=[
            by_columns(blocks, size),
            by_columns(blocks, size),
            by_columns(blocks, size),
            whole(4, 2 * own_rows, stage_wide),
            whole(rows, width),
            whole(rows, fan),
            by_columns(rows),
            by_columns(rows),
        ],
        out_specs=[
            by_columns(blocks, size),
            by_columns(blocks, size),
            whole(own_rows, 3 * width),
            whole(own_rows, width),
            whole(16, 128),
            by_columns(1, width),
            by_columns(1, fan),
        ],
        compiler_params=pltpu.CompilerParams(vmem_limit_bytes=63 * 2**20),
        name="finish",
    )(out_in, diff, cotangent, parts, rows_low, active, d_rows, d_hidden)
    return (
        block_out,
        grad_input,
        grad_qkv,
        grad_out_w,
        grad_small[:experts, :own_rows].T,
        grad_small[experts, :own_rows],
        grad_small[experts + 1, :own_rows],
        grad_small[experts + 2, :own_rows],
        grad_small[experts + 3, :own_rows],
        grad_up,
        grad_down,
    )


def solution(mesh):
    plan = kernel_plan if dict(mesh.shape) == {"dp": 8, "seq": 4} else plain_plan
    rows, vector = P(("dp", "seq"), None), P(("dp", "seq"))
    tokens = P("dp", "seq", None)
    up, down = P("dp", None, "seq"), P("dp", "seq", None)
    return jax.shard_map(
        plan,
        mesh=mesh,
        in_specs=(tokens, P("dp"), rows, rows, rows)
        + (vector,) * 4
        + (up, down, tokens),
        out_specs=(tokens, tokens, rows, rows, rows) + (vector,) * 4 + (up, down),
        check_vma=False,
    )
```
